128 devices in a mesh: row: 8 (over x, core), col: 16 (over y, z).
Axes of the slice: x: 4, y: 4, z: 4, core: 2. Of those that a mesh axis runs over, the one named last changes fastest.
Arguments:
- flow_state: float32 [5, 4, 1024, 2048], P(None, None, 'row', 'col'), may hold values from -6 to 6
- viscosity: float32 [4, 1024, 2048], P(None, 'row', 'col'), may hold values from 0.5 to 2
- metric_x: float32 [1024, 2048], P('row', 'col'), may hold values from 128 to 512
- metric_y: float32 [1024, 2048], P('row', 'col'), may hold values from 128 to 512
- jacobian_x: float32 [5, 5, 1024], P(None, None, 'row'), may hold values from -2.5 to 2.5
- jacobian_y: float32 [5, 5, 2048], P(None, None, 'col'), may hold values from -2.5 to 2.5
Outputs:
- increment: float32 [5, 4, 1024, 2048], P(None, None, 'row', 'col')
The draws below stay inside these ranges and needn't reach their ends.
All inputs are finite; a program needn't handle non-finite values.
Results may differ from the reference program's by a relative error of at most 0.0014.
Values sent between devices are 32-bit elements; how exact they have to be, the bound alone decides.
No kernel may reach another device: no remote copies, remote signals or barrier semaphores. Data moves between devices by JAX's collectives and lax.ppermute only.
A program may use at most 128 MiB of HBM per device.

```python
import math
import jax
import jax.numpy as jnp
from jax import lax

NZ = 4
NX = 1024
NY = 2048


def draw_flow_state(key, part):
    full_shape = (5, NZ, NX, NY)
    return jnp.clip(jax.random.normal(key, full_shape, jnp.float32), -6.0, 6.0)


def shard_levels(own_key, dims, shards, smallest, largest):
    level = 1.0
    for axis_at, parts in shards:
        heights = jax.random.uniform(jax.random.fold_in(jax.random.fold_in(own_key, 6), axis_at), (parts,), jnp.float32, smallest / len(shards), largest / len(shards))
        level = level * jnp.repeat(jnp.exp(heights), dims[axis_at] // parts).reshape((-1,) + (1,) * (len(dims) - 1 - axis_at))
    return level


def scatter_about(key, dims, width, most, shards=(), kind=jnp.bfloat16):
    result = width * jax.random.normal(key, dims, jnp.float32)
    if shards:
        result = result * shard_levels(key, dims, shards, -0.22, 0.18)
    return jnp.clip(result, -most, most).astype(kind)


def setup_inputs(seed: int = 0) -> dict:
    key_list = jax.random.split(jax.random.key(seed), 7)
    return {
        "flow_state": draw_flow_state(jax.random.fold_in(key_list[6], 71), 0),
        "viscosity": jnp.clip(jnp.exp(math.log(2.0) - 1.3862944 * jax.random.uniform(key_list[1], (NZ, NX, NY), jnp.float32) ** shard_levels(key_list[1], (NZ, NX, NY), ((1, 8), (2, 16)), -0.2, 0.2)), 0.5, 2.0),
        "metric_x": jnp.clip(jnp.exp(math.log(512.0) - 1.3862944 * jax.random.uniform(key_list[2], (NX, NY), jnp.float32) ** shard_levels(key_list[2], (NX, NY), ((0, 8), (1, 16)), -0.2, 0.2)), 128.0, 512.0),
        "metric_y": jnp.clip(jnp.exp(math.log(512.0) - 1.3862944 * jax.random.uniform(key_list[3], (NX, NY), jnp.float32) ** shard_levels(key_list[3], (NX, NY), ((0, 8), (1, 16)), -0.2, 0.2)), 128.0, 512.0),
        "jacobian_x": scatter_about(key_list[4], (5, 5, NX), 5 ** -0.5, 2.5, ((2, 8),), jnp.float32),
        "jacobian_y": scatter_about(key_list[5], (5, 5, NY), 5 ** -0.5, 2.5, ((2, 16),), jnp.float32),
    }


def block_product(left_mat, right_mat):
    return jnp.sum(left_mat[:, :, None] * right_mat[None], axis=1)


def block_apply(matrix, vector):
    return jnp.sum(matrix * vector[None], axis=1)


def invert_block(matrix):
    unit_entry = jnp.ones_like(matrix[0, 0])
    zero_entry = jnp.zeros_like(matrix[0, 0])
    matrix_rows = []
    for i in range(5):
        entries = [matrix[i, j] for j in range(5)]
        entries = entries + [unit_entry if i == j else zero_entry for j in range(5)]
        matrix_rows.append(entries)
    for p in range(5):
        factor = 1.0 / matrix_rows[p][p]
        matrix_rows[p] = [entry * factor for entry in matrix_rows[p]]
        for i in range(5):
            if i != p:
                weight_here = matrix_rows[i][p]
                matrix_rows[i] = [entry - weight_here * other for entry, other in zip(matrix_rows[i], matrix_rows[p])]
    return jnp.stack([jnp.stack(entries[5:]) for entries in matrix_rows])


def jacobian_term(jacobian, difference):
    summed = jacobian[:, 0] * difference[0][None]
    for d in range(1, 5):
        summed = summed + jacobian[:, d] * difference[d][None]
    return summed


def explicit_residual(flow_state, padded, viscosity, metric_x, metric_y, jacobian_x, jacobian_y):
    east_cells = padded[:, :, 2:, 1:-1]
    west_cells = padded[:, :, :-2, 1:-1]
    north_cells = padded[:, :, 1:-1, 2:]
    south_cells = padded[:, :, 1:-1, :-2]
    diffusion_x = viscosity * (metric_x * metric_x)
    diffusion_y = viscosity * (metric_y * metric_y)
    second_x = east_cells - 2.0 * flow_state + west_cells
    second_y = north_cells - 2.0 * flow_state + south_cells
    convect_x = jacobian_term(jacobian_x[:, :, None, :, None], east_cells - west_cells)
    convect_y = jacobian_term(jacobian_y[:, :, None, None, :], north_cells - south_cells)
    return ((diffusion_x * second_x - metric_x * convect_x) + diffusion_y * second_y) - metric_y * convect_y


def line_thomas(source, diffusion, metric, jacobian):
    unit = jnp.eye(5, dtype=source.dtype)[:, :, None]

    def forward(carry, cell):
        prev_gain, prev_value = carry
        right_side, diffuse, speed, local_jac = cell
        lower = -diffuse * unit - speed * local_jac
        upper = -diffuse * unit + speed * local_jac
        pivot = invert_block((1.0 + 2.0 * diffuse) * unit - block_product(lower, prev_gain))
        gain = block_product(pivot, upper)
        value = block_apply(pivot, right_side - block_apply(lower, prev_value))
        return (gain, value), (gain, value)

    zero_gain = jnp.zeros((5, 5, source.shape[2]), source.dtype)
    zero_value = jnp.zeros((5, source.shape[2]), source.dtype)
    _, (gains, values) = lax.scan(forward, (zero_gain, zero_value), (source, diffusion, metric, jacobian))

    def backward(following, cell):
        gain, value = cell
        current = value - block_apply(gain, following)
        return current, current

    _, solved = lax.scan(backward, zero_value, (gains, values), reverse=True)
    return solved


def reference(flow_state, viscosity, metric_x, metric_y, jacobian_x, jacobian_y):
    padded = jnp.pad(flow_state, ((0, 0), (0, 0), (1, 1), (1, 1)))
    source = explicit_residual(flow_state, padded, viscosity, metric_x, metric_y, jacobian_x, jacobian_y)
    diffusion_x = viscosity * (metric_x * metric_x)
    diffusion_y = viscosity * (metric_y * metric_y)
    cells_x = jnp.transpose(jacobian_x, (2, 0, 1))[..., None]
    cells_y = jnp.transpose(jacobian_y, (2, 0, 1))[..., None]

    def sweep_x(inputs):
        field, diffusion = inputs
        solved = line_thomas(jnp.transpose(field, (1, 0, 2)), diffusion, metric_x, cells_x)
        return jnp.transpose(solved, (1, 0, 2))

    partial_value = lax.map(sweep_x, (jnp.moveaxis(source, 1, 0), diffusion_x))

    def sweep_y(inputs):
        field, diffusion = inputs
        solved = line_thomas(jnp.transpose(field, (2, 0, 1)), diffusion.T, metric_y.T, cells_y)
        return jnp.transpose(solved, (1, 2, 0))

    increment = lax.map(sweep_y, (partial_value, diffusion_y))
    return jnp.moveaxis(increment, 0, 1)
```

```python
import functools

import jax
import jax.numpy as jnp
from jax import lax
from jax.experimental import pallas as pl
from jax.experimental.pallas import tpu as pltpu
from jax.sharding import PartitionSpec as P

F32 = jnp.float32
N = 128
HALF = 64
CHUNK = 8
STEPS = HALF // CHUNK
VMEM_LIMIT = 48 * 1024 * 1024


def zeros():
    return jnp.zeros((8, 128), F32)


def ones():
    return jnp.ones((8, 128), F32)


def lane(value, index):
    return jnp.broadcast_to(value[:, index : index + 1], (8, 128))


def mat_cols(matrix, columns):
    result = []
    for column in columns:
        out = []
        for i in range(5):
            total = matrix[i][0] * column[0]
            for k in range(1, 5):
                total = total + matrix[i][k] * column[k]
            out.append(total)
        result.append(out)
    return result


def solve(matrix, columns):
    m = [list(row) for row in matrix]
    cols = [list(column) for column in columns]
    inverse = []
    for p in range(5):
        inv = 1.0 / m[p][p]
        inverse.append(inv)
        for i in range(p + 1, 5):
            weight = m[i][p] * inv
            for j in range(p + 1, 5):
                m[i][j] = m[i][j] - weight * m[p][j]
            for column in cols:
                column[i] = column[i] - weight * column[p]
    for column in cols:
        for i in range(4, -1, -1):
            total = column[i]
            for j in range(i + 1, 5):
                total = total - m[i][j] * column[j]
            column[i] = total * inverse[i]
    return cols


def columns_of(matrix):
    return [[matrix[i][j] for i in range(5)] for j in range(5)]


def rows_of(columns):
    return [[columns[j][i] for j in range(5)] for i in range(5)]


def load_mat(ref, base):
    return [[ref[base + 5 * i + j] for j in range(5)] for i in range(5)]


def load_vec(ref, base):
    return [ref[base + i] for i in range(5)]


def store_mat(ref, base, matrix):
    for i in range(5):
        for j in range(5):
            ref[base + 5 * i + j] = matrix[i][j]


def store_vec(ref, base, vector):
    for i in range(5):
        ref[base + i] = vector[i]


R_AT, X_AT, W_AT, Q_AT, XQ_AT, Y_AT, STATE = 0, 25, 50, 55, 80, 105, 110


def init_state(state):
    for i in range(5):
        for j in range(5):
            state[R_AT + 5 * i + j] = ones() if i == j else zeros()
            state[X_AT + 5 * i + j] = zeros()
        state[W_AT + i] = zeros()


def init_first_edge(state):
    for i in range(5):
        for j in range(5):
            state[Q_AT + 5 * i + j] = ones() if i == j else zeros()
            state[XQ_AT + 5 * i + j] = zeros()
        state[Y_AT + i] = zeros()


def accumulate(state, r, x, w):
    q = load_mat(state, Q_AT)
    xq = load_mat(state, XQ_AT)
    y = load_vec(state, Y_AT)
    moved = mat_cols(q, columns_of(r) + columns_of(x) + [w])
    q_new = [[q[i][j] - moved[j][i] for j in range(5)] for i in range(5)]
    xq_new = [[xq[i][j] - moved[5 + j][i] for j in range(5)] for i in range(5)]
    y_new = [y[i] - moved[10][i] for i in range(5)]
    store_mat(state, Q_AT, q_new)
    store_mat(state, XQ_AT, xq_new)
    store_vec(state, Y_AT, y_new)
    return q_new, xq_new, y_new


def local_relation(speed, excess, right, r, x, w):
    cols = mat_cols(speed, columns_of(r) + columns_of(x) + [w])
    s = [[r[i][j] + cols[j][i] for j in range(5)] for i in range(5)]
    xn = [[x[i][j] + cols[5 + j][i] for j in range(5)] for i in range(5)]
    for i in range(5):
        s[i][i] = s[i][i] + excess
        xn[i][i] = xn[i][i] + excess
    g = [right[i] - w[i] - cols[10][i] for i in range(5)]
    return s, xn, g


def sweep_step(k, state, fac_ref, slot, get_cell):
    @pl.when(k == 1)
    def _():
        init_first_edge(state)

    r = load_mat(state, R_AT)
    x = load_mat(state, X_AT)
    w = load_vec(state, W_AT)
    speed, excess, right = get_cell(k)
    s, xn, g = local_relation(speed, excess, right, r, x, w)
    t = [[s[i][j] - speed[i][j] for j in range(5)] for i in range(5)]
    for i in range(5):
        t[i][i] = t[i][i] + 1.0
    solved = solve(t, columns_of(s) + columns_of(xn) + [g])
    r_new = rows_of(solved[:5])
    x_new = rows_of(solved[5:10])
    w_new = [-value for value in solved[10]]
    accumulate(state, r, x, w)
    store_mat(state, R_AT, r_new)
    store_mat(state, X_AT, x_new)
    store_vec(state, W_AT, w_new)
    for i in range(5):
        for j in range(5):
            fac_ref[slot, 5 * i + j] = r_new[i][j]
            fac_ref[slot, 25 + 5 * i + j] = x_new[i][j]
        fac_ref[slot, 50 + i] = w_new[i]


def even_rows():
    return lax.broadcasted_iota(jnp.int32, (8, 128), 0) % 2 == 0


def finish_sweep(first, state, port, port_ref, mid_ref, get_cell, prev_speed):
    r = load_mat(state, R_AT)
    x = load_mat(state, X_AT)
    w = load_vec(state, W_AT)
    q, xq, y = accumulate(state, r, x, w)
    speed, excess, right = get_cell(HALF - 1)
    s, xn, g = local_relation(speed, excess, right, r, x, w)

    def from_second(value):
        return pltpu.roll(value, 7, 0)

    q1 = [[from_second(e) for e in row] for row in q]
    xq1 = [[from_second(e) for e in row] for row in xq]
    y1 = [from_second(e) for e in y]
    cols = mat_cols(speed, columns_of(q1) + columns_of(xq1) + [y1])
    qq = [[q1[i][j] - cols[j][i] for j in range(5)] for i in range(5)]
    xx = [[xq1[i][j] - cols[5 + j][i] for j in range(5)] for i in range(5)]
    yy = [y1[i] - cols[10][i] for i in range(5)]
    t = [[s[i][j] + qq[i][j] - xx[i][j] for j in range(5)] for i in range(5)]
    mx_right = [[xx[i][j] - xn[i][j] for j in range(5)] for i in range(5)]
    m0_right = [yy[i] + g[i] for i in range(5)]
    solved = solve(t, columns_of(qq) + columns_of(mx_right) + [m0_right])
    mc, mx, m0 = rows_of(solved[:5]), rows_of(solved[5:10]), solved[10]
    for i in range(5):
        for j in range(5):
            mid_ref[5 * i + j] = mc[i][j]
            mid_ref[25 + 5 * i + j] = mx[i][j]
        mid_ref[50 + i] = m0[i]
    left = mat_cols(q, solved)
    start = jnp.broadcast_to(first, (8, 128)) > 0
    q_all = [
        [jnp.where(start, 1.0 if i == j else 0.0, left[j][i]) for j in range(5)] for i in range(5)
    ]
    xq_all = [[jnp.where(start, 0.0, xq[i][j] + left[5 + j][i]) for j in range(5)] for i in range(5)]
    y_all = [jnp.where(start, 0.0, y[i] + left[10][i]) for i in range(5)]
    cols = mat_cols(prev_speed, columns_of(q_all) + columns_of(xq_all) + [y_all])
    for i in range(5):
        for j in range(5):
            port[pl.ds(8 * (55 + 5 * i + j), 8), :] = q_all[i][j] - cols[j][i]
            port[pl.ds(8 * (80 + 5 * i + j), 8), :] = xq_all[i][j] - cols[5 + j][i]
        port[pl.ds(8 * (105 + i), 8), :] = y_all[i] - cols[10][i]
    s1 = [[from_second(e) for e in row] for row in s]
    xn1 = [[from_second(e) for e in row] for row in xn]
    g1 = [from_second(e) for e in g]
    n1 = [[xn1[i][j] - s1[i][j] for j in range(5)] for i in range(5)]
    cols = mat_cols(n1, solved)
    for i in range(5):
        for j in range(5):
            port[pl.ds(8 * (5 * i + j), 8), :] = s1[i][j] + cols[j][i]
            port[pl.ds(8 * (25 + 5 * i + j), 8), :] = xn1[i][j] + cols[5 + j][i]
        port[pl.ds(8 * (50 + i), 8), :] = g1[i] - cols[10][i]
    for e in range(110, 128):
        port[pl.ds(8 * e, 8), :] = zeros()
    for z in range(4):
        port_ref[pl.ds(128 * z, 128), :] = port[pl.ds(2 * z, 128, stride=8), :].T


def cell_rows(k):
    return pl.ds(k, 8, stride=HALF)


def read_prev_speed(up_ref, rows8):
    for z in range(4):
        value = 1.0 / (up_ref[pl.ds(20 + z, 1), :] * up_ref[pl.ds(24, 1), :])
        rows8[pl.ds(2 * z, 1), :] = value
        rows8[pl.ds(2 * z + 1, 1), :] = value
    scale = rows8[...]
    entries = jnp.broadcast_to(up_ref[pl.ds(25, 1), :], (8, 128))
    return [[scale * lane(entries, 5 * i + j) for j in range(5)] for i in range(5)]


def run_chunk(state, fac_ref, get_cell):
    step = pl.program_id(0)
    count = jnp.where(step == STEPS - 1, CHUNK - 1, CHUNK)

    def one(slot, carry):
        sweep_step(step * CHUNK + slot, state, fac_ref, slot, get_cell)
        return carry

    lax.fori_loop(0, count, one, 0)


def forward_x_kernel(
    first_ref, last_ref, q_ref, visc_ref, mx_ref, my_ref, jacx_ref, jacy_ref,
    west_ref, east_ref, south_ref, north_ref,
    fac_ref, port_ref, mid_ref,
    state, eps, dlt, g1, g2, tab, tin, before, after, port, rows8,
):
    step = pl.program_id(0)

    @pl.when(step == 0)
    def _():
        init_state(state)
        init_first_edge(state)
        mx = mx_ref[...]
        my = my_ref[...]
        not_first = jnp.where(first_ref[1] > 0, 0.0, 1.0)
        not_last = jnp.where(last_ref[1] > 0, 0.0, 1.0)
        tin[...] = jnp.zeros((128, 128), F32)
        tin[pl.ds(0, 25), :] = jacx_ref[...]
        for z in range(4):
            rows = pl.ds(128 * z, 128)
            visc = visc_ref[rows, :]
            e = 1.0 / (visc * mx)
            d = e * e * visc
            eps[rows, :] = e
            dlt[rows, :] = d
            g2[rows, :] = d * my
            g1[rows, :] = (d * my) * (my * visc)
            for c in range(5):
                tin[pl.ds(25 + c, 1), :] = south_ref[pl.ds(4 * c + z, 1), :] * not_first
                tin[pl.ds(30 + c, 1), :] = north_ref[pl.ds(4 * c + z, 1), :] * not_last
            tab[rows, :] = tin[...].T
        even = even_rows()
        open_first = jnp.where(first_ref[0] > 0, 0.0, 1.0)
        open_last = jnp.where(last_ref[0] > 0, 0.0, 1.0)
        for c in range(5):
            for z in range(4):
                before[c, pl.ds(2 * z, 1), :] = west_ref[pl.ds(4 * c + z, 1), :] * open_first
                before[c, pl.ds(2 * z + 1, 1), :] = q_ref[c, pl.ds(128 * z + HALF - 1, 1), :]
                after[c, pl.ds(2 * z, 1), :] = q_ref[c, pl.ds(128 * z + HALF, 1), :]
                after[c, pl.ds(2 * z + 1, 1), :] = east_ref[pl.ds(4 * c + z, 1), :] * open_last

    lanes = lax.broadcasted_iota(jnp.int32, (8, 128), 1)

    def get_cell(k):
        rows = cell_rows(k)
        table = tab[rows, :]
        e = eps[rows, :]
        d = dlt[rows, :]
        speed = [[e * lane(table, 5 * i + j) for j in range(5)] for i in range(5)]
        at_start = k == 0
        at_end = k == HALF - 1
        back = cell_rows(jnp.maximum(k - 1, 0))
        ahead = cell_rows(jnp.minimum(k + 1, HALF - 1))
        diff_x, diff_y, second_x, second_y = [], [], [], []
        for c in range(5):
            here = q_ref[c, rows, :]
            west = jnp.where(at_start, before[c], q_ref[c, back, :])
            east = jnp.where(at_end, after[c], q_ref[c, ahead, :])
            south = jnp.where(lanes == 0, lane(table, 25 + c), pltpu.roll(here, 1, 1))
            north = jnp.where(lanes == 127, lane(table, 30 + c), pltpu.roll(here, 127, 1))
            diff_x.append(east - west)
            diff_y.append(north - south)
            second_x.append((east - 2.0 * here) + west)
            second_y.append((north - 2.0 * here) + south)
        a, b = g1[rows, :], g2[rows, :]
        convect_x = mat_cols(speed, [diff_x])[0]
        right = []
        for i in range(5):
            total = jacy_ref[pl.ds(5 * i, 1), :] * diff_y[0]
            for j in range(1, 5):
                total = total + jacy_ref[pl.ds(5 * i + j, 1), :] * diff_y[j]
            right.append((second_x[i] - convect_x[i]) + (a * second_y[i] - b * total))
        return speed, d, right

    run_chunk(state, fac_ref, get_cell)

    @pl.when(step == STEPS - 1)
    def _():
        speed = read_prev_speed(west_ref, rows8)
        finish_sweep(first_ref[0], state, port, port_ref, mid_ref, get_cell, speed)


def forward_y_kernel(
    first_ref, p_ref, visc_ref, my_ref, jacy_ref, south_ref,
    fac_ref, port_ref, mid_ref,
    state, field, eps, dlt, tab, tin, port, rows8,
):
    step = pl.program_id(0)

    @pl.when(step == 0)
    def _():
        init_state(state)
        init_first_edge(state)
        my = my_ref[...].T
        tin[...] = jnp.zeros((128, 128), F32)
        tin[pl.ds(0, 25), :] = jacy_ref[...]
        table = tin[...].T
        for z in range(4):
            rows = pl.ds(128 * z, 128)
            visc = visc_ref[rows, :].T
            e = 1.0 / (visc * my)
            eps[rows, :] = e
            dlt[rows, :] = e * e * visc
            tab[rows, :] = table
            for c in range(5):
                field[c, rows, :] = p_ref[c, rows, :].T

    def get_cell(k):
        rows = cell_rows(k)
        table = tab[rows, :]
        e = eps[rows, :]
        d = dlt[rows, :]
        speed = [[e * lane(table, 5 * i + j) for j in range(5)] for i in range(5)]
        return speed, d, [d * field[c, rows, :] for c in range(5)]

    run_chunk(state, fac_ref, get_cell)

    @pl.when(step == STEPS - 1)
    def _():
        speed = read_prev_speed(south_ref, rows8)
        finish_sweep(first_ref[1], state, port, port_ref, mid_ref, get_cell, speed)


def reduced_kernel(count, lines, in_ref, out_ref, ports, gains):
    per = 128 // lines
    for group in range(count // per):
        turned = in_ref[pl.ds(128 * group, 128), :].T
        for q in range(per):
            ports[group * per + q] = turned if q == 0 else pltpu.roll(turned, 128 - lines * q, 1)

    def entry(piece, index):
        return ports[piece, pl.ds(index, 1), :]

    def matrix(piece, base):
        return [[entry(piece, base + 5 * i + j) for j in range(5)] for i in range(5)]

    def vector(piece, base):
        return [entry(piece, base + i) for i in range(5)]

    def eliminate(piece, following, s, g):
        qq, xx, yy = matrix(following, 55), matrix(following, 80), vector(following, 105)
        reduced = [[s[i][j] - xx[i][j] for j in range(5)] for i in range(5)]
        t = [[reduced[i][j] + qq[i][j] for j in range(5)] for i in range(5)]
        rhs = [yy[i] + g[i] for i in range(5)]
        solved = solve(t, columns_of(reduced) + [rhs])
        h, v = rows_of(solved[:5]), solved[5]
        for i in range(5):
            for j in range(5):
                gains[piece, pl.ds(5 * i + j, 1), :] = h[i][j]
            gains[piece, pl.ds(25 + i, 1), :] = v[i]

    eliminate(0, 1, matrix(0, 0), vector(0, 50))

    def forward(piece, carry):
        h = [[gains[piece - 1, pl.ds(5 * i + j, 1), :] for j in range(5)] for i in range(5)]
        v = [gains[piece - 1, pl.ds(25 + i, 1), :] for i in range(5)]
        s, xn, g = matrix(piece, 0), matrix(piece, 25), vector(piece, 50)
        gain = [[(1.0 if i == j else 0.0) - h[i][j] for j in range(5)] for i in range(5)]
        part = mat_cols(s, columns_of(h))
        rest = mat_cols(xn, columns_of(gain))
        s_all = [[part[j][i] + rest[j][i] for j in range(5)] for i in range(5)]
        difference = [[s[i][j] - xn[i][j] for j in range(5)] for i in range(5)]
        moved = mat_cols(difference, [v])[0]
        g_all = [g[i] + moved[i] for i in range(5)]
        eliminate(piece, lax.rem(piece + 1, count), s_all, g_all)
        return carry

    lax.fori_loop(1, count, forward, 0)
    out_ref[...] = jnp.zeros((count, 16, 128), F32)

    def backward(at, following):
        piece = count - 1 - at
        h = [[gains[piece, pl.ds(5 * i + j, 1), :] for j in range(5)] for i in range(5)]
        v = [gains[piece, pl.ds(25 + i, 1), :] for i in range(5)]
        moved = mat_cols(h, [list(following)])[0]
        here = tuple((following[i] - moved[i]) + v[i] for i in range(5))
        for i in range(5):
            out_ref[piece, pl.ds(5 + i, 1), :] = here[i]

        @pl.when(piece + 1 < count)
        def _():
            for i in range(5):
                out_ref[piece + 1, pl.ds(i, 1), :] = here[i]

        return here

    start = tuple(jnp.zeros((1, 128), F32) for _ in range(5))
    lax.fori_loop(0, count, backward, start)


def begin_backward(count, lines, ends_ref, mid_ref, edge, ends8):
    per = 128 // lines
    lanes = lax.broadcasted_iota(jnp.int32, (16, 128), 1)
    for z in range(4):
        block = ends_ref[per * z]
        for q in range(1, per):
            moved = pltpu.roll(ends_ref[per * z + q], lines * q, 1)
            block = jnp.where(lanes >= lines * q, moved, block)
        for e in range(10):
            ends8[e, pl.ds(2 * z, 1), :] = block[e : e + 1]
            ends8[e, pl.ds(2 * z + 1, 1), :] = block[e : e + 1]
    a = [ends8[i] for i in range(5)]
    c = [ends8[5 + i] for i in range(5)]
    gap = [c[i] - a[i] for i in range(5)]
    part = mat_cols(load_mat(mid_ref, 0), [gap])[0]
    rest = mat_cols(load_mat(mid_ref, 25), [a])[0]
    even = even_rows()
    for i in range(5):
        middle = a[i] + ((part[i] + rest[i]) + mid_ref[50 + i])
        edge[i] = jnp.where(even, a[i], pltpu.roll(middle, 1, 0))
        edge[5 + i] = jnp.where(even, middle, c[i])


def backward_chunk(fac_ref, edge, out):
    step = pl.program_id(0)
    a = [edge[i] for i in range(5)]
    begin = jnp.where(step == 0, 1, 0)

    def one(at, following):
        slot = CHUNK - 1 - at
        k = (STEPS - 1 - step) * CHUNK + slot
        gap = [following[i] - a[i] for i in range(5)]
        r = [[fac_ref[slot, 5 * i + j] for j in range(5)] for i in range(5)]
        x = [[fac_ref[slot, 25 + 5 * i + j] for j in range(5)] for i in range(5)]
        part = mat_cols(r, [gap])[0]
        rest = mat_cols(x, [a])[0]
        here = tuple(
            following[i] - ((part[i] + rest[i]) + fac_ref[slot, 50 + i]) for i in range(5)
        )
        for i in range(5):
            out[i, cell_rows(k), :] = here[i]
        return here

    final = lax.fori_loop(begin, CHUNK, one, tuple(edge[5 + i] for i in range(5)))
    for i in range(5):
        edge[5 + i] = final[i]


def backward_x_kernel(count, lines, fac_ref, mid_ref, ends_ref, out_ref, edge, ends8):
    @pl.when(pl.program_id(0) == 0)
    def _():
        begin_backward(count, lines, ends_ref, mid_ref, edge, ends8)
        for i in range(5):
            out_ref[i, cell_rows(HALF - 1), :] = edge[5 + i]

    backward_chunk(fac_ref, edge, out_ref)


def backward_y_kernel(count, lines, fac_ref, mid_ref, ends_ref, out_ref, edge, ends8, field):
    @pl.when(pl.program_id(0) == 0)
    def _():
        begin_backward(count, lines, ends_ref, mid_ref, edge, ends8)
        for i in range(5):
            field[i, cell_rows(HALF - 1), :] = edge[5 + i]

    backward_chunk(fac_ref, edge, field)

    @pl.when(pl.program_id(0) == STEPS - 1)
    def _():
        for c in range(5):
            for z in range(4):
                rows = pl.ds(128 * z, 128)
                out_ref[c, rows, :] = field[c, rows, :].T


def whole(shape):
    return pl.BlockSpec(shape, lambda i: (0,) * len(shape))


def scalars():
    return pl.BlockSpec(memory_space=pltpu.SMEM)


def params():
    return pltpu.CompilerParams(
        dimension_semantics=("arbitrary",), vmem_limit_bytes=VMEM_LIMIT
    )


FORWARD_OUT = (
    jax.ShapeDtypeStruct((HALF, 55, 8, 128), F32),
    jax.ShapeDtypeStruct((512, 128), F32),
    jax.ShapeDtypeStruct((55, 8, 128), F32),
)


def forward_specs():
    return (
        pl.BlockSpec((CHUNK, 55, 8, 128), lambda i: (i, 0, 0, 0)),
        whole((512, 128)),
        whole((55, 8, 128)),
    )


def plane():
    return pltpu.VMEM((512, 128), F32)


def forward_x(first, last, q, visc, mx, my, jacx, jacy, west, east, south, north):
    return pl.pallas_call(
        forward_x_kernel,
        grid=(STEPS,),
        in_specs=[scalars(), scalars()]
        + [whole(v.shape) for v in (q, visc, mx, my, jacx, jacy, west, east, south, north)],
        out_specs=forward_specs(),
        out_shape=FORWARD_OUT,
        scratch_shapes=[pltpu.VMEM((STATE, 8, 128), F32)]
        + [plane() for _ in range(5)]
        + [
            pltpu.VMEM((128, 128), F32),
            pltpu.VMEM((5, 8, 128), F32),
            pltpu.VMEM((5, 8, 128), F32),
            pltpu.VMEM((1024, 128), F32),
            pltpu.VMEM((8, 128), F32),
        ],
        compiler_params=params(),
        name="forward_x",
    )(first, last, q, visc, mx, my, jacx, jacy, west, east, south, north)


def forward_y(first, p, visc, my, jacy, south):
    return pl.pallas_call(
        forward_y_kernel,
        grid=(STEPS,),
        in_specs=[scalars()] + [whole(v.shape) for v in (p, visc, my, jacy, south)],
        out_specs=forward_specs(),
        out_shape=FORWARD_OUT,
        scratch_shapes=[pltpu.VMEM((STATE, 8, 128), F32), pltpu.VMEM((5, 512, 128), F32)]
        + [plane() for _ in range(3)]
        + [
            pltpu.VMEM((128, 128), F32),
            pltpu.VMEM((1024, 128), F32),
            pltpu.VMEM((8, 128), F32),
        ],
        compiler_params=params(),
        name="forward_y",
    )(first, p, visc, my, jacy, south)


def reduced(port, axis):
    count = lax.axis_size(axis)
    lines = 512 // count
    received = lax.all_to_all(
        port.reshape(count, lines, 128), axis, split_axis=0, concat_axis=0, tiled=True
    )
    ends = pl.pallas_call(
        functools.partial(reduced_kernel, count, lines),
        out_shape=jax.ShapeDtypeStruct((count, 16, 128), F32),
        in_specs=[pl.BlockSpec(memory_space=pltpu.VMEM)],
        out_specs=pl.BlockSpec(memory_space=pltpu.VMEM),
        scratch_shapes=[
            pltpu.VMEM((count, 128, 128), F32),
            pltpu.VMEM((count, 32, 128), F32),
        ],
        compiler_params=pltpu.CompilerParams(vmem_limit_bytes=VMEM_LIMIT),
        name="reduced_" + axis,
    )(received.reshape(512, 128))
    return lax.all_to_all(ends, axis, split_axis=0, concat_axis=0, tiled=True)


def backward(kernel, name, fac, mid, ends, extra):
    count = ends.shape[0]
    return pl.pallas_call(
        functools.partial(kernel, count, 512 // count),
        grid=(STEPS,),
        in_specs=[
            pl.BlockSpec((CHUNK, 55, 8, 128), lambda i: (STEPS - 1 - i, 0, 0, 0)),
            whole(mid.shape),
            whole(ends.shape),
        ],
        out_specs=whole((5, 512, 128)),
        out_shape=jax.ShapeDtypeStruct((5, 512, 128), F32),
        scratch_shapes=[pltpu.VMEM((10, 8, 128), F32), pltpu.VMEM((10, 8, 128), F32)] + extra,
        compiler_params=params(),
        name=name,
    )(fac, mid, ends)


def halos(axis, last, initial):
    devices = lax.axis_size(axis)
    up = [(i, (i + 1) % devices) for i in range(devices)]
    down = [(j, i) for i, j in up]
    return lax.ppermute(last, axis, up), lax.ppermute(initial, axis, down)


def body(flow_state, viscosity, metric_x, metric_y, jacobian_x, jacobian_y):
    spots = [lax.axis_index("row"), lax.axis_index("col")]
    sizes = [lax.axis_size("row"), lax.axis_size("col")]
    first = jnp.stack([(spot == 0).astype(jnp.int32) for spot in spots])
    last = jnp.stack([(spot == n - 1).astype(jnp.int32) for spot, n in zip(spots, sizes)])
    jacx = jacobian_x.reshape(25, 128)
    jacy = jacobian_y.reshape(25, 128)

    def last_cell(state, visc, metric, jac):
        entries = jnp.pad(jac[:, 127], (0, 103))[None]
        return jnp.concatenate([state.reshape(20, 128), visc, metric[None], entries], axis=0)

    west, east = halos(
        "row",
        last_cell(flow_state[:, :, 127], viscosity[:, 127], metric_x[127], jacx),
        flow_state[:, :, 0].reshape(20, 128),
    )
    south, north = halos(
        "col",
        last_cell(flow_state[:, :, :, 127], viscosity[:, :, 127], metric_y[:, 127], jacy),
        flow_state[:, :, :, 0].reshape(20, 128),
    )
    q = flow_state.reshape(5, 512, 128)
    visc = viscosity.reshape(512, 128)
    fac, port, mid = forward_x(
        first, last, q, visc, metric_x, metric_y, jacx, jacy, west, east, south, north
    )
    ends = reduced(port, "row")
    partial_value = backward(backward_x_kernel, "backward_x", fac, mid, ends, [])
    fac, port, mid = forward_y(first, partial_value, visc, metric_y, jacy, south)
    ends = reduced(port, "col")
    result = backward(
        backward_y_kernel, "backward_y", fac, mid, ends, [pltpu.VMEM((5, 512, 128), F32)]
    )
    return result.reshape(5, 4, 128, 128)


def solution(mesh):
    return jax.shard_map(
        body,
        mesh=mesh,
        in_specs=(
            P(None, None, "row", "col"),
            P(None, "row", "col"),
            P("row", "col"),
            P("row", "col"),
            P(None, None, "row"),
            P(None, None, "col"),
        ),
        out_specs=P(None, None, "row", "col"),
        check_vma=False,
    )
```

```python
import functools

import jax
import jax.numpy as jnp
from jax import lax
from jax.experimental import pallas as pl
from jax.experimental.pallas import tpu as pltpu
from jax.sharding import PartitionSpec as P

F32 = jnp.float32
N = 128
HALF = 64
KEPT = HALF // 2
CHUNK = 8
STEPS = KEPT // CHUNK
FACTORS = 60
VMEM_LIMIT = 48 * 1024 * 1024


def zeros():
    return jnp.zeros((8, 128), F32)


def ones():
    return jnp.ones((8, 128), F32)


def lane(value, index):
    return jnp.broadcast_to(value[:, index : index + 1], (8, 128))


def mat_cols(matrix, columns):
    result = []
    for column in columns:
        out = []
        for i in range(5):
            total = matrix[i][0] * column[0]
            for k in range(1, 5):
                total = total + matrix[i][k] * column[k]
            out.append(total)
        result.append(out)
    return result


def solve(matrix, columns):
    m = [list(row) for row in matrix]
    cols = [list(column) for column in columns]
    inverse = []
    for p in range(5):
        inv = 1.0 / m[p][p]
        inverse.append(inv)
        for i in range(p + 1, 5):
            weight = m[i][p] * inv
            for j in range(p + 1, 5):
                m[i][j] = m[i][j] - weight * m[p][j]
            for column in cols:
                column[i] = column[i] - weight * column[p]
    for column in cols:
        for i in range(4, -1, -1):
            total = column[i]
            for j in range(i + 1, 5):
                total = total - m[i][j] * column[j]
            column[i] = total * inverse[i]
    return cols


def columns_of(matrix):
    return [[matrix[i][j] for i in range(5)] for j in range(5)]


def rows_of(columns):
    return [[columns[j][i] for j in range(5)] for i in range(5)]


def load_mat(ref, base):
    return [[ref[base + 5 * i + j] for j in range(5)] for i in range(5)]


def load_vec(ref, base):
    return [ref[base + i] for i in range(5)]


def store_mat(ref, base, matrix):
    for i in range(5):
        for j in range(5):
            ref[base + 5 * i + j] = matrix[i][j]


def store_vec(ref, base, vector):
    for i in range(5):
        ref[base + i] = vector[i]


R_AT, X_AT, W_AT, Q_AT, XQ_AT, Y_AT, STATE = 0, 25, 50, 55, 80, 105, 110


def init_state(state):
    for i in range(5):
        for j in range(5):
            state[R_AT + 5 * i + j] = ones() if i == j else zeros()
            state[X_AT + 5 * i + j] = zeros()
        state[W_AT + i] = zeros()


def init_first_edge(state):
    for i in range(5):
        for j in range(5):
            state[Q_AT + 5 * i + j] = ones() if i == j else zeros()
            state[XQ_AT + 5 * i + j] = zeros()
        state[Y_AT + i] = zeros()


def accumulate(state, r, x, w):
    q = load_mat(state, Q_AT)
    xq = load_mat(state, XQ_AT)
    y = load_vec(state, Y_AT)
    moved = mat_cols(q, columns_of(r) + columns_of(x) + [w])
    q_new = [[q[i][j] - moved[j][i] for j in range(5)] for i in range(5)]
    xq_new = [[xq[i][j] - moved[5 + j][i] for j in range(5)] for i in range(5)]
    y_new = [y[i] - moved[10][i] for i in range(5)]
    store_mat(state, Q_AT, q_new)
    store_mat(state, XQ_AT, xq_new)
    store_vec(state, Y_AT, y_new)
    return q_new, xq_new, y_new


def table_mat(table, base):
    return [[lane(table, base + 5 * i + j) for j in range(5)] for i in range(5)]


def kept_equation(m, source, tab, eps, dlt, last):
    k = 2 * m + 1
    here, back = cell_rows(k), cell_rows(k - 1)
    table = tab[here, :]
    e0, d0 = eps[here, :], dlt[here, :]
    em, dm = eps[back, :], dlt[back, :]
    cm = 1.0 / (2.0 + dm)
    a = table_mat(table, 0)
    a1, a2 = cm * e0, cm * em
    a3 = a1 * em
    am, aam = table_mat(tab[back, :], 0), table_mat(table, 35)
    lower = [
        [(a1 * a[i][j] + a2 * am[i][j]) + a3 * aam[i][j] for j in range(5)] for i in range(5)
    ]
    fm, f0, fp = source
    low = cm * dm
    if last:
        shift, tilt = d0 + low, e0 * low
        first = [cm * fm[i] for i in range(5)]
        second = first
    else:
        ahead = cell_rows(k + 1)
        ep, dp = eps[ahead, :], dlt[ahead, :]
        cp = 1.0 / (2.0 + dp)
        b1, b2 = cp * e0, cp * ep
        b3 = b1 * ep
        ap, aap = table_mat(tab[ahead, :], 0), table_mat(table, 60)
        upper = [
            [b3 * aap[i][j] - (b1 * a[i][j] + b2 * ap[i][j]) for j in range(5)] for i in range(5)
        ]
        high = cp * dp
        shift, tilt = d0 + (low + high), e0 * (low - high)
        first = [cm * fm[i] + cp * fp[i] for i in range(5)]
        second = [cm * fm[i] - cp * fp[i] for i in range(5)]
    excess = [[tilt * a[i][j] for j in range(5)] for i in range(5)]
    for i in range(5):
        excess[i][i] = excess[i][i] + shift
        lower[i][i] = lower[i][i] + cm
        if not last:
            upper[i][i] = upper[i][i] + cp
    moved = mat_cols(a, [[e0 * value for value in second]])[0]
    right = [(f0[i] + first[i]) + moved[i] for i in range(5)]
    if last:
        speed = [[e0 * a[i][j] for j in range(5)] for i in range(5)]
        return lower, excess, right, speed
    return lower, excess, right, upper


def local_relation(lower, excess, right, r, x, w):
    cols = mat_cols(lower, columns_of(r) + columns_of(x) + [w])
    s = [[cols[j][i] + excess[i][j] for j in range(5)] for i in range(5)]
    xn = [[cols[5 + j][i] + excess[i][j] for j in range(5)] for i in range(5)]
    g = [right[i] - cols[10][i] for i in range(5)]
    return s, xn, g


def sweep_step(m, state, fac_ref, slot, raw, keep, tables):
    @pl.when(m == 1)
    def _():
        init_first_edge(state)

    r = load_mat(state, R_AT)
    x = load_mat(state, X_AT)
    w = load_vec(state, W_AT)
    fm = load_vec(keep, 0)
    f0, fp = raw(2 * m + 1), raw(2 * m + 2)
    lower, excess, right, upper = kept_equation(m, (fm, f0, fp), *tables, False)
    s, xn, g = local_relation(lower, excess, right, r, x, w)
    t = [[s[i][j] + upper[i][j] for j in range(5)] for i in range(5)]
    solved = solve(t, columns_of(s) + columns_of(xn) + [g])
    r_new = rows_of(solved[:5])
    x_new = rows_of(solved[5:10])
    w_new = [-value for value in solved[10]]
    accumulate(state, r, x, w)
    store_mat(state, R_AT, r_new)
    store_mat(state, X_AT, x_new)
    store_vec(state, W_AT, w_new)
    store_vec(keep, 0, fp)
    for i in range(5):
        for j in range(5):
            fac_ref[slot, 5 * i + j] = r_new[i][j]
            fac_ref[slot, 25 + 5 * i + j] = x_new[i][j]
        fac_ref[slot, 50 + i] = w_new[i]
        fac_ref[slot, 55 + i] = fp[i]


def even_rows():
    return lax.broadcasted_iota(jnp.int32, (8, 128), 0) % 2 == 0


def finish_sweep(first, state, port, port_ref, mid_ref, raw, keep, tables):
    tab, eps, dlt = tables
    r = load_mat(state, R_AT)
    x = load_mat(state, X_AT)
    w = load_vec(state, W_AT)
    q, xq, y = accumulate(state, r, x, w)
    rows = cell_rows(0)
    e0, d0 = eps[rows, :], dlt[rows, :]
    c0 = 1.0 / (2.0 + d0)
    start_speed = [[e0 * value for value in row] for row in table_mat(tab[rows, :], 0)]
    cols = mat_cols(start_speed, columns_of(q) + columns_of(xq) + [y])
    q = [[c0 * (q[i][j] - cols[j][i]) for j in range(5)] for i in range(5)]
    xq = [[c0 * (xq[i][j] - cols[5 + j][i]) for j in range(5)] for i in range(5)]
    for i in range(5):
        xq[i][i] = xq[i][i] - c0 * d0
    y = [c0 * ((y[i] - cols[10][i]) + mid_ref[55 + i]) for i in range(5)]
    source = (load_vec(keep, 0), raw(HALF - 1), None)
    lower, excess, right, speed = kept_equation(KEPT - 1, source, tab, eps, dlt, True)
    s, xn, g = local_relation(lower, excess, right, r, x, w)
    ahead = [[(1.0 if i == j else 0.0) - speed[i][j] for j in range(5)] for i in range(5)]
    scaled = solve(ahead, columns_of(s) + columns_of(xn) + [g])
    s, xn, g = rows_of(scaled[:5]), rows_of(scaled[5:10]), scaled[10]

    def from_second(value):
        return pltpu.roll(value, 7, 0)

    q1 = [[from_second(e) for e in row] for row in q]
    xq1 = [[from_second(e) for e in row] for row in xq]
    y1 = [from_second(e) for e in y]
    t = [[s[i][j] + (q1[i][j] - xq1[i][j]) for j in range(5)] for i in range(5)]
    mx_right = [[xq1[i][j] - xn[i][j] for j in range(5)] for i in range(5)]
    m0_right = [y1[i] + g[i] for i in range(5)]
    solved = solve(t, columns_of(q1) + columns_of(mx_right) + [m0_right])
    mc, mx, m0 = rows_of(solved[:5]), rows_of(solved[5:10]), solved[10]
    for i in range(5):
        for j in range(5):
            mid_ref[5 * i + j] = mc[i][j]
            mid_ref[25 + 5 * i + j] = mx[i][j]
        mid_ref[50 + i] = m0[i]
    left = mat_cols(q, solved)
    start = jnp.broadcast_to(first, (8, 128)) > 0
    s1 = [[from_second(e) for e in row] for row in s]
    xn1 = [[from_second(e) for e in row] for row in xn]
    g1 = [from_second(e) for e in g]
    n1 = [[xn1[i][j] - s1[i][j] for j in range(5)] for i in range(5)]
    cols = mat_cols(n1, solved)
    for i in range(5):
        for j in range(5):
            at = 5 * i + j
            unit = 1.0 if i == j else 0.0
            port[pl.ds(8 * at, 8), :] = s1[i][j] + cols[j][i]
            port[pl.ds(8 * (25 + at), 8), :] = xn1[i][j] + cols[5 + j][i]
            port[pl.ds(8 * (55 + at), 8), :] = jnp.where(start, unit, left[j][i])
            port[pl.ds(8 * (80 + at), 8), :] = jnp.where(start, 0.0, xq[i][j] + left[5 + j][i])
        port[pl.ds(8 * (50 + i), 8), :] = g1[i] - cols[10][i]
        port[pl.ds(8 * (105 + i), 8), :] = jnp.where(start, 0.0, y[i] + left[10][i])
    for e in range(110, 128):
        port[pl.ds(8 * e, 8), :] = zeros()
    for z in range(4):
        port_ref[pl.ds(128 * z, 128), :] = port[pl.ds(2 * z, 128, stride=8), :].T


def cell_rows(k):
    return pl.ds(k, 8, stride=HALF)


def start_tables(jac_ref, tin, turned):
    tin[...] = jnp.zeros((128, 128), F32)
    jac = jac_ref[...]
    tin[pl.ds(0, 25), :] = jac
    for base, shift in ((35, 1), (60, 127)):
        turned[...] = pltpu.roll(jac, shift, 1)
        for i in range(5):
            for j in range(5):
                total = jac_ref[pl.ds(5 * i, 1), :] * turned[pl.ds(j, 1), :]
                for k in range(1, 5):
                    total = total + jac_ref[pl.ds(5 * i + k, 1), :] * turned[pl.ds(5 * k + j, 1), :]
                tin[pl.ds(base + 5 * i + j, 1), :] = total


def start_sweep(state, keep, mid_ref, raw):
    init_state(state)
    init_first_edge(state)
    f = raw(0)
    for i in range(5):
        keep[i] = f[i]
        mid_ref[55 + i] = f[i]


def run_chunk(state, fac_ref, raw, keep, tables):
    step = pl.program_id(0)
    count = jnp.where(step == STEPS - 1, CHUNK - 1, CHUNK)

    def one(slot, carry):
        sweep_step(step * CHUNK + slot, state, fac_ref, slot, raw, keep, tables)
        return carry

    lax.fori_loop(0, count, one, 0)


def forward_x_kernel(
    first_ref, last_ref, q_ref, visc_ref, mx_ref, my_ref, jacx_ref, jacy_ref,
    south_ref, north_ref,
    fac_ref, port_ref, mid_ref, tab, eps, dlt,
    state, keep, g1, g2, tin, turned, port,
):
    step = pl.program_id(0)
    lanes = lax.broadcasted_iota(jnp.int32, (8, 128), 1)

    def raw(k):
        rows = cell_rows(k)
        table = tab[rows, :]
        d, a, b = dlt[rows, :], g1[rows, :], g2[rows, :]
        diff_y, base = [], []
        for c in range(5):
            here = q_ref[c, rows, :]
            south = jnp.where(lanes == 0, lane(table, 25 + c), pltpu.roll(here, 1, 1))
            north = jnp.where(lanes == 127, lane(table, 30 + c), pltpu.roll(here, 127, 1))
            diff_y.append(north - south)
            base.append(d * here + a * ((north - 2.0 * here) + south))
        right = []
        for i in range(5):
            total = jacy_ref[pl.ds(5 * i, 1), :] * diff_y[0]
            for j in range(1, 5):
                total = total + jacy_ref[pl.ds(5 * i + j, 1), :] * diff_y[j]
            right.append(base[i] - b * total)
        return right

    @pl.when(step == 0)
    def _():
        mx = mx_ref[...]
        my = my_ref[...]
        not_first = jnp.where(first_ref[1] > 0, 0.0, 1.0)
        not_last = jnp.where(last_ref[1] > 0, 0.0, 1.0)
        start_tables(jacx_ref, tin, turned)
        for z in range(4):
            rows = pl.ds(128 * z, 128)
            visc = visc_ref[rows, :]
            e = 1.0 / (visc * mx)
            d = e * e * visc
            eps[rows, :] = e
            dlt[rows, :] = d
            g2[rows, :] = d * my
            g1[rows, :] = (d * my) * (my * visc)
            for c in range(5):
                tin[pl.ds(25 + c, 1), :] = south_ref[pl.ds(4 * c + z, 1), :] * not_first
                tin[pl.ds(30 + c, 1), :] = north_ref[pl.ds(4 * c + z, 1), :] * not_last
            tab[rows, :] = tin[...].T
        start_sweep(state, keep, mid_ref, raw)

    tables = (tab, eps, dlt)
    run_chunk(state, fac_ref, raw, keep, tables)

    @pl.when(step == STEPS - 1)
    def _():
        finish_sweep(first_ref[0], state, port, port_ref, mid_ref, raw, keep, tables)


def forward_y_kernel(
    first_ref, p_ref, visc_ref, my_ref, jacy_ref,
    fac_ref, port_ref, mid_ref, tab, eps, dlt,
    state, keep, field, tin, turned, port,
):
    step = pl.program_id(0)

    def raw(k):
        rows = cell_rows(k)
        d = dlt[rows, :]
        return [d * field[c, rows, :] for c in range(5)]

    @pl.when(step == 0)
    def _():
        my = my_ref[...].T
        start_tables(jacy_ref, tin, turned)
        table = tin[...].T
        for z in range(4):
            rows = pl.ds(128 * z, 128)
            visc = visc_ref[rows, :].T
            e = 1.0 / (visc * my)
            eps[rows, :] = e
            dlt[rows, :] = e * e * visc
            tab[rows, :] = table
            for c in range(5):
                field[c, rows, :] = p_ref[c, rows, :].T
        start_sweep(state, keep, mid_ref, raw)

    tables = (tab, eps, dlt)
    run_chunk(state, fac_ref, raw, keep, tables)

    @pl.when(step == STEPS - 1)
    def _():
        finish_sweep(first_ref[1], state, port, port_ref, mid_ref, raw, keep, tables)


def reduced_kernel(count, lines, in_ref, out_ref, ports, gains):
    per = 128 // lines
    for group in range(count // per):
        turned = in_ref[pl.ds(128 * group, 128), :].T
        for q in range(per):
            ports[group * per + q] = turned if q == 0 else pltpu.roll(turned, 128 - lines * q, 1)

    def entry(piece, index):
        return ports[piece, pl.ds(index, 1), :]

    def matrix(piece, base):
        return [[entry(piece, base + 5 * i + j) for j in range(5)] for i in range(5)]

    def vector(piece, base):
        return [entry(piece, base + i) for i in range(5)]

    def eliminate(piece, following, s, g):
        qq, xx, yy = matrix(following, 55), matrix(following, 80), vector(following, 105)
        reduced = [[s[i][j] - xx[i][j] for j in range(5)] for i in range(5)]
        t = [[reduced[i][j] + qq[i][j] for j in range(5)] for i in range(5)]
        rhs = [yy[i] + g[i] for i in range(5)]
        solved = solve(t, columns_of(reduced) + [rhs])
        h, v = rows_of(solved[:5]), solved[5]
        for i in range(5):
            for j in range(5):
                gains[piece, pl.ds(5 * i + j, 1), :] = h[i][j]
            gains[piece, pl.ds(25 + i, 1), :] = v[i]

    eliminate(0, 1, matrix(0, 0), vector(0, 50))

    def forward(piece, carry):
        h = [[gains[piece - 1, pl.ds(5 * i + j, 1), :] for j in range(5)] for i in range(5)]
        v = [gains[piece - 1, pl.ds(25 + i, 1), :] for i in range(5)]
        s, xn, g = matrix(piece, 0), matrix(piece, 25), vector(piece, 50)
        gain = [[(1.0 if i == j else 0.0) - h[i][j] for j in range(5)] for i in range(5)]
        part = mat_cols(s, columns_of(h))
        rest = mat_cols(xn, columns_of(gain))
        s_all = [[part[j][i] + rest[j][i] for j in range(5)] for i in range(5)]
        difference = [[s[i][j] - xn[i][j] for j in range(5)] for i in range(5)]
        moved = mat_cols(difference, [v])[0]
        g_all = [g[i] + moved[i] for i in range(5)]
        eliminate(piece, lax.rem(piece + 1, count), s_all, g_all)
        return carry

    lax.fori_loop(1, count, forward, 0)
    out_ref[...] = jnp.zeros((count, 16, 128), F32)

    def backward(at, following):
        piece = count - 1 - at
        h = [[gains[piece, pl.ds(5 * i + j, 1), :] for j in range(5)] for i in range(5)]
        v = [gains[piece, pl.ds(25 + i, 1), :] for i in range(5)]
        moved = mat_cols(h, [list(following)])[0]
        here = tuple((following[i] - moved[i]) + v[i] for i in range(5))
        for i in range(5):
            out_ref[piece, pl.ds(5 + i, 1), :] = here[i]

        @pl.when(piece + 1 < count)
        def _():
            for i in range(5):
                out_ref[piece + 1, pl.ds(i, 1), :] = here[i]

        return here

    start = tuple(jnp.zeros((1, 128), F32) for _ in range(5))
    lax.fori_loop(0, count, backward, start)


def begin_backward(count, lines, ends_ref, mid_ref, edge, ends8):
    per = 128 // lines
    lanes = lax.broadcasted_iota(jnp.int32, (16, 128), 1)
    for z in range(4):
        block = ends_ref[per * z]
        for q in range(1, per):
            moved = pltpu.roll(ends_ref[per * z + q], lines * q, 1)
            block = jnp.where(lanes >= lines * q, moved, block)
        for e in range(10):
            ends8[e, pl.ds(2 * z, 1), :] = block[e : e + 1]
            ends8[e, pl.ds(2 * z + 1, 1), :] = block[e : e + 1]
    a = [ends8[i] for i in range(5)]
    c = [ends8[5 + i] for i in range(5)]
    gap = [c[i] - a[i] for i in range(5)]
    part = mat_cols(load_mat(mid_ref, 0), [gap])[0]
    rest = mat_cols(load_mat(mid_ref, 25), [a])[0]
    even = even_rows()
    for i in range(5):
        middle = a[i] + ((part[i] + rest[i]) + mid_ref[50 + i])
        edge[i] = jnp.where(even, a[i], pltpu.roll(middle, 1, 0))
        edge[5 + i] = jnp.where(even, middle, c[i])


def between(k, left, right, tables, source):
    tab, eps, dlt = tables
    rows = cell_rows(k)
    e, d = eps[rows, :], dlt[rows, :]
    c = 1.0 / (2.0 + d)
    gap = [right[i] - left[i] for i in range(5)]
    moved = mat_cols(table_mat(tab[rows, :], 0), [[e * value for value in gap]])[0]
    return [
        right[i] - c * ((gap[i] + moved[i]) + (d * right[i] - source[i])) for i in range(5)
    ]


def backward_chunk(fac_ref, mid_ref, edge, write, tables):
    step = pl.program_id(0)
    a = [edge[i] for i in range(5)]
    begin = jnp.where(step == 0, 1, 0)

    def one(at, following):
        slot = CHUNK - 1 - at
        m = (STEPS - 1 - step) * CHUNK + slot
        gap = [following[i] - a[i] for i in range(5)]
        r = [[fac_ref[slot, 5 * i + j] for j in range(5)] for i in range(5)]
        x = [[fac_ref[slot, 25 + 5 * i + j] for j in range(5)] for i in range(5)]
        part = mat_cols(r, [gap])[0]
        rest = mat_cols(x, [a])[0]
        here = tuple(
            following[i] - ((part[i] + rest[i]) + fac_ref[slot, 50 + i]) for i in range(5)
        )
        source = [fac_ref[slot, 55 + i] for i in range(5)]
        write(2 * m + 2, between(2 * m + 2, here, following, tables, source))
        write(2 * m + 1, here)
        return here

    final = lax.fori_loop(begin, CHUNK, one, tuple(edge[5 + i] for i in range(5)))
    for i in range(5):
        edge[5 + i] = final[i]

    @pl.when(step == STEPS - 1)
    def _():
        write(0, between(0, a, final, tables, [mid_ref[55 + i] for i in range(5)]))


def backward_x_kernel(
    count, lines, fac_ref, mid_ref, ends_ref, tab, eps, dlt, q_ref, out_ref, edge, ends8
):
    def write(k, value):
        rows = cell_rows(k)
        for i in range(5):
            out_ref[i, rows, :] = value[i] - q_ref[i, rows, :]

    @pl.when(pl.program_id(0) == 0)
    def _():
        begin_backward(count, lines, ends_ref, mid_ref, edge, ends8)
        write(HALF - 1, [edge[5 + i] for i in range(5)])

    backward_chunk(fac_ref, mid_ref, edge, write, (tab, eps, dlt))


def backward_y_kernel(
    count, lines, fac_ref, mid_ref, ends_ref, tab, eps, dlt, out_ref, edge, ends8, field
):
    def write(k, value):
        for i in range(5):
            field[i, cell_rows(k), :] = value[i]

    @pl.when(pl.program_id(0) == 0)
    def _():
        begin_backward(count, lines, ends_ref, mid_ref, edge, ends8)
        write(HALF - 1, [edge[5 + i] for i in range(5)])

    backward_chunk(fac_ref, mid_ref, edge, write, (tab, eps, dlt))

    @pl.when(pl.program_id(0) == STEPS - 1)
    def _():
        for c in range(5):
            for z in range(4):
                rows = pl.ds(128 * z, 128)
                out_ref[c, rows, :] = field[c, rows, :].T


def whole(shape):
    return pl.BlockSpec(shape, lambda i: (0,) * len(shape))


def scalars():
    return pl.BlockSpec(memory_space=pltpu.SMEM)


def params():
    return pltpu.CompilerParams(
        dimension_semantics=("arbitrary",), vmem_limit_bytes=VMEM_LIMIT
    )


PLANE = (512, 128)
FORWARD_OUT = tuple(
    jax.ShapeDtypeStruct(shape, F32)
    for shape in ((KEPT, FACTORS, 8, 128), PLANE, (60, 8, 128), PLANE, PLANE, PLANE)
)


def forward_specs():
    block = pl.BlockSpec((CHUNK, FACTORS, 8, 128), lambda i: (i, 0, 0, 0))
    return (block,) + tuple(whole(value.shape) for value in FORWARD_OUT[1:])


def forward_scratch(fields):
    return (
        [pltpu.VMEM((STATE, 8, 128), F32), pltpu.VMEM((5, 8, 128), F32)]
        + fields
        + [
            pltpu.VMEM((128, 128), F32),
            pltpu.VMEM((25, 128), F32),
            pltpu.VMEM((1024, 128), F32),
        ]
    )


def forward(kernel, name, flags, operands, fields):
    return pl.pallas_call(
        kernel,
        grid=(STEPS,),
        in_specs=[scalars() for _ in flags] + [whole(value.shape) for value in operands],
        out_specs=forward_specs(),
        out_shape=FORWARD_OUT,
        scratch_shapes=forward_scratch(fields),
        compiler_params=params(),
        name=name,
    )(*flags, *operands)


def reduced(port, axis):
    count = lax.axis_size(axis)
    lines = 512 // count
    received = lax.all_to_all(
        port.reshape(count, lines, 128), axis, split_axis=0, concat_axis=0, tiled=True
    )
    ends = pl.pallas_call(
        functools.partial(reduced_kernel, count, lines),
        out_shape=jax.ShapeDtypeStruct((count, 16, 128), F32),
        in_specs=[pl.BlockSpec(memory_space=pltpu.VMEM)],
        out_specs=pl.BlockSpec(memory_space=pltpu.VMEM),
        scratch_shapes=[
            pltpu.VMEM((count, 128, 128), F32),
            pltpu.VMEM((count, 32, 128), F32),
        ],
        compiler_params=pltpu.CompilerParams(vmem_limit_bytes=VMEM_LIMIT),
        name="reduced_" + axis,
    )(received.reshape(512, 128))
    return lax.all_to_all(ends, axis, split_axis=0, concat_axis=0, tiled=True)


def backward(kernel, name, operands, extra):
    count = operands[2].shape[0]
    return pl.pallas_call(
        functools.partial(kernel, count, 512 // count),
        grid=(STEPS,),
        in_specs=[pl.BlockSpec((CHUNK, FACTORS, 8, 128), lambda i: (STEPS - 1 - i, 0, 0, 0))]
        + [whole(value.shape) for value in operands[1:]],
        out_specs=whole((5, 512, 128)),
        out_shape=jax.ShapeDtypeStruct((5, 512, 128), F32),
        scratch_shapes=[pltpu.VMEM((10, 8, 128), F32), pltpu.VMEM((10, 8, 128), F32)] + extra,
        compiler_params=params(),
        name=name,
    )(*operands)


def halos(axis, last, initial):
    devices = lax.axis_size(axis)
    up = [(i, (i + 1) % devices) for i in range(devices)]
    down = [(j, i) for i, j in up]
    return lax.ppermute(last, axis, up), lax.ppermute(initial, axis, down)


def body(flow_state, viscosity, metric_x, metric_y, jacobian_x, jacobian_y):
    spots = [lax.axis_index("row"), lax.axis_index("col")]
    sizes = [lax.axis_size("row"), lax.axis_size("col")]
    first = jnp.stack([(spot == 0).astype(jnp.int32) for spot in spots])
    last = jnp.stack([(spot == n - 1).astype(jnp.int32) for spot, n in zip(spots, sizes)])
    jacx = jacobian_x.reshape(25, 128)
    jacy = jacobian_y.reshape(25, 128)

    south, north = halos(
        "col",
        flow_state[:, :, :, 127].reshape(20, 128),
        flow_state[:, :, :, 0].reshape(20, 128),
    )
    q = flow_state.reshape(5, 512, 128)
    visc = viscosity.reshape(512, 128)
    plane = [pltpu.VMEM(PLANE, F32), pltpu.VMEM(PLANE, F32)]
    field = pltpu.VMEM((5, 512, 128), F32)
    fac, port, mid, *tables = forward(
        forward_x_kernel, "forward_x", (first, last),
        (q, visc, metric_x, metric_y, jacx, jacy, south, north), plane,
    )
    ends = reduced(port, "row")
    partial_value = backward(
        backward_x_kernel, "backward_x", (fac, mid, ends, *tables, q), []
    )
    fac, port, mid, *tables = forward(
        forward_y_kernel, "forward_y", (first,), (partial_value, visc, metric_y, jacy), [field]
    )
    ends = reduced(port, "col")
    result = backward(
        backward_y_kernel, "backward_y", (fac, mid, ends, *tables), [field]
    )
    return result.reshape(5, 4, 128, 128)


def solution(mesh):
    return jax.shard_map(
        body,
        mesh=mesh,
        in_specs=(
            P(None, None, "row", "col"),
            P(None, "row", "col"),
            P("row", "col"),
            P("row", "col"),
            P(None, None, "row"),
            P(None, None, "col"),
        ),
        out_specs=P(None, None, "row", "col"),
        check_vma=False,
    )
```

```python
import functools

import jax
import jax.numpy as jnp
from jax import lax
from jax.experimental import pallas as pl
from jax.experimental.pallas import tpu as pltpu
from jax.sharding import PartitionSpec as P

F32 = jnp.float32
N = 128
HALF = 64
KEPT = HALF // 2
CHUNK = 8
STEPS = KEPT // CHUNK
VMEM_LIMIT = 48 * 1024 * 1024


def zeros():
    return jnp.zeros((8, 128), F32)


def ones():
    return jnp.ones((8, 128), F32)


def lane(value, index):
    return jnp.broadcast_to(value[:, index : index + 1], (8, 128))


def mat_cols(matrix, columns):
    result = []
    for column in columns:
        out = []
        for i in range(5):
            total = matrix[i][0] * column[0]
            for k in range(1, 5):
                total = total + matrix[i][k] * column[k]
            out.append(total)
        result.append(out)
    return result


def inverse(matrix):
    m = [list(row) for row in matrix]
    for p in range(5):
        inv = 1.0 / m[p][p]
        for j in range(5):
            m[p][j] = inv if j == p else m[p][j] * inv
        for i in range(5):
            if i != p:
                weight = m[i][p]
                for j in range(5):
                    m[i][j] = -weight * inv if j == p else m[i][j] - weight * m[p][j]
    return m


def apply(matrix, vector):
    return mat_cols(matrix, [vector])[0]


def product(left, right):
    return rows_of(mat_cols(left, columns_of(right)))


def entrywise(function, *matrices):
    return [[function(*(m[i][j] for m in matrices)) for j in range(5)] for i in range(5)]


def add(left, right):
    return entrywise(lambda a, b: a + b, left, right)


def subtract(left, right):
    return entrywise(lambda a, b: a - b, left, right)


def unit_matrix():
    return [[ones() if i == j else zeros() for j in range(5)] for i in range(5)]


def zero_matrix():
    return [[zeros() for _ in range(5)] for _ in range(5)]


def columns_of(matrix):
    return [[matrix[i][j] for i in range(5)] for j in range(5)]


def rows_of(columns):
    return [[columns[j][i] for j in range(5)] for i in range(5)]


def load_vec(ref, base, *at):
    return [ref[(*at, base + i)] for i in range(5)]


def load_mat(ref, base, *at):
    return [load_vec(ref, base + 5 * i, *at) for i in range(5)]


def store_vec(ref, base, vector, *at):
    for i in range(5):
        ref[(*at, base + i)] = vector[i]


def store_mat(ref, base, matrix, *at):
    for i in range(5):
        store_vec(ref, base + 5 * i, matrix[i], *at)


def cell_rows(k):
    return pl.ds(k, 8, stride=HALF)


def even_rows():
    return lax.broadcasted_iota(jnp.int32, (8, 128), 0) % 2 == 0


def from_second(value):
    return pltpu.roll(value, 7, 0)


def table_mat(table, base):
    return [[lane(table, base + 5 * i + j) for j in range(5)] for i in range(5)]


R_AT, X_AT, Q_AT, XQ_AT, STATE = 0, 25, 50, 75, 100
LOWER_AT, PIVOT_AT, FIRST_AT, SWEEP = 0, 25, 50, 75


def kept_matrices(m, tables, last):
    tab, eps, dlt = tables
    k = 2 * m + 1
    here, back = cell_rows(k), cell_rows(k - 1)
    table = tab[here, :]
    e0, d0 = eps[here, :], dlt[here, :]
    em, dm = eps[back, :], dlt[back, :]
    cm = 1.0 / (2.0 + dm)
    a = table_mat(table, 0)
    a1, a2 = cm * e0, cm * em
    a3 = a1 * em
    am, aam = table_mat(tab[back, :], 0), table_mat(table, 35)
    lower = entrywise(lambda x, y, z: (a1 * x + a2 * y) + a3 * z, a, am, aam)
    low = cm * dm
    if last:
        shift, tilt = d0 + low, e0 * low
        upper = entrywise(lambda x: -(e0 * x), a)
    else:
        ahead = cell_rows(k + 1)
        ep, dp = eps[ahead, :], dlt[ahead, :]
        cp = 1.0 / (2.0 + dp)
        b1, b2 = cp * e0, cp * ep
        b3 = b1 * ep
        ap, aap = table_mat(tab[ahead, :], 0), table_mat(table, 60)
        upper = entrywise(lambda x, y, z: b3 * z - (b1 * x + b2 * y), a, ap, aap)
        high = cp * dp
        shift, tilt = d0 + (low + high), e0 * (low - high)
    excess = entrywise(lambda x: tilt * x, a)
    for i in range(5):
        excess[i][i] = excess[i][i] + shift
        lower[i][i] = lower[i][i] + cm
        upper[i][i] = upper[i][i] + (1.0 if last else cp)
    return lower, excess, upper


def kept_source(m, tables, fm, f0, fp):
    tab, eps, dlt = tables
    k = 2 * m + 1
    here = cell_rows(k)
    low = 1.0 / (2.0 + dlt[cell_rows(k - 1), :])
    first = [low * value for value in fm]
    second = first
    if fp is not None:
        high = 1.0 / (2.0 + dlt[cell_rows(k + 1), :])
        later = [high * value for value in fp]
        second = [first[i] - later[i] for i in range(5)]
        first = [first[i] + later[i] for i in range(5)]
    e0 = eps[here, :]
    moved = apply(table_mat(tab[here, :], 0), [e0 * value for value in second])
    return [(f0[i] + first[i]) + moved[i] for i in range(5)]


def left_part(lower, excess, r, x):
    cols = mat_cols(lower, columns_of(r) + columns_of(x))
    return add(rows_of(cols[:5]), excess), add(rows_of(cols[5:]), excess)


def accumulate(state, r, x):
    q = load_mat(state, Q_AT)
    moved = mat_cols(q, columns_of(r) + columns_of(x))
    q_new = subtract(q, rows_of(moved[:5]))
    xq_new = subtract(load_mat(state, XQ_AT), rows_of(moved[5:]))
    store_mat(state, Q_AT, q_new)
    store_mat(state, XQ_AT, xq_new)
    return q_new, xq_new


def matrix_step(m, state, sweep_ref, back_ref, slot, tables):
    @pl.when(m == 1)
    def _():
        store_mat(state, Q_AT, unit_matrix())
        store_mat(state, XQ_AT, zero_matrix())

    r = load_mat(state, R_AT)
    x = load_mat(state, X_AT)
    lower, excess, upper = kept_matrices(m, tables, False)
    s, xn = left_part(lower, excess, r, x)
    pivot = inverse(add(s, upper))
    solved = mat_cols(pivot, columns_of(s) + columns_of(xn))
    r_new, x_new = rows_of(solved[:5]), rows_of(solved[5:])
    q, _ = accumulate(state, r, x)
    store_mat(state, R_AT, r_new)
    store_mat(state, X_AT, x_new)
    store_mat(sweep_ref, LOWER_AT, lower, slot)
    store_mat(sweep_ref, PIVOT_AT, pivot, slot)
    store_mat(sweep_ref, FIRST_AT, q, slot)
    store_mat(back_ref, 0, r_new, slot)
    store_mat(back_ref, 25, x_new, slot)


def first_edge_scale(tables):
    tab, eps, dlt = tables
    rows = cell_rows(0)
    e0, d0 = eps[rows, :], dlt[rows, :]
    c0 = 1.0 / (2.0 + d0)
    return entrywise(lambda x: e0 * x, table_mat(tab[rows, :], 0)), c0, d0


def finish_matrices(first, state, sweep_ref, join_ref, mid_ref, port, port_ref, tables):
    r = load_mat(state, R_AT)
    x = load_mat(state, X_AT)
    q, xq = accumulate(state, r, x)
    speed, c0, d0 = first_edge_scale(tables)
    cols = mat_cols(speed, columns_of(q) + columns_of(xq))
    q = entrywise(lambda a, b: c0 * (a - b), q, rows_of(cols[:5]))
    xq = entrywise(lambda a, b: c0 * (a - b), xq, rows_of(cols[5:]))
    for i in range(5):
        xq[i][i] = xq[i][i] - c0 * d0
    lower, excess, ahead = kept_matrices(KEPT - 1, tables, True)
    s, xn = left_part(lower, excess, r, x)
    pivot = inverse(ahead)
    store_mat(sweep_ref, LOWER_AT, lower, CHUNK - 1)
    store_mat(sweep_ref, PIVOT_AT, pivot, CHUNK - 1)
    store_mat(sweep_ref, FIRST_AT, zero_matrix(), CHUNK - 1)
    s, xn = product(pivot, s), product(pivot, xn)
    q1 = entrywise(from_second, q)
    xq1 = entrywise(from_second, xq)
    coupling = inverse(add(s, subtract(q1, xq1)))
    mc = product(coupling, q1)
    mx = product(coupling, subtract(xq1, xn))
    store_mat(mid_ref, 0, mc)
    store_mat(mid_ref, 25, mx)
    s1 = entrywise(from_second, s)
    xn1 = entrywise(from_second, xn)
    n1 = subtract(xn1, s1)
    store_mat(join_ref, 0, coupling)
    store_mat(join_ref, 25, q)
    store_mat(join_ref, 50, n1)
    start = jnp.broadcast_to(first, (8, 128)) > 0
    ports = (
        add(s1, product(n1, mc)),
        add(xn1, product(n1, mx)),
        entrywise(lambda a, b: jnp.where(start, b, a), product(q, mc), unit_matrix()),
        entrywise(lambda a: jnp.where(start, 0.0, a), add(xq, product(q, mx))),
    )
    for at, matrix in enumerate(ports):
        for i in range(5):
            for j in range(5):
                port[pl.ds(8 * (25 * at + 5 * i + j), 8), :] = matrix[i][j]
    port_ref[...] = port[pl.ds(0, 400, stride=2), :]


def start_tables(jac_ref, tin, turned):
    tin[...] = jnp.zeros((128, 128), F32)
    jac = jac_ref[...]
    tin[pl.ds(0, 25), :] = jac
    for base, shift in ((35, 1), (60, 127)):
        turned[...] = pltpu.roll(jac, shift, 1)
        for i in range(5):
            for j in range(5):
                total = jac_ref[pl.ds(5 * i, 1), :] * turned[pl.ds(j, 1), :]
                for k in range(1, 5):
                    total = total + jac_ref[pl.ds(5 * i + k, 1), :] * turned[pl.ds(5 * k + j, 1), :]
                tin[pl.ds(base + 5 * i + j, 1), :] = total


def matrix_kernel(
    turn, first_ref, visc_ref, metric_ref, jac_ref,
    sweep_ref, back_ref, join_ref, mid_ref, port_ref, tab, eps, dlt,
    state, tin, turned, port,
):
    step = pl.program_id(0)

    @pl.when(step == 0)
    def _():
        store_mat(state, R_AT, unit_matrix())
        store_mat(state, X_AT, zero_matrix())
        store_mat(state, Q_AT, unit_matrix())
        store_mat(state, XQ_AT, zero_matrix())
        metric = metric_ref[...].T if turn else metric_ref[...]
        start_tables(jac_ref, tin, turned)
        table = tin[...].T
        for z in range(4):
            rows = pl.ds(128 * z, 128)
            visc = visc_ref[rows, :].T if turn else visc_ref[rows, :]
            e = 1.0 / (visc * metric)
            eps[rows, :] = e
            dlt[rows, :] = e * e * visc
            tab[rows, :] = table

    tables = (tab, eps, dlt)
    count = jnp.where(step == STEPS - 1, CHUNK - 1, CHUNK)

    def one(slot, carry):
        matrix_step(step * CHUNK + slot, state, sweep_ref, back_ref, slot, tables)
        return carry

    lax.fori_loop(0, count, one, 0)

    @pl.when(step == 0)
    def _():
        store_mat(sweep_ref, FIRST_AT, unit_matrix(), 0)

    @pl.when(step == STEPS - 1)
    def _():
        store_mat(back_ref, 0, zero_matrix(), CHUNK - 1)
        store_mat(back_ref, 25, zero_matrix(), CHUNK - 1)
        finish_matrices(
            first_ref[0], state, sweep_ref, join_ref, mid_ref, port, port_ref, tables
        )


def source_sweep(first, sweep_ref, join_ref, vec_ref, mid_ref, port_ref, state, port, raw, tables):
    step = pl.program_id(0)

    @pl.when(step == 0)
    def _():
        start = raw(0)
        for i in range(5):
            state[i] = zeros()
            state[5 + i] = zeros()
            state[10 + i] = start[i]
            mid_ref[5 + i] = start[i]

    count = jnp.where(step == STEPS - 1, CHUNK - 1, CHUNK)

    def one(slot, carry):
        w, y, fm = carry[:5], carry[5:10], carry[10:]
        m = step * CHUNK + slot
        fp = raw(2 * m + 2)
        right = kept_source(m, tables, fm, raw(2 * m + 1), fp)
        moved = apply(load_mat(sweep_ref, LOWER_AT, slot), w)
        w = apply(load_mat(sweep_ref, PIVOT_AT, slot), [moved[i] - right[i] for i in range(5)])
        moved = apply(load_mat(sweep_ref, FIRST_AT, slot), w)
        y = [y[i] - moved[i] for i in range(5)]
        store_vec(vec_ref, 0, w, slot)
        store_vec(vec_ref, 5, fp, slot)
        return tuple(w) + tuple(y) + tuple(fp)

    final = lax.fori_loop(0, count, one, tuple(state[i] for i in range(15)))
    for i in range(15):
        state[i] = final[i]

    @pl.when(step == STEPS - 1)
    def _():
        w, y, fm = load_vec(state, 0), load_vec(state, 5), load_vec(state, 10)
        for i in range(10):
            vec_ref[CHUNK - 1, i] = zeros()
        speed, c0, _ = first_edge_scale(tables)
        moved = apply(speed, y)
        y = [c0 * ((y[i] - moved[i]) + mid_ref[5 + i]) for i in range(5)]
        right = kept_source(KEPT - 1, tables, fm, raw(HALF - 1), None)
        moved = apply(load_mat(sweep_ref, LOWER_AT, CHUNK - 1), w)
        g = apply(
            load_mat(sweep_ref, PIVOT_AT, CHUNK - 1), [right[i] - moved[i] for i in range(5)]
        )
        y1, g1 = [from_second(e) for e in y], [from_second(e) for e in g]
        middle = apply(load_mat(join_ref, 0), [y1[i] + g[i] for i in range(5)])
        store_vec(mid_ref, 0, middle)
        ahead = apply(load_mat(join_ref, 25), middle)
        moved = apply(load_mat(join_ref, 50), middle)
        start = jnp.broadcast_to(first, (8, 128)) > 0
        for i in range(5):
            port[pl.ds(8 * i, 8), :] = g1[i] - moved[i]
            port[pl.ds(8 * (5 + i), 8), :] = jnp.where(start, 0.0, y[i] + ahead[i])
        port_ref[...] = port[pl.ds(0, 40, stride=2), :]


def source_x_kernel(
    first_ref, last_ref, sweep_ref, join_ref, tab, eps, dlt,
    q_ref, visc_ref, my_ref, jacy_ref, south_ref, north_ref,
    vec_ref, mid_ref, port_ref,
    state, port, g1, g2, beside, tin,
):
    lanes = lax.broadcasted_iota(jnp.int32, (8, 128), 1)

    def raw(k):
        rows = cell_rows(k)
        table = beside[rows, :]
        d, a, b = dlt[rows, :], g1[rows, :], g2[rows, :]
        diff_y, base = [], []
        for c in range(5):
            here = q_ref[c, rows, :]
            south = jnp.where(lanes == 0, lane(table, c), pltpu.roll(here, 1, 1))
            north = jnp.where(lanes == 127, lane(table, 5 + c), pltpu.roll(here, 127, 1))
            diff_y.append(north - south)
            base.append(d * here + a * ((north - 2.0 * here) + south))
        right = []
        for i in range(5):
            total = jacy_ref[pl.ds(5 * i, 1), :] * diff_y[0]
            for j in range(1, 5):
                total = total + jacy_ref[pl.ds(5 * i + j, 1), :] * diff_y[j]
            right.append(base[i] - b * total)
        return right

    @pl.when(pl.program_id(0) == 0)
    def _():
        my = my_ref[...]
        not_first = jnp.where(first_ref[1] > 0, 0.0, 1.0)
        not_last = jnp.where(last_ref[1] > 0, 0.0, 1.0)
        tin[...] = jnp.zeros((128, 128), F32)
        for z in range(4):
            rows = pl.ds(128 * z, 128)
            scaled = dlt[rows, :] * my
            g2[rows, :] = scaled
            g1[rows, :] = scaled * (my * visc_ref[rows, :])
            for c in range(5):
                tin[pl.ds(c, 1), :] = south_ref[pl.ds(4 * c + z, 1), :] * not_first
                tin[pl.ds(5 + c, 1), :] = north_ref[pl.ds(4 * c + z, 1), :] * not_last
            beside[rows, :] = tin[...].T

    source_sweep(
        first_ref[0], sweep_ref, join_ref, vec_ref, mid_ref, port_ref, state, port, raw,
        (tab, eps, dlt),
    )


def source_y_kernel(
    first_ref, sweep_ref, join_ref, tab, eps, dlt, p_ref,
    vec_ref, mid_ref, port_ref,
    state, port, field,
):
    def raw(k):
        rows = cell_rows(k)
        d = dlt[rows, :]
        return [d * field[c, rows, :] for c in range(5)]

    @pl.when(pl.program_id(0) == 0)
    def _():
        for z in range(4):
            rows = pl.ds(128 * z, 128)
            for c in range(5):
                field[c, rows, :] = p_ref[c, rows, :].T

    source_sweep(
        first_ref[1], sweep_ref, join_ref, vec_ref, mid_ref, port_ref, state, port, raw,
        (tab, eps, dlt),
    )


def line_vec(ref, piece, base):
    return [ref[piece, pl.ds(4 * (base + i), 4), :] for i in range(5)]


def line_mat(ref, piece, base):
    return [line_vec(ref, piece, base + 5 * i) for i in range(5)]


def put_line_mat(ref, piece, base, matrix):
    for i in range(5):
        for j in range(5):
            ref[piece, pl.ds(4 * (base + 5 * i + j), 4), :] = matrix[i][j]


def reduced_kernel(count, in_ref, out_ref):
    def eliminate(piece, following, s):
        reduced = subtract(s, line_mat(in_ref, following, 75))
        pivot = inverse(add(reduced, line_mat(in_ref, following, 50)))
        h = product(pivot, reduced)
        put_line_mat(out_ref, piece, 0, pivot)
        put_line_mat(out_ref, piece, 25, h)
        return h

    def forward(piece, flat):
        h = [list(flat[5 * i : 5 * i + 5]) for i in range(5)]
        s, xn = line_mat(in_ref, piece, 0), line_mat(in_ref, piece, 25)
        gain = [[(1.0 if i == j else 0.0) - h[i][j] for j in range(5)] for i in range(5)]
        put_line_mat(out_ref, piece, 50, subtract(s, xn))
        s_all = add(product(s, h), product(xn, gain))
        h = eliminate(piece, lax.rem(piece + 1, count), s_all)
        return tuple(value for row in h for value in row)

    h = eliminate(0, 1, line_mat(in_ref, 0, 0))
    for e in range(25):
        out_ref[0, pl.ds(4 * (50 + e), 4), :] = jnp.zeros((4, 128), F32)
    lax.fori_loop(1, count, forward, tuple(value for row in h for value in row))


def substitute(count, spots_ref, axis, red_ref, sources, gathered, values):
    inner = sources[0].shape[0]
    me = spots_ref[axis]
    outer_at, inner_at = me // inner, lax.rem(me, inner)
    for far, source in enumerate(sources):
        for near in range(inner):
            place = lax.rem(outer_at + far, 4) * inner + lax.rem(inner_at + near, inner)
            gathered[place] = source[near]
    zero = tuple(jnp.zeros((4, 128), F32) for _ in range(5))

    def forward(piece, v):
        moved = apply(line_mat(red_ref, piece, 50), list(v))
        g = line_vec(gathered, piece, 0)
        yy = line_vec(gathered, lax.rem(piece + 1, count), 5)
        v = apply(line_mat(red_ref, piece, 0), [(g[i] + moved[i]) + yy[i] for i in range(5)])
        for i in range(5):
            values[piece + 1, i] = v[i]
        return tuple(v)

    lax.fori_loop(0, count, forward, zero)

    def backward(at, p):
        piece = count - 1 - at
        moved = apply(line_mat(red_ref, piece, 25), list(p))
        p = tuple((p[i] - moved[i]) + values[piece + 1, i] for i in range(5))
        for i in range(5):
            values[piece + 1, i] = p[i]
        return p

    lax.fori_loop(0, count, backward, zero)
    for i in range(5):
        values[0, i] = zero[0]
    return [values[me, i] for i in range(5)], [values[me + 1, i] for i in range(5)]


def between(k, left, right, tables, source):
    tab, eps, dlt = tables
    rows = cell_rows(k)
    e, d = eps[rows, :], dlt[rows, :]
    c = 1.0 / (2.0 + d)
    gap = [right[i] - left[i] for i in range(5)]
    moved = apply(table_mat(tab[rows, :], 0), [e * value for value in gap])
    return [
        right[i] - c * ((gap[i] + moved[i]) + (d * right[i] - source[i])) for i in range(5)
    ]


def backward_sweep(
    count, axis, spots_ref, back_ref, vec_ref, join_ref, mid_ref, red_ref, sources, tables,
    edge, ends8, gathered, values, write,
):
    step = pl.program_id(0)

    @pl.when(step == 0)
    def _():
        left, right = substitute(count, spots_ref, axis, red_ref, sources, gathered, values)
        for i in range(5):
            for z in range(4):
                ends8[i, pl.ds(2 * z, 1), :] = left[i][z : z + 1]
                ends8[i, pl.ds(2 * z + 1, 1), :] = left[i][z : z + 1]
                ends8[5 + i, pl.ds(2 * z, 1), :] = right[i][z : z + 1]
                ends8[5 + i, pl.ds(2 * z + 1, 1), :] = right[i][z : z + 1]
        a, c = load_vec(ends8, 0), load_vec(ends8, 5)
        part = apply(load_mat(join_ref, 0), [c[i] - a[i] for i in range(5)])
        rest = apply(load_mat(join_ref, 25), a)
        even = even_rows()
        for i in range(5):
            middle = a[i] + ((part[i] + rest[i]) + mid_ref[i])
            edge[i] = jnp.where(even, a[i], pltpu.roll(middle, 1, 0))
            edge[5 + i] = jnp.where(even, middle, c[i])
        write(HALF - 1, load_vec(edge, 5))

    a = load_vec(edge, 0)
    begin = jnp.where(step == 0, 1, 0)

    def one(at, following):
        slot = CHUNK - 1 - at
        m = (STEPS - 1 - step) * CHUNK + slot
        part = apply(load_mat(back_ref, 0, slot), [following[i] - a[i] for i in range(5)])
        rest = apply(load_mat(back_ref, 25, slot), a)
        w, source = load_vec(vec_ref, 0, slot), load_vec(vec_ref, 5, slot)
        here = tuple(following[i] - ((part[i] + rest[i]) + w[i]) for i in range(5))
        write(2 * m + 2, between(2 * m + 2, here, following, tables, source))
        write(2 * m + 1, here)
        return here

    final = lax.fori_loop(begin, CHUNK, one, tuple(edge[5 + i] for i in range(5)))
    store_vec(edge, 5, final)

    @pl.when(step == STEPS - 1)
    def _():
        write(0, between(0, a, final, tables, load_vec(mid_ref, 5)))


def backward_x_kernel(
    count, spots_ref, back_ref, vec_ref, join_ref, mid_ref, red_ref, s0, s1, s2, s3,
    tab, eps, dlt, q_ref, out_ref, edge, ends8, gathered, values,
):
    def write(k, value):
        rows = cell_rows(k)
        for i in range(5):
            out_ref[i, rows, :] = value[i] - q_ref[i, rows, :]

    backward_sweep(
        count, 0, spots_ref, back_ref, vec_ref, join_ref, mid_ref, red_ref, (s0, s1, s2, s3),
        (tab, eps, dlt), edge, ends8, gathered, values, write,
    )


def backward_y_kernel(
    count, spots_ref, back_ref, vec_ref, join_ref, mid_ref, red_ref, s0, s1, s2, s3,
    tab, eps, dlt, out_ref, edge, ends8, gathered, values, field,
):
    def write(k, value):
        for i in range(5):
            field[i, cell_rows(k), :] = value[i]

    backward_sweep(
        count, 1, spots_ref, back_ref, vec_ref, join_ref, mid_ref, red_ref, (s0, s1, s2, s3),
        (tab, eps, dlt), edge, ends8, gathered, values, write,
    )

    @pl.when(pl.program_id(0) == STEPS - 1)
    def _():
        for c in range(5):
            for z in range(4):
                rows = pl.ds(128 * z, 128)
                out_ref[c, rows, :] = field[c, rows, :].T


def whole(shape):
    return pl.BlockSpec(shape, lambda i: (0,) * len(shape))


def rising(entries):
    return pl.BlockSpec((CHUNK, entries, 8, 128), lambda i: (i, 0, 0, 0))


def falling(entries):
    return pl.BlockSpec((CHUNK, entries, 8, 128), lambda i: (STEPS - 1 - i, 0, 0, 0))


def scalars():
    return pl.BlockSpec(memory_space=pltpu.SMEM)


def call(kernel, name, flags, operands, outputs, scratch, gflops):
    shapes = tuple(jax.ShapeDtypeStruct(shape, F32) for _, shape in outputs)
    moved = 4 * sum(value.size for _, value in operands)
    return pl.pallas_call(
        kernel,
        grid=(STEPS,),
        in_specs=[scalars() for _ in flags]
        + [whole(value.shape) if spec is None else spec for spec, value in operands],
        out_specs=tuple(whole(shape) if spec is None else spec for spec, shape in outputs),
        out_shape=shapes,
        scratch_shapes=[pltpu.VMEM(shape, F32) for shape in scratch],
        compiler_params=pltpu.CompilerParams(
            dimension_semantics=("arbitrary",), vmem_limit_bytes=VMEM_LIMIT
        ),
        cost_estimate=pl.CostEstimate(
            flops=int(gflops * 1e9), bytes_accessed=moved, transcendentals=0
        ),
        name=name,
    )(*flags, *(value for _, value in operands))


PLANE = (512, 128)
FIELD = (5, 512, 128)


def matrices(name, turn, first, visc, metric, jac):
    return call(
        functools.partial(matrix_kernel, turn),
        name,
        (first,),
        [(None, visc), (None, metric), (None, jac)],
        [
            (rising(SWEEP), (KEPT, SWEEP, 8, 128)),
            (rising(50), (KEPT, 50, 8, 128)),
            (None, (75, 8, 128)),
            (None, (50, 8, 128)),
            (None, (400, 128)),
            (None, PLANE),
            (None, PLANE),
            (None, PLANE),
        ],
        [(STATE, 8, 128), (128, 128), (25, 128), (800, 128)],
        0.12,
    )


SOURCE_OUT = [
    (rising(10), (KEPT, 10, 8, 128)),
    (None, (10, 8, 128)),
    (None, (40, 128)),
]


def reduced(name, ports):
    count = ports.shape[0]
    return pl.pallas_call(
        functools.partial(reduced_kernel, count),
        out_shape=jax.ShapeDtypeStruct((count, 300, 128), F32),
        in_specs=[pl.BlockSpec(memory_space=pltpu.VMEM)],
        out_specs=pl.BlockSpec(memory_space=pltpu.VMEM),
        compiler_params=pltpu.CompilerParams(vmem_limit_bytes=VMEM_LIMIT),
        name=name,
    )(ports)


def permute(value, axis, moves):
    return lax.ppermute(value, axis, moves)


def gather_sources(port, axis):
    count = lax.axis_size(axis)
    inner = count // 4
    groups = [port]
    for near in range(1, inner):
        moves = [((i // inner) * inner + (i + near) % inner, i) for i in range(count)]
        groups.append(permute(port, axis, moves))
    block = jnp.stack(groups)
    blocks = [block]
    for far in range(1, 4):
        moves = [((i + far * inner) % count, i) for i in range(count)]
        blocks.append(permute(block, axis, moves))
    return blocks


def after(value, other):
    return lax.optimization_barrier((value, other))[0]


def halos(axis, last, initial):
    devices = lax.axis_size(axis)
    up = [(i, (i + 1) % devices) for i in range(devices)]
    down = [(j, i) for i, j in up]
    return lax.ppermute(last, axis, up), lax.ppermute(initial, axis, down)


def body(flow_state, viscosity, metric_x, metric_y, jacobian_x, jacobian_y):
    spots = jnp.stack([lax.axis_index("row"), lax.axis_index("col")]).astype(jnp.int32)
    sizes = jnp.array([lax.axis_size("row"), lax.axis_size("col")], jnp.int32)
    first = (spots == 0).astype(jnp.int32)
    last = (spots == sizes - 1).astype(jnp.int32)
    jacx = jacobian_x.reshape(25, 128)
    jacy = jacobian_y.reshape(25, 128)
    south, north = halos(
        "col",
        flow_state[:, :, :, 127].reshape(20, 128),
        flow_state[:, :, :, 0].reshape(20, 128),
    )
    q = flow_state.reshape(5, 512, 128)
    visc = viscosity.reshape(512, 128)
    sweep_x, back_x, join_x, mid_x, port_x, *tables_x = matrices(
        "matrices_x", False, first, visc, metric_x, jacx
    )
    ports_x = lax.all_gather(port_x, "row")
    sweep_y, back_y, join_y, mid_y, port_y, *tables_y = matrices(
        "matrices_y", True, after(first[1:], port_x), visc, metric_y, jacy
    )
    ports_y = lax.all_gather(port_y, "col")
    vec, mid, port = call(
        source_x_kernel,
        "source_x",
        (after(first, port_y), last),
        [(rising(SWEEP), sweep_x), (None, join_x)]
        + [(None, value) for value in (*tables_x, q, visc, metric_y, jacy, south, north)],
        SOURCE_OUT,
        [(15, 8, 128), (80, 128), PLANE, PLANE, PLANE, (128, 128)],
        0.03,
    )
    sources = gather_sources(port, "row")
    red = reduced("reduced_x", after(ports_x, port))
    (partial_value,) = call(
        functools.partial(backward_x_kernel, 8),
        "backward_x",
        (spots,),
        [(falling(50), back_x), (falling(10), vec)]
        + [(None, value) for value in (mid_x, mid, red, *sources, *tables_x, q)],
        [(None, FIELD)],
        [(10, 8, 128), (10, 8, 128), (8, 40, 128), (9, 5, 4, 128)],
        0.03,
    )
    vec, mid, port = call(
        source_y_kernel,
        "source_y",
        (first,),
        [(rising(SWEEP), sweep_y), (None, join_y)]
        + [(None, value) for value in (*tables_y, partial_value)],
        SOURCE_OUT,
        [(15, 8, 128), (80, 128), FIELD],
        0.03,
    )
    sources = gather_sources(port, "col")
    red = reduced("reduced_y", after(ports_y, port))
    (result,) = call(
        functools.partial(backward_y_kernel, 16),
        "backward_y",
        (spots,),
        [(falling(50), back_y), (falling(10), vec)]
        + [(None, value) for value in (mid_y, mid, red, *sources, *tables_y)],
        [(None, FIELD)],
        [(10, 8, 128), (10, 8, 128), (16, 40, 128), (17, 5, 4, 128), FIELD],
        0.03,
    )
    return result.reshape(5, 4, 128, 128)


def solution(mesh):
    return jax.shard_map(
        body,
        mesh=mesh,
        in_specs=(
            P(None, None, "row", "col"),
            P(None, "row", "col"),
            P("row", "col"),
            P("row", "col"),
            P(None, None, "row"),
            P(None, None, "col"),
        ),
        out_specs=P(None, None, "row", "col"),
        check_vma=False,
    )
```

```python
import functools

import jax
import jax.numpy as jnp
from jax import lax
from jax.experimental import pallas as pl
from jax.experimental.pallas import tpu as pltpu
from jax.sharding import PartitionSpec as P

F32 = jnp.float32
N = 128
HALF = 64
ENTRIES = 112
KEPT = HALF // 2
CHUNK = 8
STEPS = KEPT // CHUNK
FACTORS = 60
VMEM_LIMIT = 48 * 1024 * 1024


def zeros():
    return jnp.zeros((8, 128), F32)


def ones():
    return jnp.ones((8, 128), F32)


def lane(value, index):
    return jnp.broadcast_to(value[:, index : index + 1], (8, 128))


def mat_cols(matrix, columns):
    result = []
    for column in columns:
        out = []
        for i in range(5):
            total = matrix[i][0] * column[0]
            for k in range(1, 5):
                total = total + matrix[i][k] * column[k]
            out.append(total)
        result.append(out)
    return result


def reciprocal(value):
    guess = pl.reciprocal(value, approx=True)
    return guess * (2.0 - value * guess)


def factor(matrix):
    m = [list(row) for row in matrix]
    inverse = []
    for p in range(5):
        inv = reciprocal(m[p][p])
        inverse.append(inv)
        for i in range(p + 1, 5):
            m[i][p] = m[i][p] * inv
            for j in range(p + 1, 5):
                m[i][j] = m[i][j] - m[i][p] * m[p][j]
    for i in range(5):
        for j in range(i + 1, 5):
            m[i][j] = m[i][j] * inverse[i]
    return m, inverse


def triangular(factored, column):
    m, inverse = factored
    x = list(column)
    for i in range(1, 5):
        for p in range(i):
            x[i] = x[i] - m[i][p] * x[p]
    x = [x[i] * inverse[i] for i in range(5)]
    for i in range(3, -1, -1):
        for j in range(i + 1, 5):
            x[i] = x[i] - m[i][j] * x[j]
    return x


def solve(matrix, columns):
    factored = factor(matrix)
    return [triangular(factored, column) for column in columns]


def columns_of(matrix):
    return [[matrix[i][j] for i in range(5)] for j in range(5)]


def rows_of(columns):
    return [[columns[j][i] for j in range(5)] for i in range(5)]


def load_mat(ref, base):
    return [[ref[base + 5 * i + j] for j in range(5)] for i in range(5)]


def load_vec(ref, base):
    return [ref[base + i] for i in range(5)]


def store_mat(ref, base, matrix):
    for i in range(5):
        for j in range(5):
            ref[base + 5 * i + j] = matrix[i][j]


def store_vec(ref, base, vector):
    for i in range(5):
        ref[base + i] = vector[i]


R_AT, X_AT, W_AT, Q_AT, XQ_AT, Y_AT, STATE = 0, 25, 50, 55, 80, 105, 110


def init_state(state):
    for i in range(5):
        for j in range(5):
            state[R_AT + 5 * i + j] = ones() if i == j else zeros()
            state[X_AT + 5 * i + j] = zeros()
        state[W_AT + i] = zeros()


def init_first_edge(state):
    for i in range(5):
        for j in range(5):
            state[Q_AT + 5 * i + j] = ones() if i == j else zeros()
            state[XQ_AT + 5 * i + j] = zeros()
        state[Y_AT + i] = zeros()


def accumulate(state, r, x, w):
    q = load_mat(state, Q_AT)
    xq = load_mat(state, XQ_AT)
    y = load_vec(state, Y_AT)
    moved = mat_cols(q, columns_of(r) + columns_of(x) + [w])
    q_new = [[q[i][j] - moved[j][i] for j in range(5)] for i in range(5)]
    xq_new = [[xq[i][j] - moved[5 + j][i] for j in range(5)] for i in range(5)]
    y_new = [y[i] - moved[10][i] for i in range(5)]
    store_mat(state, Q_AT, q_new)
    store_mat(state, XQ_AT, xq_new)
    store_vec(state, Y_AT, y_new)
    return q_new, xq_new, y_new


def table_mat(table, base):
    return [[lane(table, base + 5 * i + j) for j in range(5)] for i in range(5)]


def kept_equation(m, source, tab, eps, dlt, last):
    k = 2 * m + 1
    here, back = cell_rows(k), cell_rows(k - 1)
    table = tab[here, :]
    e0, d0 = eps[here, :], dlt[here, :]
    em, dm = eps[back, :], dlt[back, :]
    cm = reciprocal(2.0 + dm)
    a = table_mat(table, 0)
    a1, a2 = cm * e0, cm * em
    a3 = a1 * em
    am, aam = table_mat(tab[back, :], 0), table_mat(table, 35)
    lower = [
        [(a1 * a[i][j] + a2 * am[i][j]) + a3 * aam[i][j] for j in range(5)] for i in range(5)
    ]
    fm, f0, fp = source
    low = cm * dm
    if last:
        shift, tilt = d0 + low, e0 * low
        first = [cm * fm[i] for i in range(5)]
        second = first
    else:
        ahead = cell_rows(k + 1)
        ep, dp = eps[ahead, :], dlt[ahead, :]
        cp = reciprocal(2.0 + dp)
        b1, b2 = cp * e0, cp * ep
        b3 = b1 * ep
        ap, aap = table_mat(tab[ahead, :], 0), table_mat(table, 60)
        upper = [
            [b3 * aap[i][j] - (b1 * a[i][j] + b2 * ap[i][j]) for j in range(5)] for i in range(5)
        ]
        high = cp * dp
        shift, tilt = d0 + (low + high), e0 * (low - high)
        first = [cm * fm[i] + cp * fp[i] for i in range(5)]
        second = [cm * fm[i] - cp * fp[i] for i in range(5)]
    excess = [[tilt * a[i][j] for j in range(5)] for i in range(5)]
    for i in range(5):
        excess[i][i] = excess[i][i] + shift
        lower[i][i] = lower[i][i] + cm
        if not last:
            upper[i][i] = upper[i][i] + cp
    moved = mat_cols(a, [[e0 * value for value in second]])[0]
    right = [(f0[i] + first[i]) + moved[i] for i in range(5)]
    if last:
        speed = [[e0 * a[i][j] for j in range(5)] for i in range(5)]
        return lower, excess, right, speed
    return lower, excess, right, upper


def local_relation(lower, excess, right, r, x, w):
    cols = mat_cols(lower, columns_of(r) + columns_of(x) + [w])
    s = [[cols[j][i] + excess[i][j] for j in range(5)] for i in range(5)]
    xn = [[cols[5 + j][i] + excess[i][j] for j in range(5)] for i in range(5)]
    g = [right[i] - cols[10][i] for i in range(5)]
    return s, xn, g


def sweep_step(m, state, fac_ref, slot, raw, keep, tables):
    r = load_mat(state, R_AT)
    x = load_mat(state, X_AT)
    w = load_vec(state, W_AT)
    fm = load_vec(keep, 0)
    f0, fp = raw(2 * m + 1), raw(2 * m + 2)
    lower, excess, right, upper = kept_equation(m, (fm, f0, fp), *tables, False)
    s, xn, g = local_relation(lower, excess, right, r, x, w)
    t = [[s[i][j] + upper[i][j] for j in range(5)] for i in range(5)]
    solved = solve(t, columns_of(s) + columns_of(xn) + [g])
    r_new = rows_of(solved[:5])
    x_new = rows_of(solved[5:10])
    w_new = [-value for value in solved[10]]
    live = jnp.where(m == 0, 0.0, 1.0)
    accumulate(
        state,
        [[live * e for e in row] for row in r],
        [[live * e for e in row] for row in x],
        [live * e for e in w],
    )
    store_mat(state, R_AT, r_new)
    store_mat(state, X_AT, x_new)
    store_vec(state, W_AT, w_new)
    store_vec(keep, 0, fp)
    for i in range(5):
        for j in range(5):
            fac_ref[slot, 5 * i + j] = r_new[i][j]
            fac_ref[slot, 25 + 5 * i + j] = x_new[i][j]
        fac_ref[slot, 50 + i] = w_new[i]
        fac_ref[slot, 55 + i] = fp[i]


def even_rows():
    return lax.broadcasted_iota(jnp.int32, (8, 128), 0) % 2 == 0


def finish_sweep(at, inner, state, port, port_refs, mid_ref, raw, keep, tables):
    tab, eps, dlt = tables
    r = load_mat(state, R_AT)
    x = load_mat(state, X_AT)
    w = load_vec(state, W_AT)
    q, xq, y = accumulate(state, r, x, w)
    rows = cell_rows(0)
    e0, d0 = eps[rows, :], dlt[rows, :]
    c0 = reciprocal(2.0 + d0)
    start_speed = [[e0 * value for value in row] for row in table_mat(tab[rows, :], 0)]
    cols = mat_cols(start_speed, columns_of(q) + columns_of(xq) + [y])
    q = [[c0 * (q[i][j] - cols[j][i]) for j in range(5)] for i in range(5)]
    xq = [[c0 * (xq[i][j] - cols[5 + j][i]) for j in range(5)] for i in range(5)]
    for i in range(5):
        xq[i][i] = xq[i][i] - c0 * d0
    y = [c0 * ((y[i] - cols[10][i]) + mid_ref[55 + i]) for i in range(5)]
    source = (load_vec(keep, 0), raw(HALF - 1), None)
    lower, excess, right, speed = kept_equation(KEPT - 1, source, tab, eps, dlt, True)
    s, xn, g = local_relation(lower, excess, right, r, x, w)
    ahead = [[(1.0 if i == j else 0.0) - speed[i][j] for j in range(5)] for i in range(5)]
    scaled = solve(ahead, columns_of(s) + columns_of(xn) + [g])
    s, xn, g = rows_of(scaled[:5]), rows_of(scaled[5:10]), scaled[10]

    def from_second(value):
        return pltpu.roll(value, 7, 0)

    q1 = [[from_second(e) for e in row] for row in q]
    xq1 = [[from_second(e) for e in row] for row in xq]
    y1 = [from_second(e) for e in y]
    t = [[s[i][j] + (q1[i][j] - xq1[i][j]) for j in range(5)] for i in range(5)]
    mx_right = [[xq1[i][j] - xn[i][j] for j in range(5)] for i in range(5)]
    m0_right = [y1[i] + g[i] for i in range(5)]
    solved = solve(t, columns_of(q1) + columns_of(mx_right) + [m0_right])
    mc, mx, m0 = rows_of(solved[:5]), rows_of(solved[5:10]), solved[10]
    for i in range(5):
        for j in range(5):
            mid_ref[5 * i + j] = mc[i][j]
            mid_ref[25 + 5 * i + j] = mx[i][j]
        mid_ref[50 + i] = m0[i]
    left = mat_cols(q, solved)
    s1 = [[from_second(e) for e in row] for row in s]
    xn1 = [[from_second(e) for e in row] for row in xn]
    g1 = [from_second(e) for e in g]
    n1 = [[xn1[i][j] - s1[i][j] for j in range(5)] for i in range(5)]
    cols = mat_cols(n1, solved)
    for i in range(5):
        for j in range(5):
            entry = 5 * i + j
            port[pl.ds(8 * entry, 8), :] = s1[i][j] + cols[j][i]
            port[pl.ds(8 * (25 + entry), 8), :] = xn1[i][j] + cols[5 + j][i]
            port[pl.ds(8 * (55 + entry), 8), :] = left[j][i]
            port[pl.ds(8 * (80 + entry), 8), :] = xq[i][j] + left[5 + j][i]
        port[pl.ds(8 * (50 + i), 8), :] = g1[i] - cols[10][i]
        port[pl.ds(8 * (105 + i), 8), :] = y[i] + left[10][i]
    for e in range(110, ENTRIES):
        port[pl.ds(8 * e, 8), :] = zeros()
    planes = 4 // inner
    for offset, port_ref in enumerate(port_refs):
        target = lax.rem(at + offset, inner) * planes
        for z in range(planes):
            block = port[pl.ds(2 * (target + z), ENTRIES, stride=8), :]
            port_ref[pl.ds(z, ENTRIES, stride=planes), :] = block


def cell_rows(k):
    return pl.ds(k, 8, stride=HALF)


def start_tables(jac_ref, tin, turned):
    tin[...] = jnp.zeros((128, 128), F32)
    jac = jac_ref[...]
    tin[pl.ds(0, 25), :] = jac
    for base, shift in ((35, 1), (60, 127)):
        turned[...] = pltpu.roll(jac, shift, 1)
        for i in range(5):
            for j in range(5):
                total = jac_ref[pl.ds(5 * i, 1), :] * turned[pl.ds(j, 1), :]
                for k in range(1, 5):
                    total = total + jac_ref[pl.ds(5 * i + k, 1), :] * turned[pl.ds(5 * k + j, 1), :]
                tin[pl.ds(base + 5 * i + j, 1), :] = total


def start_sweep(state, keep, mid_ref, raw):
    init_state(state)
    init_first_edge(state)
    f = raw(0)
    for i in range(5):
        keep[i] = f[i]
        mid_ref[55 + i] = f[i]


def run_chunk(state, fac_ref, raw, keep, tables):
    step = pl.program_id(0)
    count = jnp.where(step == STEPS - 1, CHUNK - 1, CHUNK)

    def one(slot, carry):
        sweep_step(step * CHUNK + slot, state, fac_ref, slot, raw, keep, tables)
        return carry

    def two(pair, carry):
        one(2 * pair, carry)
        return one(2 * pair + 1, carry)

    lax.fori_loop(0, count // 2, two, 0)

    @pl.when(count % 2 == 1)
    def _():
        one(count - 1, 0)


def forward_x_kernel(
    spots_ref, first_ref, last_ref, q_ref, visc_ref, mx_ref, my_ref, jacx_ref, jacy_ref,
    south_ref, north_ref,
    fac_ref, mid_ref, tab, eps, dlt, port0, port1,
    state, keep, g1, g2, tin, turned, port,
):
    step = pl.program_id(0)
    lanes = lax.broadcasted_iota(jnp.int32, (8, 128), 1)

    def raw(k):
        rows = cell_rows(k)
        table = tab[rows, :]
        d, a, b = dlt[rows, :], g1[rows, :], g2[rows, :]
        diff_y, base = [], []
        for c in range(5):
            here = q_ref[c, rows, :]
            south = jnp.where(lanes == 0, lane(table, 25 + c), pltpu.roll(here, 1, 1))
            north = jnp.where(lanes == 127, lane(table, 30 + c), pltpu.roll(here, 127, 1))
            diff_y.append(north - south)
            base.append(d * here + a * ((north - 2.0 * here) + south))
        right = []
        for i in range(5):
            total = jacy_ref[pl.ds(5 * i, 1), :] * diff_y[0]
            for j in range(1, 5):
                total = total + jacy_ref[pl.ds(5 * i + j, 1), :] * diff_y[j]
            right.append(base[i] - b * total)
        return right

    @pl.when(step == 0)
    def _():
        mx = mx_ref[...]
        my = my_ref[...]
        not_first = jnp.where(first_ref[1] > 0, 0.0, 1.0)
        not_last = jnp.where(last_ref[1] > 0, 0.0, 1.0)
        start_tables(jacx_ref, tin, turned)
        for z in range(4):
            rows = pl.ds(128 * z, 128)
            visc = visc_ref[rows, :]
            e = 1.0 / (visc * mx)
            d = e * e * visc
            eps[rows, :] = e
            dlt[rows, :] = d
            g2[rows, :] = d * my
            g1[rows, :] = (d * my) * (my * visc)
            for c in range(5):
                tin[pl.ds(25 + c, 1), :] = south_ref[pl.ds(4 * c + z, 1), :] * not_first
                tin[pl.ds(30 + c, 1), :] = north_ref[pl.ds(4 * c + z, 1), :] * not_last
            tab[rows, :] = tin[...].T
        start_sweep(state, keep, mid_ref, raw)

    tables = (tab, eps, dlt)
    run_chunk(state, fac_ref, raw, keep, tables)

    @pl.when(step == STEPS - 1)
    def _():
        ports = (port0, port1)
        finish_sweep(spots_ref[1], 2, state, port, ports, mid_ref, raw, keep, tables)


def forward_y_kernel(
    spots_ref, p_ref, visc_ref, my_ref, jacy_ref,
    fac_ref, mid_ref, tab, eps, dlt, port0, port1, port2, port3,
    state, keep, field, tin, turned, port,
):
    step = pl.program_id(0)

    def raw(k):
        rows = cell_rows(k)
        d = dlt[rows, :]
        return [d * field[c, rows, :] for c in range(5)]

    @pl.when(step == 0)
    def _():
        my = my_ref[...].T
        start_tables(jacy_ref, tin, turned)
        table = tin[...].T
        for z in range(4):
            rows = pl.ds(128 * z, 128)
            visc = visc_ref[rows, :].T
            e = 1.0 / (visc * my)
            eps[rows, :] = e
            dlt[rows, :] = e * e * visc
            tab[rows, :] = table
            for c in range(5):
                field[c, rows, :] = p_ref[c, rows, :].T
        start_sweep(state, keep, mid_ref, raw)

    tables = (tab, eps, dlt)
    run_chunk(state, fac_ref, raw, keep, tables)

    @pl.when(step == STEPS - 1)
    def _():
        ports = (port0, port1, port2, port3)
        finish_sweep(spots_ref[3], 4, state, port, ports, mid_ref, raw, keep, tables)


S_IN, XN_IN, G_IN, QQ_IN, XX_IN, YY_IN = 0, 25, 50, 55, 80, 105


def get_vec(ref, rows, base, *at):
    return [ref[(*at, pl.ds(rows * (base + i), rows), slice(None))] for i in range(5)]


def get_mat(ref, rows, base, *at):
    return [get_vec(ref, rows, base + 5 * i, *at) for i in range(5)]


def put_vec(ref, rows, base, vector, *at):
    for i in range(5):
        ref[(*at, pl.ds(rows * (base + i), rows), slice(None))] = vector[i]


def put_mat(ref, rows, base, matrix, *at):
    for i in range(5):
        put_vec(ref, rows, base + 5 * i, matrix[i], *at)


def combine(left, right, sign):
    return [[a + sign * b for a, b in zip(p, q)] for p, q in zip(left, right)]


def get_port(ref, rows, *at):
    return (
        get_mat(ref, rows, S_IN, *at),
        get_mat(ref, rows, XN_IN, *at),
        get_vec(ref, rows, G_IN, *at),
        get_mat(ref, rows, QQ_IN, *at),
        get_mat(ref, rows, XX_IN, *at),
        get_vec(ref, rows, YY_IN, *at),
    )


def join_kernel(inner, *refs):
    spots_ref, blocks = refs[0], refs[1 : 1 + inner]
    port_ref, mid_ref, pieces = refs[1 + inner :]
    rows = 4 // inner
    at = spots_ref[1] if inner == 2 else spots_ref[3]
    for offset, block in enumerate(blocks):
        pieces[lax.rem(at + offset, inner)] = block[...]
    whole_port = get_port(pieces, rows, 0)
    for piece in range(1, inner):
        s, xn, g, qq, xx, yy = whole_port
        s1, xn1, g1, q1, x1, y1 = get_port(pieces, rows, piece)
        t = combine(s, combine(q1, x1, -1.0), 1.0)
        rhs = [y1[i] + g[i] for i in range(5)]
        solved = solve(t, columns_of(q1) + columns_of(combine(x1, xn, -1.0)) + [rhs])
        put_mat(mid_ref, rows, 0, rows_of(solved[:5]), piece - 1)
        put_mat(mid_ref, rows, 25, rows_of(solved[5:10]), piece - 1)
        put_vec(mid_ref, rows, 50, solved[10], piece - 1)
        left = mat_cols(qq, solved)
        right = mat_cols(combine(xn1, s1, -1.0), solved)
        whole_port = (
            combine(s1, rows_of(right[:5]), 1.0),
            combine(xn1, rows_of(right[5:10]), 1.0),
            [g1[i] - right[10][i] for i in range(5)],
            rows_of(left[:5]),
            combine(xx, rows_of(left[5:10]), 1.0),
            [yy[i] + left[10][i] for i in range(5)],
        )
    for base, part in zip((S_IN, XN_IN, G_IN, QQ_IN, XX_IN, YY_IN), whole_port):
        (put_vec if base in (G_IN, YY_IN) else put_mat)(port_ref, rows, base, part)
    port_ref[pl.ds(110 * rows, 2 * rows), :] = jnp.zeros((2 * rows, 128), F32)


def solve_kernel(inner, spots_ref, b0, b1, b2, b3, mid_ref, out_ref, ports, values):
    rows = 4 // inner
    group = spots_ref[0] if inner == 2 else spots_ref[2]
    for far, block in enumerate((b0, b1, b2, b3)):
        ports[lax.rem(group + far, 4)] = block[...]
    gains = []
    for piece in range(4):
        s, xn = get_mat(ports, rows, S_IN, piece), get_mat(ports, rows, XN_IN, piece)
        g = get_vec(ports, rows, G_IN, piece)
        if piece:
            h, v = gains[-1]
            gain = [[(1.0 if i == j else 0.0) - h[i][j] for j in range(5)] for i in range(5)]
            part = combine(
                rows_of(mat_cols(s, columns_of(h))), rows_of(mat_cols(xn, columns_of(gain))), 1.0
            )
            moved = mat_cols(combine(s, xn, -1.0), [v])[0]
            g = [g[i] + moved[i] for i in range(5)]
            s = part
        if piece < 3:
            yy = get_vec(ports, rows, YY_IN, piece + 1)
            reduced = combine(s, get_mat(ports, rows, XX_IN, piece + 1), -1.0)
            t = combine(reduced, get_mat(ports, rows, QQ_IN, piece + 1), 1.0)
            solved = solve(t, columns_of(reduced) + [[yy[i] + g[i] for i in range(5)]])
            gains.append((rows_of(solved[:5]), solved[5]))
        else:
            t = [[s[i][j] + (1.0 if i == j else 0.0) for j in range(5)] for i in range(5)]
            p = solve(t, [g])[0]
            put_vec(values, rows, 0, p, 4)
    for piece in range(2, -1, -1):
        h, v = gains[piece]
        moved = mat_cols(h, [p])[0]
        p = [(p[i] - moved[i]) + v[i] for i in range(5)]
        put_vec(values, rows, 0, p, piece + 1)
    put_vec(values, rows, 0, [jnp.zeros((rows, 128), F32)] * 5, 0)
    a = get_vec(values, rows, 0, group)
    c = get_vec(values, rows, 0, group + 1)
    out_ref[...] = jnp.zeros(out_ref.shape, F32)
    put_vec(out_ref, rows, 0, a)
    put_vec(out_ref, rows, 5 * inner, c)
    for piece in range(inner - 1, 0, -1):
        part = mat_cols(get_mat(mid_ref, rows, 0, piece - 1), [[c[i] - a[i] for i in range(5)]])[0]
        rest = mat_cols(get_mat(mid_ref, rows, 25, piece - 1), [a])[0]
        m0 = get_vec(mid_ref, rows, 50, piece - 1)
        c = [a[i] + ((part[i] + rest[i]) + m0[i]) for i in range(5)]
        put_vec(out_ref, rows, 5 * piece, c)


def begin_backward(inner, spots_ref, ends_refs, mid_ref, edge, ends8):
    rows = 4 // inner
    at = spots_ref[1] if inner == 2 else spots_ref[3]
    for offset, ends_ref in enumerate(ends_refs):
        plane = lax.rem(at + offset, inner) * rows
        for e in range(10):
            for z in range(rows):
                row = ends_ref[pl.ds(rows * (5 * at + e) + z, 1), :]
                ends8[e, pl.ds(2 * (plane + z), 1), :] = row
                ends8[e, pl.ds(2 * (plane + z) + 1, 1), :] = row
    a = [ends8[i] for i in range(5)]
    c = [ends8[5 + i] for i in range(5)]
    gap = [c[i] - a[i] for i in range(5)]
    part = mat_cols(load_mat(mid_ref, 0), [gap])[0]
    rest = mat_cols(load_mat(mid_ref, 25), [a])[0]
    even = even_rows()
    for i in range(5):
        middle = a[i] + ((part[i] + rest[i]) + mid_ref[50 + i])
        edge[i] = jnp.where(even, a[i], pltpu.roll(middle, 1, 0))
        edge[5 + i] = jnp.where(even, middle, c[i])


def between(k, left, right, tables, source):
    tab, eps, dlt = tables
    rows = cell_rows(k)
    e, d = eps[rows, :], dlt[rows, :]
    c = reciprocal(2.0 + d)
    gap = [right[i] - left[i] for i in range(5)]
    moved = mat_cols(table_mat(tab[rows, :], 0), [[e * value for value in gap]])[0]
    return [
        right[i] - c * ((gap[i] + moved[i]) + (d * right[i] - source[i])) for i in range(5)
    ]


def backward_chunk(fac_ref, mid_ref, edge, write, tables):
    step = pl.program_id(0)
    a = [edge[i] for i in range(5)]
    begin = jnp.where(step == 0, 1, 0)

    def one(at, following):
        slot = CHUNK - 1 - at
        m = (STEPS - 1 - step) * CHUNK + slot
        gap = [following[i] - a[i] for i in range(5)]
        r = [[fac_ref[slot, 5 * i + j] for j in range(5)] for i in range(5)]
        x = [[fac_ref[slot, 25 + 5 * i + j] for j in range(5)] for i in range(5)]
        part = mat_cols(r, [gap])[0]
        rest = mat_cols(x, [a])[0]
        here = tuple(
            following[i] - ((part[i] + rest[i]) + fac_ref[slot, 50 + i]) for i in range(5)
        )
        source = [fac_ref[slot, 55 + i] for i in range(5)]
        write(2 * m + 2, between(2 * m + 2, here, following, tables, source))
        write(2 * m + 1, here)
        return here

    @pl.when(step == 0)
    def _():
        here = one(1, tuple(edge[5 + i] for i in range(5)))
        for i in range(5):
            edge[5 + i] = here[i]

    def two(pair, following):
        return one(2 * pair + 1, one(2 * pair, following))

    final = lax.fori_loop(begin, CHUNK // 2, two, tuple(edge[5 + i] for i in range(5)))
    for i in range(5):
        edge[5 + i] = final[i]

    @pl.when(step == STEPS - 1)
    def _():
        write(0, between(0, a, final, tables, [mid_ref[55 + i] for i in range(5)]))


def backward_x_kernel(
    spots_ref, fac_ref, mid_ref, e0, e1, tab, eps, dlt, q_ref, out_ref, edge, ends8
):
    def write(k, value):
        rows = cell_rows(k)
        for i in range(5):
            out_ref[i, rows, :] = value[i] - q_ref[i, rows, :]

    @pl.when(pl.program_id(0) == 0)
    def _():
        begin_backward(2, spots_ref, (e0, e1), mid_ref, edge, ends8)
        write(HALF - 1, [edge[5 + i] for i in range(5)])

    backward_chunk(fac_ref, mid_ref, edge, write, (tab, eps, dlt))


def backward_y_kernel(
    spots_ref, fac_ref, mid_ref, e0, e1, e2, e3, tab, eps, dlt, out_ref, edge, ends8, field
):
    def write(k, value):
        for i in range(5):
            field[i, cell_rows(k), :] = value[i]

    @pl.when(pl.program_id(0) == 0)
    def _():
        begin_backward(4, spots_ref, (e0, e1, e2, e3), mid_ref, edge, ends8)
        write(HALF - 1, [edge[5 + i] for i in range(5)])

    backward_chunk(fac_ref, mid_ref, edge, write, (tab, eps, dlt))

    @pl.when(pl.program_id(0) == STEPS - 1)
    def _():
        for c in range(5):
            for z in range(4):
                rows = pl.ds(128 * z, 128)
                out_ref[c, rows, :] = field[c, rows, :].T


def whole(shape):
    return pl.BlockSpec(shape, lambda i: (0,) * len(shape))


def scalars():
    return pl.BlockSpec(memory_space=pltpu.SMEM)


def params():
    return pltpu.CompilerParams(
        dimension_semantics=("arbitrary",), vmem_limit_bytes=VMEM_LIMIT
    )


PLANE = (512, 128)


def forward_out(inner):
    ports = [(ENTRIES * 4 // inner, 128)] * inner
    shapes = [(KEPT, FACTORS, 8, 128), (60, 8, 128), PLANE, PLANE, PLANE] + ports
    return tuple(jax.ShapeDtypeStruct(shape, F32) for shape in shapes)


def forward_specs(inner):
    block = pl.BlockSpec((CHUNK, FACTORS, 8, 128), lambda i: (i, 0, 0, 0))
    return (block,) + tuple(whole(value.shape) for value in forward_out(inner)[1:])


def forward_scratch(fields):
    return (
        [pltpu.VMEM((STATE, 8, 128), F32), pltpu.VMEM((5, 8, 128), F32)]
        + fields
        + [
            pltpu.VMEM((128, 128), F32),
            pltpu.VMEM((25, 128), F32),
            pltpu.VMEM((1024, 128), F32),
        ]
    )


def forward(kernel, name, inner, flags, operands, fields):
    return pl.pallas_call(
        kernel,
        grid=(STEPS,),
        in_specs=[scalars() for _ in flags] + [whole(value.shape) for value in operands],
        out_specs=forward_specs(inner),
        out_shape=forward_out(inner),
        scratch_shapes=forward_scratch(fields),
        compiler_params=params(),
        name=name,
    )(*flags, *operands)


def small(kernel, name, flags, operands, outputs, scratch):
    vmem = pl.BlockSpec(memory_space=pltpu.VMEM)
    return pl.pallas_call(
        kernel,
        out_shape=tuple(jax.ShapeDtypeStruct(shape, F32) for shape in outputs),
        in_specs=[scalars() for _ in flags] + [vmem for _ in operands],
        out_specs=tuple(vmem for _ in outputs),
        scratch_shapes=[pltpu.VMEM(shape, F32) for shape in scratch],
        compiler_params=pltpu.CompilerParams(vmem_limit_bytes=VMEM_LIMIT),
        name=name,
    )(*flags, *operands)


FARTHEST_FIRST = {2: (1,), 4: (2, 1, 3)}


def exchange(values, axis, inner):
    count = lax.axis_size(axis)
    received = {0: values[0]}
    for offset in FARTHEST_FIRST[inner]:
        back = inner - offset
        moves = [(i, (i // inner) * inner + (i + back) % inner) for i in range(count)]
        received[offset] = lax.ppermute(values[back], axis, moves)
    return [received[offset] for offset in range(inner)]


def line_ends(ports, axis, spots):
    inner = len(ports)
    rows = 4 // inner
    count = lax.axis_size(axis)
    port_shape = (ENTRIES * rows, 128)
    mid_shape = (inner - 1, 56 * rows, 128)
    port, mid = small(
        functools.partial(join_kernel, inner), "join_" + axis, (spots,),
        exchange(ports, axis, inner), (port_shape, mid_shape), [(inner, *port_shape)],
    )
    blocks = {0: port}
    for far in FARTHEST_FIRST[4]:
        moves = [((i + far * inner) % count, i) for i in range(count)]
        blocks[far] = lax.ppermute(port, axis, moves)
    blocks = [blocks[far] for far in range(4)]
    (ends,) = small(
        functools.partial(solve_kernel, inner), "solve_" + axis, (spots,), (*blocks, mid),
        ((32, 128),), [(4, *port_shape), (5, 8 * rows, 128)],
    )
    return exchange([ends] * inner, axis, inner)


def backward(kernel, name, spots, operands, extra):
    return pl.pallas_call(
        kernel,
        grid=(STEPS,),
        in_specs=[
            scalars(),
            pl.BlockSpec((CHUNK, FACTORS, 8, 128), lambda i: (STEPS - 1 - i, 0, 0, 0)),
        ]
        + [whole(value.shape) for value in operands[1:]],
        out_specs=whole((5, 512, 128)),
        out_shape=jax.ShapeDtypeStruct((5, 512, 128), F32),
        scratch_shapes=[pltpu.VMEM((10, 8, 128), F32), pltpu.VMEM((10, 8, 128), F32)] + extra,
        compiler_params=params(),
        name=name,
    )(spots, *operands)


def halos(axis, last, initial):
    devices = lax.axis_size(axis)
    up = [(i, (i + 1) % devices) for i in range(devices)]
    down = [(j, i) for i, j in up]
    return lax.ppermute(last, axis, up), lax.ppermute(initial, axis, down)


def body(flow_state, viscosity, metric_x, metric_y, jacobian_x, jacobian_y):
    row, col = lax.axis_index("row"), lax.axis_index("col")
    spots = jnp.stack([row // 2, row % 2, col // 4, col % 4]).astype(jnp.int32)
    places = jnp.stack([row, col]).astype(jnp.int32)
    sizes = jnp.array([lax.axis_size("row"), lax.axis_size("col")], jnp.int32)
    first = (places == 0).astype(jnp.int32)
    last = (places == sizes - 1).astype(jnp.int32)
    jacx = jacobian_x.reshape(25, 128)
    jacy = jacobian_y.reshape(25, 128)

    south, north = halos(
        "col",
        flow_state[:, :, :, 127].reshape(20, 128),
        flow_state[:, :, :, 0].reshape(20, 128),
    )
    q = flow_state.reshape(5, 512, 128)
    visc = viscosity.reshape(512, 128)
    plane = [pltpu.VMEM(PLANE, F32), pltpu.VMEM(PLANE, F32)]
    field = pltpu.VMEM((5, 512, 128), F32)
    fac, mid, tab, eps, dlt, *ports = forward(
        forward_x_kernel, "forward_x", 2, (spots, first, last),
        (q, visc, metric_x, metric_y, jacx, jacy, south, north), plane,
    )
    ends = line_ends(ports, "row", spots)
    partial_value = backward(
        backward_x_kernel, "backward_x", spots, (fac, mid, *ends, tab, eps, dlt, q), []
    )
    fac, mid, tab, eps, dlt, *ports = forward(
        forward_y_kernel, "forward_y", 4, (spots,), (partial_value, visc, metric_y, jacy), [field]
    )
    ends = line_ends(ports, "col", spots)
    result = backward(
        backward_y_kernel, "backward_y", spots, (fac, mid, *ends, tab, eps, dlt), [field]
    )
    return result.reshape(5, 4, 128, 128)


def solution(mesh):
    return jax.shard_map(
        body,
        mesh=mesh,
        in_specs=(
            P(None, None, "row", "col"),
            P(None, "row", "col"),
            P("row", "col"),
            P("row", "col"),
            P(None, None, "row"),
            P(None, None, "col"),
        ),
        out_specs=P(None, None, "row", "col"),
        check_vma=False,
    )
```

```python
import functools

import jax
import jax.numpy as jnp
from jax import lax
from jax.experimental import pallas as pl
from jax.experimental.pallas import tpu as pltpu
from jax.sharding import PartitionSpec as P

F32 = jnp.float32
N = 128
HALF = 64
ENTRIES = 112
KEPT = HALF // 2
CHUNK = 8
STEPS = KEPT // CHUNK
FACTORS = 60
VMEM_LIMIT = 20 * 1024 * 1024


def zeros():
    return jnp.zeros((8, 128), F32)


def ones():
    return jnp.ones((8, 128), F32)


def lane(value, index):
    return jnp.broadcast_to(value[:, index : index + 1], (8, 128))


def mat_cols(matrix, columns):
    result = []
    for column in columns:
        out = []
        for i in range(5):
            total = matrix[i][0] * column[0]
            for k in range(1, 5):
                total = total + matrix[i][k] * column[k]
            out.append(total)
        result.append(out)
    return result


def reciprocal(value):
    guess = pl.reciprocal(value, approx=True)
    return guess * (2.0 - value * guess)


def factor(matrix):
    m = [list(row) for row in matrix]
    inverse = []
    for p in range(5):
        inv = reciprocal(m[p][p])
        inverse.append(inv)
        for i in range(p + 1, 5):
            m[i][p] = m[i][p] * inv
            for j in range(p + 1, 5):
                m[i][j] = m[i][j] - m[i][p] * m[p][j]
    for i in range(5):
        for j in range(i + 1, 5):
            m[i][j] = m[i][j] * inverse[i]
    return m, inverse


def triangular(factored, column):
    m, inverse = factored
    x = list(column)
    for i in range(1, 5):
        for p in range(i):
            x[i] = x[i] - m[i][p] * x[p]
    x = [x[i] * inverse[i] for i in range(5)]
    for i in range(3, -1, -1):
        for j in range(i + 1, 5):
            x[i] = x[i] - m[i][j] * x[j]
    return x


def solve(matrix, columns):
    factored = factor(matrix)
    return [triangular(factored, column) for column in columns]


def columns_of(matrix):
    return [[matrix[i][j] for i in range(5)] for j in range(5)]


def rows_of(columns):
    return [[columns[j][i] for j in range(5)] for i in range(5)]


def load_mat(ref, base):
    return [[ref[base + 5 * i + j] for j in range(5)] for i in range(5)]


def load_vec(ref, base):
    return [ref[base + i] for i in range(5)]


def store_mat(ref, base, matrix):
    for i in range(5):
        for j in range(5):
            ref[base + 5 * i + j] = matrix[i][j]


def store_vec(ref, base, vector):
    for i in range(5):
        ref[base + i] = vector[i]


R_AT, X_AT, W_AT, Q_AT, XQ_AT, Y_AT, STATE = 0, 25, 50, 55, 80, 105, 110


def init_state(state):
    for i in range(5):
        for j in range(5):
            state[R_AT + 5 * i + j] = ones() if i == j else zeros()
            state[X_AT + 5 * i + j] = zeros()
        state[W_AT + i] = zeros()


def init_first_edge(state):
    for i in range(5):
        for j in range(5):
            state[Q_AT + 5 * i + j] = ones() if i == j else zeros()
            state[XQ_AT + 5 * i + j] = zeros()
        state[Y_AT + i] = zeros()


def accumulate(state, r, x, w):
    q = load_mat(state, Q_AT)
    xq = load_mat(state, XQ_AT)
    y = load_vec(state, Y_AT)
    moved = mat_cols(q, columns_of(r) + columns_of(x) + [w])
    q_new = [[q[i][j] - moved[j][i] for j in range(5)] for i in range(5)]
    xq_new = [[xq[i][j] - moved[5 + j][i] for j in range(5)] for i in range(5)]
    y_new = [y[i] - moved[10][i] for i in range(5)]
    store_mat(state, Q_AT, q_new)
    store_mat(state, XQ_AT, xq_new)
    store_vec(state, Y_AT, y_new)
    return q_new, xq_new, y_new


def table_mat(table, base):
    return [[lane(table, base + 5 * i + j) for j in range(5)] for i in range(5)]


def kept_equation(m, source, tab, eps, dlt, last):
    k = 2 * m + 1
    here, back = cell_rows(k), cell_rows(k - 1)
    table = tab[here, :]
    e0, d0 = eps[here, :], dlt[here, :]
    em, dm = eps[back, :], dlt[back, :]
    cm = reciprocal(2.0 + dm)
    a = table_mat(table, 0)
    a1, a2 = cm * e0, cm * em
    a3 = a1 * em
    am, aam = table_mat(tab[back, :], 0), table_mat(table, 35)
    lower = [
        [(a1 * a[i][j] + a2 * am[i][j]) + a3 * aam[i][j] for j in range(5)] for i in range(5)
    ]
    fm, f0, fp = source
    low = cm * dm
    if last:
        shift, tilt = d0 + low, e0 * low
        first = [cm * fm[i] for i in range(5)]
        second = first
    else:
        ahead = cell_rows(k + 1)
        ep, dp = eps[ahead, :], dlt[ahead, :]
        cp = reciprocal(2.0 + dp)
        b1, b2 = cp * e0, cp * ep
        b3 = b1 * ep
        ap, aap = table_mat(tab[ahead, :], 0), table_mat(table, 60)
        upper = [
            [b3 * aap[i][j] - (b1 * a[i][j] + b2 * ap[i][j]) for j in range(5)] for i in range(5)
        ]
        high = cp * dp
        shift, tilt = d0 + (low + high), e0 * (low - high)
        first = [cm * fm[i] + cp * fp[i] for i in range(5)]
        second = [cm * fm[i] - cp * fp[i] for i in range(5)]
    excess = [[tilt * a[i][j] for j in range(5)] for i in range(5)]
    for i in range(5):
        excess[i][i] = excess[i][i] + shift
        lower[i][i] = lower[i][i] + cm
        if not last:
            upper[i][i] = upper[i][i] + cp
    moved = mat_cols(a, [[e0 * value for value in second]])[0]
    right = [(f0[i] + first[i]) + moved[i] for i in range(5)]
    if last:
        speed = [[e0 * a[i][j] for j in range(5)] for i in range(5)]
        return lower, excess, right, speed
    return lower, excess, right, upper


def local_relation(lower, excess, right, r, x, w):
    cols = mat_cols(lower, columns_of(r) + columns_of(x) + [w])
    s = [[cols[j][i] + excess[i][j] for j in range(5)] for i in range(5)]
    xn = [[cols[5 + j][i] + excess[i][j] for j in range(5)] for i in range(5)]
    g = [right[i] - cols[10][i] for i in range(5)]
    return s, xn, g


def sweep_step(m, state, fac_ref, slot, raw, keep, tables):
    r = load_mat(state, R_AT)
    x = load_mat(state, X_AT)
    w = load_vec(state, W_AT)
    fm = load_vec(keep, 0)
    f0, fp = raw(2 * m + 1), raw(2 * m + 2)
    lower, excess, right, upper = kept_equation(m, (fm, f0, fp), *tables, False)
    s, xn, g = local_relation(lower, excess, right, r, x, w)
    t = [[s[i][j] + upper[i][j] for j in range(5)] for i in range(5)]
    solved = solve(t, columns_of(s) + columns_of(xn) + [g])
    r_new = rows_of(solved[:5])
    x_new = rows_of(solved[5:10])
    w_new = [-value for value in solved[10]]
    live = jnp.where(m == 0, 0.0, 1.0)
    accumulate(
        state,
        [[live * e for e in row] for row in r],
        [[live * e for e in row] for row in x],
        [live * e for e in w],
    )
    store_mat(state, R_AT, r_new)
    store_mat(state, X_AT, x_new)
    store_vec(state, W_AT, w_new)
    store_vec(keep, 0, fp)
    for i in range(5):
        for j in range(5):
            fac_ref[slot, 5 * i + j] = r_new[i][j]
            fac_ref[slot, 25 + 5 * i + j] = x_new[i][j]
        fac_ref[slot, 50 + i] = w_new[i]
        fac_ref[slot, 55 + i] = fp[i]


def even_rows():
    return lax.broadcasted_iota(jnp.int32, (8, 128), 0) % 2 == 0


def finish_sweep(at, inner, state, port, port_refs, mid_ref, raw, keep, tables):
    tab, eps, dlt = tables
    r = load_mat(state, R_AT)
    x = load_mat(state, X_AT)
    w = load_vec(state, W_AT)
    q, xq, y = accumulate(state, r, x, w)
    rows = cell_rows(0)
    e0, d0 = eps[rows, :], dlt[rows, :]
    c0 = reciprocal(2.0 + d0)
    start_speed = [[e0 * value for value in row] for row in table_mat(tab[rows, :], 0)]
    cols = mat_cols(start_speed, columns_of(q) + columns_of(xq) + [y])
    q = [[c0 * (q[i][j] - cols[j][i]) for j in range(5)] for i in range(5)]
    xq = [[c0 * (xq[i][j] - cols[5 + j][i]) for j in range(5)] for i in range(5)]
    for i in range(5):
        xq[i][i] = xq[i][i] - c0 * d0
    y = [c0 * ((y[i] - cols[10][i]) + mid_ref[55 + i]) for i in range(5)]
    source = (load_vec(keep, 0), raw(HALF - 1), None)
    lower, excess, right, speed = kept_equation(KEPT - 1, source, tab, eps, dlt, True)
    s, xn, g = local_relation(lower, excess, right, r, x, w)
    ahead = [[(1.0 if i == j else 0.0) - speed[i][j] for j in range(5)] for i in range(5)]
    scaled = solve(ahead, columns_of(s) + columns_of(xn) + [g])
    s, xn, g = rows_of(scaled[:5]), rows_of(scaled[5:10]), scaled[10]

    def from_second(value):
        return pltpu.roll(value, 7, 0)

    q1 = [[from_second(e) for e in row] for row in q]
    xq1 = [[from_second(e) for e in row] for row in xq]
    y1 = [from_second(e) for e in y]
    t = [[s[i][j] + (q1[i][j] - xq1[i][j]) for j in range(5)] for i in range(5)]
    mx_right = [[xq1[i][j] - xn[i][j] for j in range(5)] for i in range(5)]
    m0_right = [y1[i] + g[i] for i in range(5)]
    solved = solve(t, columns_of(q1) + columns_of(mx_right) + [m0_right])
    mc, mx, m0 = rows_of(solved[:5]), rows_of(solved[5:10]), solved[10]
    for i in range(5):
        for j in range(5):
            mid_ref[5 * i + j] = mc[i][j]
            mid_ref[25 + 5 * i + j] = mx[i][j]
        mid_ref[50 + i] = m0[i]
    left = mat_cols(q, solved)
    s1 = [[from_second(e) for e in row] for row in s]
    xn1 = [[from_second(e) for e in row] for row in xn]
    g1 = [from_second(e) for e in g]
    n1 = [[xn1[i][j] - s1[i][j] for j in range(5)] for i in range(5)]
    cols = mat_cols(n1, solved)
    for i in range(5):
        for j in range(5):
            entry = 5 * i + j
            port[pl.ds(8 * entry, 8), :] = s1[i][j] + cols[j][i]
            port[pl.ds(8 * (25 + entry), 8), :] = xn1[i][j] + cols[5 + j][i]
            port[pl.ds(8 * (55 + entry), 8), :] = left[j][i]
            port[pl.ds(8 * (80 + entry), 8), :] = xq[i][j] + left[5 + j][i]
        port[pl.ds(8 * (50 + i), 8), :] = g1[i] - cols[10][i]
        port[pl.ds(8 * (105 + i), 8), :] = y[i] + left[10][i]
    for e in range(110, ENTRIES):
        port[pl.ds(8 * e, 8), :] = zeros()
    planes = 4 // inner
    for offset, port_ref in enumerate(port_refs):
        target = lax.rem(at + offset, inner) * planes
        for z in range(planes):
            block = port[pl.ds(2 * (target + z), ENTRIES, stride=8), :]
            port_ref[pl.ds(z, ENTRIES, stride=planes), :] = block


def cell_rows(k):
    return pl.ds(k, 8, stride=HALF)


def start_tables(jac_ref, tin, turned):
    tin[...] = jnp.zeros((128, 128), F32)
    jac = jac_ref[...]
    tin[pl.ds(0, 25), :] = jac
    for base, shift in ((35, 1), (60, 127)):
        turned[...] = pltpu.roll(jac, shift, 1)
        for i in range(5):
            for j in range(5):
                total = jac_ref[pl.ds(5 * i, 1), :] * turned[pl.ds(j, 1), :]
                for k in range(1, 5):
                    total = total + jac_ref[pl.ds(5 * i + k, 1), :] * turned[pl.ds(5 * k + j, 1), :]
                tin[pl.ds(base + 5 * i + j, 1), :] = total


def start_sweep(state, keep, mid_ref, raw):
    init_state(state)
    init_first_edge(state)
    f = raw(0)
    for i in range(5):
        keep[i] = f[i]
        mid_ref[55 + i] = f[i]


def run_chunk(state, fac_ref, raw, keep, tables):
    step = pl.program_id(0)
    count = jnp.where(step == STEPS - 1, CHUNK - 1, CHUNK)

    def one(slot, carry):
        sweep_step(step * CHUNK + slot, state, fac_ref, slot, raw, keep, tables)
        return carry

    def two(pair, carry):
        one(2 * pair, carry)
        return one(2 * pair + 1, carry)

    lax.fori_loop(0, count // 2, two, 0)

    @pl.when(count % 2 == 1)
    def _():
        one(count - 1, 0)


def forward_x_kernel(
    spots_ref, first_ref, last_ref, q_ref, visc_ref, mx_ref, my_ref, jacx_ref, jacy_ref,
    south_ref, north_ref,
    fac_ref, mid_ref, tab, eps, dlt, port0, port1,
    state, keep, g1, g2, tin, turned, port,
):
    step = pl.program_id(0)
    lanes = lax.broadcasted_iota(jnp.int32, (8, 128), 1)

    def raw(k):
        rows = cell_rows(k)
        table = tab[rows, :]
        d, a, b = dlt[rows, :], g1[rows, :], g2[rows, :]
        diff_y, base = [], []
        for c in range(5):
            here = q_ref[c, rows, :]
            south = jnp.where(lanes == 0, lane(table, 25 + c), pltpu.roll(here, 1, 1))
            north = jnp.where(lanes == 127, lane(table, 30 + c), pltpu.roll(here, 127, 1))
            diff_y.append(north - south)
            base.append(d * here + a * ((north - 2.0 * here) + south))
        right = []
        for i in range(5):
            total = jacy_ref[pl.ds(5 * i, 1), :] * diff_y[0]
            for j in range(1, 5):
                total = total + jacy_ref[pl.ds(5 * i + j, 1), :] * diff_y[j]
            right.append(base[i] - b * total)
        return right

    @pl.when(step == 0)
    def _():
        mx = mx_ref[...]
        my = my_ref[...]
        not_first = jnp.where(first_ref[1] > 0, 0.0, 1.0)
        not_last = jnp.where(last_ref[1] > 0, 0.0, 1.0)
        start_tables(jacx_ref, tin, turned)
        for z in range(4):
            rows = pl.ds(128 * z, 128)
            visc = visc_ref[rows, :]
            e = 1.0 / (visc * mx)
            d = e * e * visc
            eps[rows, :] = e
            dlt[rows, :] = d
            g2[rows, :] = d * my
            g1[rows, :] = (d * my) * (my * visc)
            for c in range(5):
                tin[pl.ds(25 + c, 1), :] = south_ref[pl.ds(4 * c + z, 1), :] * not_first
                tin[pl.ds(30 + c, 1), :] = north_ref[pl.ds(4 * c + z, 1), :] * not_last
            tab[rows, :] = tin[...].T
        start_sweep(state, keep, mid_ref, raw)

    tables = (tab, eps, dlt)
    run_chunk(state, fac_ref, raw, keep, tables)

    @pl.when(step == STEPS - 1)
    def _():
        ports = (port0, port1)
        finish_sweep(spots_ref[1], 2, state, port, ports, mid_ref, raw, keep, tables)


def forward_y_kernel(
    spots_ref, p_ref, visc_ref, my_ref, jacy_ref,
    fac_ref, mid_ref, tab, eps, dlt, port0, port1, port2, port3,
    state, keep, field, tin, turned, port,
):
    step = pl.program_id(0)

    def raw(k):
        rows = cell_rows(k)
        d = dlt[rows, :]
        return [d * field[c, rows, :] for c in range(5)]

    @pl.when(step == 0)
    def _():
        my = my_ref[...].T
        start_tables(jacy_ref, tin, turned)
        table = tin[...].T
        for z in range(4):
            rows = pl.ds(128 * z, 128)
            visc = visc_ref[rows, :].T
            e = 1.0 / (visc * my)
            eps[rows, :] = e
            dlt[rows, :] = e * e * visc
            tab[rows, :] = table
            for c in range(5):
                field[c, rows, :] = p_ref[c, rows, :].T
        start_sweep(state, keep, mid_ref, raw)

    tables = (tab, eps, dlt)
    run_chunk(state, fac_ref, raw, keep, tables)

    @pl.when(step == STEPS - 1)
    def _():
        ports = (port0, port1, port2, port3)
        finish_sweep(spots_ref[3], 4, state, port, ports, mid_ref, raw, keep, tables)


S_IN, XN_IN, G_IN, QQ_IN, XX_IN, YY_IN = 0, 25, 50, 55, 80, 105


def get_vec(ref, rows, base, *at):
    return [ref[(*at, pl.ds(rows * (base + i), rows), slice(None))] for i in range(5)]


def get_mat(ref, rows, base, *at):
    return [get_vec(ref, rows, base + 5 * i, *at) for i in range(5)]


def put_vec(ref, rows, base, vector, *at):
    for i in range(5):
        ref[(*at, pl.ds(rows * (base + i), rows), slice(None))] = vector[i]


def put_mat(ref, rows, base, matrix, *at):
    for i in range(5):
        put_vec(ref, rows, base + 5 * i, matrix[i], *at)


def combine(left, right, sign):
    return [[a + sign * b for a, b in zip(p, q)] for p, q in zip(left, right)]


def get_port(ref, rows, *at):
    return (
        get_mat(ref, rows, S_IN, *at),
        get_mat(ref, rows, XN_IN, *at),
        get_vec(ref, rows, G_IN, *at),
        get_mat(ref, rows, QQ_IN, *at),
        get_mat(ref, rows, XX_IN, *at),
        get_vec(ref, rows, YY_IN, *at),
    )


def join_kernel(inner, *refs):
    spots_ref, blocks = refs[0], refs[1 : 1 + inner]
    port_ref, mid_ref, pieces = refs[1 + inner :]
    rows = 4 // inner
    at = spots_ref[1] if inner == 2 else spots_ref[3]
    for offset, block in enumerate(blocks):
        pieces[lax.rem(at + offset, inner)] = block[...]
    whole_port = get_port(pieces, rows, 0)
    for piece in range(1, inner):
        s, xn, g, qq, xx, yy = whole_port
        s1, xn1, g1, q1, x1, y1 = get_port(pieces, rows, piece)
        t = combine(s, combine(q1, x1, -1.0), 1.0)
        rhs = [y1[i] + g[i] for i in range(5)]
        solved = solve(t, columns_of(q1) + columns_of(combine(x1, xn, -1.0)) + [rhs])
        put_mat(mid_ref, rows, 0, rows_of(solved[:5]), piece - 1)
        put_mat(mid_ref, rows, 25, rows_of(solved[5:10]), piece - 1)
        put_vec(mid_ref, rows, 50, solved[10], piece - 1)
        left = mat_cols(qq, solved)
        right = mat_cols(combine(xn1, s1, -1.0), solved)
        whole_port = (
            combine(s1, rows_of(right[:5]), 1.0),
            combine(xn1, rows_of(right[5:10]), 1.0),
            [g1[i] - right[10][i] for i in range(5)],
            rows_of(left[:5]),
            combine(xx, rows_of(left[5:10]), 1.0),
            [yy[i] + left[10][i] for i in range(5)],
        )
    for base, part in zip((S_IN, XN_IN, G_IN, QQ_IN, XX_IN, YY_IN), whole_port):
        (put_vec if base in (G_IN, YY_IN) else put_mat)(port_ref, rows, base, part)
    port_ref[pl.ds(110 * rows, 2 * rows), :] = jnp.zeros((2 * rows, 128), F32)


def solve_kernel(inner, spots_ref, b0, b1, b2, b3, mid_ref, out_ref, ports, values):
    rows = 4 // inner
    group = spots_ref[0] if inner == 2 else spots_ref[2]
    for far, block in enumerate((b0, b1, b2, b3)):
        ports[lax.rem(group + far, 4)] = block[...]
    gains = []
    for piece in range(4):
        s, xn = get_mat(ports, rows, S_IN, piece), get_mat(ports, rows, XN_IN, piece)
        g = get_vec(ports, rows, G_IN, piece)
        if piece:
            h, v = gains[-1]
            gain = [[(1.0 if i == j else 0.0) - h[i][j] for j in range(5)] for i in range(5)]
            part = combine(
                rows_of(mat_cols(s, columns_of(h))), rows_of(mat_cols(xn, columns_of(gain))), 1.0
            )
            moved = mat_cols(combine(s, xn, -1.0), [v])[0]
            g = [g[i] + moved[i] for i in range(5)]
            s = part
        if piece < 3:
            yy = get_vec(ports, rows, YY_IN, piece + 1)
            reduced = combine(s, get_mat(ports, rows, XX_IN, piece + 1), -1.0)
            t = combine(reduced, get_mat(ports, rows, QQ_IN, piece + 1), 1.0)
            solved = solve(t, columns_of(reduced) + [[yy[i] + g[i] for i in range(5)]])
            gains.append((rows_of(solved[:5]), solved[5]))
        else:
            t = [[s[i][j] + (1.0 if i == j else 0.0) for j in range(5)] for i in range(5)]
            p = solve(t, [g])[0]
            put_vec(values, rows, 0, p, 4)
    for piece in range(2, -1, -1):
        h, v = gains[piece]
        moved = mat_cols(h, [p])[0]
        p = [(p[i] - moved[i]) + v[i] for i in range(5)]
        put_vec(values, rows, 0, p, piece + 1)
    put_vec(values, rows, 0, [jnp.zeros((rows, 128), F32)] * 5, 0)
    a = get_vec(values, rows, 0, group)
    c = get_vec(values, rows, 0, group + 1)
    out_ref[...] = jnp.zeros(out_ref.shape, F32)
    put_vec(out_ref, rows, 0, a)
    put_vec(out_ref, rows, 5 * inner, c)
    for piece in range(inner - 1, 0, -1):
        part = mat_cols(get_mat(mid_ref, rows, 0, piece - 1), [[c[i] - a[i] for i in range(5)]])[0]
        rest = mat_cols(get_mat(mid_ref, rows, 25, piece - 1), [a])[0]
        m0 = get_vec(mid_ref, rows, 50, piece - 1)
        c = [a[i] + ((part[i] + rest[i]) + m0[i]) for i in range(5)]
        put_vec(out_ref, rows, 5 * piece, c)


def begin_backward(inner, spots_ref, ends_refs, mid_ref, edge, ends8):
    rows = 4 // inner
    at = spots_ref[1] if inner == 2 else spots_ref[3]
    for offset, ends_ref in enumerate(ends_refs):
        plane = lax.rem(at + offset, inner) * rows
        for e in range(10):
            for z in range(rows):
                row = ends_ref[pl.ds(rows * (5 * at + e) + z, 1), :]
                ends8[e, pl.ds(2 * (plane + z), 1), :] = row
                ends8[e, pl.ds(2 * (plane + z) + 1, 1), :] = row
    a = [ends8[i] for i in range(5)]
    c = [ends8[5 + i] for i in range(5)]
    gap = [c[i] - a[i] for i in range(5)]
    part = mat_cols(load_mat(mid_ref, 0), [gap])[0]
    rest = mat_cols(load_mat(mid_ref, 25), [a])[0]
    even = even_rows()
    for i in range(5):
        middle = a[i] + ((part[i] + rest[i]) + mid_ref[50 + i])
        edge[i] = jnp.where(even, a[i], pltpu.roll(middle, 1, 0))
        edge[5 + i] = jnp.where(even, middle, c[i])


def between(k, left, right, tables, source):
    tab, eps, dlt = tables
    rows = cell_rows(k)
    e, d = eps[rows, :], dlt[rows, :]
    c = reciprocal(2.0 + d)
    gap = [right[i] - left[i] for i in range(5)]
    moved = mat_cols(table_mat(tab[rows, :], 0), [[e * value for value in gap]])[0]
    return [
        right[i] - c * ((gap[i] + moved[i]) + (d * right[i] - source[i])) for i in range(5)
    ]


def backward_chunk(fac_ref, mid_ref, edge, write, tables):
    step = pl.program_id(0)
    a = [edge[i] for i in range(5)]
    begin = jnp.where(step == 0, 1, 0)

    def one(at, following):
        slot = CHUNK - 1 - at
        m = (STEPS - 1 - step) * CHUNK + slot
        gap = [following[i] - a[i] for i in range(5)]
        r = [[fac_ref[slot, 5 * i + j] for j in range(5)] for i in range(5)]
        x = [[fac_ref[slot, 25 + 5 * i + j] for j in range(5)] for i in range(5)]
        part = mat_cols(r, [gap])[0]
        rest = mat_cols(x, [a])[0]
        here = tuple(
            following[i] - ((part[i] + rest[i]) + fac_ref[slot, 50 + i]) for i in range(5)
        )
        source = [fac_ref[slot, 55 + i] for i in range(5)]
        write(2 * m + 2, between(2 * m + 2, here, following, tables, source))
        write(2 * m + 1, here)
        return here

    @pl.when(step == 0)
    def _():
        here = one(1, tuple(edge[5 + i] for i in range(5)))
        for i in range(5):
            edge[5 + i] = here[i]

    def two(pair, following):
        return one(2 * pair + 1, one(2 * pair, following))

    final = lax.fori_loop(begin, CHUNK // 2, two, tuple(edge[5 + i] for i in range(5)))
    for i in range(5):
        edge[5 + i] = final[i]

    @pl.when(step == STEPS - 1)
    def _():
        write(0, between(0, a, final, tables, [mid_ref[55 + i] for i in range(5)]))


def backward_x_kernel(
    spots_ref, fac_ref, mid_ref, e0, e1, tab, eps, dlt, q_ref, out_ref, edge, ends8
):
    def write(k, value):
        rows = cell_rows(k)
        for i in range(5):
            out_ref[i, rows, :] = value[i] - q_ref[i, rows, :]

    @pl.when(pl.program_id(0) == 0)
    def _():
        begin_backward(2, spots_ref, (e0, e1), mid_ref, edge, ends8)
        write(HALF - 1, [edge[5 + i] for i in range(5)])

    backward_chunk(fac_ref, mid_ref, edge, write, (tab, eps, dlt))


def backward_y_kernel(
    spots_ref, fac_ref, mid_ref, e0, e1, e2, e3, tab, eps, dlt, out_ref, edge, ends8, field
):
    def write(k, value):
        for i in range(5):
            field[i, cell_rows(k), :] = value[i]

    @pl.when(pl.program_id(0) == 0)
    def _():
        begin_backward(4, spots_ref, (e0, e1, e2, e3), mid_ref, edge, ends8)
        write(HALF - 1, [edge[5 + i] for i in range(5)])

    backward_chunk(fac_ref, mid_ref, edge, write, (tab, eps, dlt))

    @pl.when(pl.program_id(0) == STEPS - 1)
    def _():
        for c in range(5):
            for z in range(4):
                rows = pl.ds(128 * z, 128)
                out_ref[c, rows, :] = field[c, rows, :].T


def whole(shape):
    return pl.BlockSpec(shape, lambda i: (0,) * len(shape))


def scalars():
    return pl.BlockSpec(memory_space=pltpu.SMEM)


def params():
    return pltpu.CompilerParams(
        dimension_semantics=("arbitrary",), vmem_limit_bytes=VMEM_LIMIT
    )


PLANE = (512, 128)


def forward_out(inner):
    ports = [(ENTRIES * 4 // inner, 128)] * inner
    shapes = [(KEPT, FACTORS, 8, 128), (60, 8, 128), PLANE, PLANE, PLANE] + ports
    return tuple(jax.ShapeDtypeStruct(shape, F32) for shape in shapes)


def forward_specs(inner):
    block = pl.BlockSpec((CHUNK, FACTORS, 8, 128), lambda i: (i, 0, 0, 0))
    return (block,) + tuple(whole(value.shape) for value in forward_out(inner)[1:])


def forward_scratch(fields):
    return (
        [pltpu.VMEM((STATE, 8, 128), F32), pltpu.VMEM((5, 8, 128), F32)]
        + fields
        + [
            pltpu.VMEM((128, 128), F32),
            pltpu.VMEM((25, 128), F32),
            pltpu.VMEM((1024, 128), F32),
        ]
    )


def forward(kernel, name, inner, flags, operands, fields):
    return pl.pallas_call(
        kernel,
        grid=(STEPS,),
        in_specs=[scalars() for _ in flags] + [whole(value.shape) for value in operands],
        out_specs=forward_specs(inner),
        out_shape=forward_out(inner),
        scratch_shapes=forward_scratch(fields),
        compiler_params=params(),
        name=name,
    )(*flags, *operands)


def small(kernel, name, flags, operands, outputs, scratch):
    vmem = pl.BlockSpec(memory_space=pltpu.VMEM)
    return pl.pallas_call(
        kernel,
        out_shape=tuple(jax.ShapeDtypeStruct(shape, F32) for shape in outputs),
        in_specs=[scalars() for _ in flags] + [vmem for _ in operands],
        out_specs=tuple(vmem for _ in outputs),
        scratch_shapes=[pltpu.VMEM(shape, F32) for shape in scratch],
        compiler_params=pltpu.CompilerParams(vmem_limit_bytes=VMEM_LIMIT),
        name=name,
    )(*flags, *operands)


FARTHEST_FIRST = {2: (1,), 4: (2, 1, 3)}


def exchange(values, axis, inner):
    count = lax.axis_size(axis)
    received = {0: values[0]}
    for offset in FARTHEST_FIRST[inner]:
        back = inner - offset
        moves = [(i, (i // inner) * inner + (i + back) % inner) for i in range(count)]
        received[offset] = lax.ppermute(values[back], axis, moves)
    return [received[offset] for offset in range(inner)]


def line_ends(ports, axis, spots):
    inner = len(ports)
    rows = 4 // inner
    count = lax.axis_size(axis)
    port_shape = (ENTRIES * rows, 128)
    mid_shape = (inner - 1, 56 * rows, 128)
    port, mid = small(
        functools.partial(join_kernel, inner), "join_" + axis, (spots,),
        exchange(ports, axis, inner), (port_shape, mid_shape), [(inner, *port_shape)],
    )
    blocks = {0: port}
    for far in FARTHEST_FIRST[4]:
        moves = [((i + far * inner) % count, i) for i in range(count)]
        blocks[far] = lax.ppermute(port, axis, moves)
    blocks = [blocks[far] for far in range(4)]
    (ends,) = small(
        functools.partial(solve_kernel, inner), "solve_" + axis, (spots,), (*blocks, mid),
        ((32, 128),), [(4, *port_shape), (5, 8 * rows, 128)],
    )
    return exchange([ends] * inner, axis, inner)


def backward(kernel, name, spots, operands, extra):
    return pl.pallas_call(
        kernel,
        grid=(STEPS,),
        in_specs=[
            scalars(),
            pl.BlockSpec((CHUNK, FACTORS, 8, 128), lambda i: (STEPS - 1 - i, 0, 0, 0)),
        ]
        + [whole(value.shape) for value in operands[1:]],
        out_specs=whole((5, 512, 128)),
        out_shape=jax.ShapeDtypeStruct((5, 512, 128), F32),
        scratch_shapes=[pltpu.VMEM((10, 8, 128), F32), pltpu.VMEM((10, 8, 128), F32)] + extra,
        compiler_params=params(),
        name=name,
    )(spots, *operands)


def halos(axis, last, initial):
    devices = lax.axis_size(axis)
    up = [(i, (i + 1) % devices) for i in range(devices)]
    down = [(j, i) for i, j in up]
    return lax.ppermute(last, axis, up), lax.ppermute(initial, axis, down)


def body(flow_state, viscosity, metric_x, metric_y, jacobian_x, jacobian_y):
    row, col = lax.axis_index("row"), lax.axis_index("col")
    spots = jnp.stack([row // 2, row % 2, col // 4, col % 4]).astype(jnp.int32)
    places = jnp.stack([row, col]).astype(jnp.int32)
    sizes = jnp.array([lax.axis_size("row"), lax.axis_size("col")], jnp.int32)
    first = (places == 0).astype(jnp.int32)
    last = (places == sizes - 1).astype(jnp.int32)
    jacx = jacobian_x.reshape(25, 128)
    jacy = jacobian_y.reshape(25, 128)

    south, north = halos(
        "col",
        flow_state[:, :, :, 127].reshape(20, 128),
        flow_state[:, :, :, 0].reshape(20, 128),
    )
    q = flow_state.reshape(5, 512, 128)
    visc = viscosity.reshape(512, 128)
    plane = [pltpu.VMEM(PLANE, F32), pltpu.VMEM(PLANE, F32)]
    field = pltpu.VMEM((5, 512, 128), F32)
    fac, mid, tab, eps, dlt, *ports = forward(
        forward_x_kernel, "forward_x", 2, (spots, first, last),
        (q, visc, metric_x, metric_y, jacx, jacy, south, north), plane,
    )
    ends = line_ends(ports, "row", spots)
    partial_value = backward(
        backward_x_kernel, "backward_x", spots, (fac, mid, *ends, tab, eps, dlt, q), []
    )
    fac, mid, tab, eps, dlt, *ports = forward(
        forward_y_kernel, "forward_y", 4, (spots,), (partial_value, visc, metric_y, jacy), [field]
    )
    ends = line_ends(ports, "col", spots)
    result = backward(
        backward_y_kernel, "backward_y", spots, (fac, mid, *ends, tab, eps, dlt), [field]
    )
    return result.reshape(5, 4, 128, 128)


def solution(mesh):
    return jax.shard_map(
        body,
        mesh=mesh,
        in_specs=(
            P(None, None, "row", "col"),
            P(None, "row", "col"),
            P("row", "col"),
            P("row", "col"),
            P(None, None, "row"),
            P(None, None, "col"),
        ),
        out_specs=P(None, None, "row", "col"),
        check_vma=False,
    )
```

```python
import functools

import jax
import jax.numpy as jnp
from jax import lax
from jax.experimental import pallas as pl
from jax.experimental.pallas import tpu as pltpu
from jax.sharding import PartitionSpec as P

F32 = jnp.float32
N = 128
HALF = 64
ENTRIES = 112
KEPT = HALF // 2
CHUNK = 8
STEPS = KEPT // CHUNK
FACTORS = 60
VMEM_LIMIT = 20 * 1024 * 1024


def zeros():
    return jnp.zeros((8, 128), F32)


def ones():
    return jnp.ones((8, 128), F32)


def lane(value, index):
    return jnp.broadcast_to(value[:, index : index + 1], (8, 128))


def mat_cols(matrix, columns):
    result = []
    for column in columns:
        out = []
        for i in range(5):
            total = matrix[i][0] * column[0]
            for k in range(1, 5):
                total = total + matrix[i][k] * column[k]
            out.append(total)
        result.append(out)
    return result


def reciprocal(value):
    guess = pl.reciprocal(value, approx=True)
    return guess * (2.0 - value * guess)


def factor(matrix):
    m = [list(row) for row in matrix]
    inverse = []
    for p in range(5):
        inv = reciprocal(m[p][p])
        inverse.append(inv)
        for i in range(p + 1, 5):
            m[i][p] = m[i][p] * inv
            for j in range(p + 1, 5):
                m[i][j] = m[i][j] - m[i][p] * m[p][j]
    for i in range(5):
        for j in range(i + 1, 5):
            m[i][j] = m[i][j] * inverse[i]
    return m, inverse


def triangular(factored, column):
    m, inverse = factored
    x = list(column)
    for i in range(1, 5):
        for p in range(i):
            x[i] = x[i] - m[i][p] * x[p]
    x = [x[i] * inverse[i] for i in range(5)]
    for i in range(3, -1, -1):
        for j in range(i + 1, 5):
            x[i] = x[i] - m[i][j] * x[j]
    return x


def solve(matrix, columns):
    factored = factor(matrix)
    return [triangular(factored, column) for column in columns]


def columns_of(matrix):
    return [[matrix[i][j] for i in range(5)] for j in range(5)]


def rows_of(columns):
    return [[columns[j][i] for j in range(5)] for i in range(5)]


def load_mat(ref, base):
    return [[ref[base + 5 * i + j] for j in range(5)] for i in range(5)]


def load_vec(ref, base):
    return [ref[base + i] for i in range(5)]


def store_mat(ref, base, matrix):
    for i in range(5):
        for j in range(5):
            ref[base + 5 * i + j] = matrix[i][j]


def store_vec(ref, base, vector):
    for i in range(5):
        ref[base + i] = vector[i]


R_AT, X_AT, W_AT, Q_AT, XQ_AT, Y_AT, STATE = 0, 25, 50, 55, 80, 105, 110


def init_state(state):
    for i in range(5):
        for j in range(5):
            state[R_AT + 5 * i + j] = ones() if i == j else zeros()
            state[X_AT + 5 * i + j] = zeros()
        state[W_AT + i] = zeros()


def init_first_edge(state):
    for i in range(5):
        for j in range(5):
            state[Q_AT + 5 * i + j] = ones() if i == j else zeros()
            state[XQ_AT + 5 * i + j] = zeros()
        state[Y_AT + i] = zeros()


def accumulate(state, r, x, w):
    q = load_mat(state, Q_AT)
    xq = load_mat(state, XQ_AT)
    y = load_vec(state, Y_AT)
    moved = mat_cols(q, columns_of(r) + columns_of(x) + [w])
    q_new = [[q[i][j] - moved[j][i] for j in range(5)] for i in range(5)]
    xq_new = [[xq[i][j] - moved[5 + j][i] for j in range(5)] for i in range(5)]
    y_new = [y[i] - moved[10][i] for i in range(5)]
    store_mat(state, Q_AT, q_new)
    store_mat(state, XQ_AT, xq_new)
    store_vec(state, Y_AT, y_new)
    return q_new, xq_new, y_new


def table_mat(table, base):
    return [[lane(table, base + 5 * i + j) for j in range(5)] for i in range(5)]


def kept_equation(m, source, tab, eps, dlt, last):
    k = 2 * m + 1
    here, back = cell_rows(k), cell_rows(k - 1)
    table = tab[here, :]
    e0, d0 = eps[here, :], dlt[here, :]
    em, dm = eps[back, :], dlt[back, :]
    cm = reciprocal(2.0 + dm)
    a = table_mat(table, 0)
    a1, a2 = cm * e0, cm * em
    a3 = a1 * em
    am, aam = table_mat(tab[back, :], 0), table_mat(table, 35)
    lower = [
        [(a1 * a[i][j] + a2 * am[i][j]) + a3 * aam[i][j] for j in range(5)] for i in range(5)
    ]
    fm, f0, fp = source
    low = cm * dm
    if last:
        shift, tilt = d0 + low, e0 * low
        first = [cm * fm[i] for i in range(5)]
        second = first
    else:
        ahead = cell_rows(k + 1)
        ep, dp = eps[ahead, :], dlt[ahead, :]
        cp = reciprocal(2.0 + dp)
        b1, b2 = cp * e0, cp * ep
        b3 = b1 * ep
        ap, aap = table_mat(tab[ahead, :], 0), table_mat(table, 60)
        upper = [
            [b3 * aap[i][j] - (b1 * a[i][j] + b2 * ap[i][j]) for j in range(5)] for i in range(5)
        ]
        high = cp * dp
        shift, tilt = d0 + (low + high), e0 * (low - high)
        first = [cm * fm[i] + cp * fp[i] for i in range(5)]
        second = [cm * fm[i] - cp * fp[i] for i in range(5)]
    excess = [[tilt * a[i][j] for j in range(5)] for i in range(5)]
    for i in range(5):
        excess[i][i] = excess[i][i] + shift
        lower[i][i] = lower[i][i] + cm
        if not last:
            upper[i][i] = upper[i][i] + cp
    moved = mat_cols(a, [[e0 * value for value in second]])[0]
    right = [(f0[i] + first[i]) + moved[i] for i in range(5)]
    if last:
        speed = [[e0 * a[i][j] for j in range(5)] for i in range(5)]
        return lower, excess, right, speed
    return lower, excess, right, upper


def local_relation(lower, excess, right, r, x, w):
    cols = mat_cols(lower, columns_of(r) + columns_of(x) + [w])
    s = [[cols[j][i] + excess[i][j] for j in range(5)] for i in range(5)]
    xn = [[cols[5 + j][i] + excess[i][j] for j in range(5)] for i in range(5)]
    g = [right[i] - cols[10][i] for i in range(5)]
    return s, xn, g


def sweep_step(m, state, fac_ref, slot, raw, keep, tables):
    r = load_mat(state, R_AT)
    x = load_mat(state, X_AT)
    w = load_vec(state, W_AT)
    fm = load_vec(keep, 0)
    f0, fp = raw(2 * m + 1), raw(2 * m + 2)
    lower, excess, right, upper = kept_equation(m, (fm, f0, fp), *tables, False)
    s, xn, g = local_relation(lower, excess, right, r, x, w)
    t = [[s[i][j] + upper[i][j] for j in range(5)] for i in range(5)]
    solved = solve(t, columns_of(s) + columns_of(xn) + [g])
    r_new = rows_of(solved[:5])
    x_new = rows_of(solved[5:10])
    w_new = [-value for value in solved[10]]
    live = jnp.where(m == 0, 0.0, 1.0)
    accumulate(
        state,
        [[live * e for e in row] for row in r],
        [[live * e for e in row] for row in x],
        [live * e for e in w],
    )
    store_mat(state, R_AT, r_new)
    store_mat(state, X_AT, x_new)
    store_vec(state, W_AT, w_new)
    store_vec(keep, 0, fp)
    for i in range(5):
        for j in range(5):
            fac_ref[slot, 5 * i + j] = r_new[i][j]
            fac_ref[slot, 25 + 5 * i + j] = x_new[i][j]
        fac_ref[slot, 50 + i] = w_new[i]
        fac_ref[slot, 55 + i] = fp[i]


def even_rows():
    return lax.broadcasted_iota(jnp.int32, (8, 128), 0) % 2 == 0


def finish_sweep(at, inner, state, port, port_refs, mid_ref, raw, keep, tables):
    tab, eps, dlt = tables
    r = load_mat(state, R_AT)
    x = load_mat(state, X_AT)
    w = load_vec(state, W_AT)
    q, xq, y = accumulate(state, r, x, w)
    rows = cell_rows(0)
    e0, d0 = eps[rows, :], dlt[rows, :]
    c0 = reciprocal(2.0 + d0)
    start_speed = [[e0 * value for value in row] for row in table_mat(tab[rows, :], 0)]
    cols = mat_cols(start_speed, columns_of(q) + columns_of(xq) + [y])
    q = [[c0 * (q[i][j] - cols[j][i]) for j in range(5)] for i in range(5)]
    xq = [[c0 * (xq[i][j] - cols[5 + j][i]) for j in range(5)] for i in range(5)]
    for i in range(5):
        xq[i][i] = xq[i][i] - c0 * d0
    y = [c0 * ((y[i] - cols[10][i]) + mid_ref[55 + i]) for i in range(5)]
    source = (load_vec(keep, 0), raw(HALF - 1), None)
    lower, excess, right, speed = kept_equation(KEPT - 1, source, tab, eps, dlt, True)
    s, xn, g = local_relation(lower, excess, right, r, x, w)
    ahead = [[(1.0 if i == j else 0.0) - speed[i][j] for j in range(5)] for i in range(5)]
    scaled = solve(ahead, columns_of(s) + columns_of(xn) + [g])
    s, xn, g = rows_of(scaled[:5]), rows_of(scaled[5:10]), scaled[10]

    def from_second(value):
        return pltpu.roll(value, 7, 0)

    q1 = [[from_second(e) for e in row] for row in q]
    xq1 = [[from_second(e) for e in row] for row in xq]
    y1 = [from_second(e) for e in y]
    t = [[s[i][j] + (q1[i][j] - xq1[i][j]) for j in range(5)] for i in range(5)]
    mx_right = [[xq1[i][j] - xn[i][j] for j in range(5)] for i in range(5)]
    m0_right = [y1[i] + g[i] for i in range(5)]
    solved = solve(t, columns_of(q1) + columns_of(mx_right) + [m0_right])
    mc, mx, m0 = rows_of(solved[:5]), rows_of(solved[5:10]), solved[10]
    for i in range(5):
        for j in range(5):
            mid_ref[5 * i + j] = mc[i][j]
            mid_ref[25 + 5 * i + j] = mx[i][j]
        mid_ref[50 + i] = m0[i]
    left = mat_cols(q, solved)
    s1 = [[from_second(e) for e in row] for row in s]
    xn1 = [[from_second(e) for e in row] for row in xn]
    g1 = [from_second(e) for e in g]
    n1 = [[xn1[i][j] - s1[i][j] for j in range(5)] for i in range(5)]
    cols = mat_cols(n1, solved)
    for i in range(5):
        for j in range(5):
            entry = 5 * i + j
            port[pl.ds(8 * entry, 8), :] = s1[i][j] + cols[j][i]
            port[pl.ds(8 * (25 + entry), 8), :] = xn1[i][j] + cols[5 + j][i]
            port[pl.ds(8 * (55 + entry), 8), :] = left[j][i]
            port[pl.ds(8 * (80 + entry), 8), :] = xq[i][j] + left[5 + j][i]
        port[pl.ds(8 * (50 + i), 8), :] = g1[i] - cols[10][i]
        port[pl.ds(8 * (105 + i), 8), :] = y[i] + left[10][i]
    for e in range(110, ENTRIES):
        port[pl.ds(8 * e, 8), :] = zeros()
    planes = 4 // inner
    for offset, port_ref in enumerate(port_refs):
        target = lax.rem(at + offset, inner) * planes
        for z in range(planes):
            block = port[pl.ds(2 * (target + z), ENTRIES, stride=8), :]
            port_ref[pl.ds(z, ENTRIES, stride=planes), :] = block


def cell_rows(k):
    return pl.ds(k, 8, stride=HALF)


def start_tables(jac_ref, tin, turned):
    tin[...] = jnp.zeros((128, 128), F32)
    jac = jac_ref[...]
    tin[pl.ds(0, 25), :] = jac
    for base, shift in ((35, 1), (60, 127)):
        turned[...] = pltpu.roll(jac, shift, 1)
        for i in range(5):
            for j in range(5):
                total = jac_ref[pl.ds(5 * i, 1), :] * turned[pl.ds(j, 1), :]
                for k in range(1, 5):
                    total = total + jac_ref[pl.ds(5 * i + k, 1), :] * turned[pl.ds(5 * k + j, 1), :]
                tin[pl.ds(base + 5 * i + j, 1), :] = total


def start_sweep(state, keep, mid_ref, raw):
    init_state(state)
    init_first_edge(state)
    f = raw(0)
    for i in range(5):
        keep[i] = f[i]
        mid_ref[55 + i] = f[i]


def run_chunk(state, fac_ref, raw, keep, tables):
    step = pl.program_id(0)
    count = jnp.where(step == STEPS - 1, CHUNK - 1, CHUNK)

    def one(slot, carry):
        sweep_step(step * CHUNK + slot, state, fac_ref, slot, raw, keep, tables)
        return carry

    def two(pair, carry):
        one(2 * pair, carry)
        return one(2 * pair + 1, carry)

    def four(quad, carry):
        two(2 * quad, carry)
        return two(2 * quad + 1, carry)

    lax.fori_loop(0, count // 4, four, 0)

    @pl.when(count % 4 == 3)
    def _():
        two(count // 2 - 1, 0)
        one(count - 1, 0)


def forward_x_kernel(
    spots_ref, first_ref, last_ref, q_ref, visc_ref, mx_ref, my_ref, jacx_ref, jacy_ref,
    south_ref, north_ref,
    fac_ref, mid_ref, tab, eps, dlt, port0, port1,
    state, keep, g1, g2, tin, turned, port,
):
    step = pl.program_id(0)
    lanes = lax.broadcasted_iota(jnp.int32, (8, 128), 1)

    def raw(k):
        rows = cell_rows(k)
        table = tab[rows, :]
        d, a, b = dlt[rows, :], g1[rows, :], g2[rows, :]
        diff_y, base = [], []
        for c in range(5):
            here = q_ref[c, rows, :]
            south = jnp.where(lanes == 0, lane(table, 25 + c), pltpu.roll(here, 1, 1))
            north = jnp.where(lanes == 127, lane(table, 30 + c), pltpu.roll(here, 127, 1))
            diff_y.append(north - south)
            base.append(d * here + a * ((north - 2.0 * here) + south))
        right = []
        for i in range(5):
            total = jacy_ref[pl.ds(5 * i, 1), :] * diff_y[0]
            for j in range(1, 5):
                total = total + jacy_ref[pl.ds(5 * i + j, 1), :] * diff_y[j]
            right.append(base[i] - b * total)
        return right

    @pl.when(step == 0)
    def _():
        mx = mx_ref[...]
        my = my_ref[...]
        not_first = jnp.where(first_ref[1] > 0, 0.0, 1.0)
        not_last = jnp.where(last_ref[1] > 0, 0.0, 1.0)
        start_tables(jacx_ref, tin, turned)
        for z in range(4):
            rows = pl.ds(128 * z, 128)
            visc = visc_ref[rows, :]
            e = 1.0 / (visc * mx)
            d = e * e * visc
            eps[rows, :] = e
            dlt[rows, :] = d
            g2[rows, :] = d * my
            g1[rows, :] = (d * my) * (my * visc)
            for c in range(5):
                tin[pl.ds(25 + c, 1), :] = south_ref[pl.ds(4 * c + z, 1), :] * not_first
                tin[pl.ds(30 + c, 1), :] = north_ref[pl.ds(4 * c + z, 1), :] * not_last
            tab[rows, :] = tin[...].T
        start_sweep(state, keep, mid_ref, raw)

    tables = (tab, eps, dlt)
    run_chunk(state, fac_ref, raw, keep, tables)

    @pl.when(step == STEPS - 1)
    def _():
        ports = (port0, port1)
        finish_sweep(spots_ref[1], 2, state, port, ports, mid_ref, raw, keep, tables)


def forward_y_kernel(
    spots_ref, p_ref, visc_ref, my_ref, jacy_ref,
    fac_ref, mid_ref, tab, eps, dlt, port0, port1, port2, port3,
    state, keep, field, tin, turned, port,
):
    step = pl.program_id(0)

    def raw(k):
        rows = cell_rows(k)
        d = dlt[rows, :]
        return [d * field[c, rows, :] for c in range(5)]

    @pl.when(step == 0)
    def _():
        my = my_ref[...].T
        start_tables(jacy_ref, tin, turned)
        table = tin[...].T
        for z in range(4):
            rows = pl.ds(128 * z, 128)
            visc = visc_ref[rows, :].T
            e = 1.0 / (visc * my)
            eps[rows, :] = e
            dlt[rows, :] = e * e * visc
            tab[rows, :] = table
            for c in range(5):
                field[c, rows, :] = p_ref[c, rows, :].T
        start_sweep(state, keep, mid_ref, raw)

    tables = (tab, eps, dlt)
    run_chunk(state, fac_ref, raw, keep, tables)

    @pl.when(step == STEPS - 1)
    def _():
        ports = (port0, port1, port2, port3)
        finish_sweep(spots_ref[3], 4, state, port, ports, mid_ref, raw, keep, tables)


S_IN, XN_IN, G_IN, QQ_IN, XX_IN, YY_IN = 0, 25, 50, 55, 80, 105


def get_vec(ref, rows, base, *at):
    return [ref[(*at, pl.ds(rows * (base + i), rows), slice(None))] for i in range(5)]


def get_mat(ref, rows, base, *at):
    return [get_vec(ref, rows, base + 5 * i, *at) for i in range(5)]


def put_vec(ref, rows, base, vector, *at):
    for i in range(5):
        ref[(*at, pl.ds(rows * (base + i), rows), slice(None))] = vector[i]


def put_mat(ref, rows, base, matrix, *at):
    for i in range(5):
        put_vec(ref, rows, base + 5 * i, matrix[i], *at)


def combine(left, right, sign):
    return [[a + sign * b for a, b in zip(p, q)] for p, q in zip(left, right)]


def get_port(ref, rows, *at):
    return (
        get_mat(ref, rows, S_IN, *at),
        get_mat(ref, rows, XN_IN, *at),
        get_vec(ref, rows, G_IN, *at),
        get_mat(ref, rows, QQ_IN, *at),
        get_mat(ref, rows, XX_IN, *at),
        get_vec(ref, rows, YY_IN, *at),
    )


def join_kernel(inner, *refs):
    spots_ref, blocks = refs[0], refs[1 : 1 + inner]
    port_ref, mid_ref, pieces = refs[1 + inner :]
    rows = 4 // inner
    at = spots_ref[1] if inner == 2 else spots_ref[3]
    for offset, block in enumerate(blocks):
        pieces[lax.rem(at + offset, inner)] = block[...]
    whole_port = get_port(pieces, rows, 0)
    for piece in range(1, inner):
        s, xn, g, qq, xx, yy = whole_port
        s1, xn1, g1, q1, x1, y1 = get_port(pieces, rows, piece)
        t = combine(s, combine(q1, x1, -1.0), 1.0)
        rhs = [y1[i] + g[i] for i in range(5)]
        solved = solve(t, columns_of(q1) + columns_of(combine(x1, xn, -1.0)) + [rhs])
        put_mat(mid_ref, rows, 0, rows_of(solved[:5]), piece - 1)
        put_mat(mid_ref, rows, 25, rows_of(solved[5:10]), piece - 1)
        put_vec(mid_ref, rows, 50, solved[10], piece - 1)
        left = mat_cols(qq, solved)
        right = mat_cols(combine(xn1, s1, -1.0), solved)
        whole_port = (
            combine(s1, rows_of(right[:5]), 1.0),
            combine(xn1, rows_of(right[5:10]), 1.0),
            [g1[i] - right[10][i] for i in range(5)],
            rows_of(left[:5]),
            combine(xx, rows_of(left[5:10]), 1.0),
            [yy[i] + left[10][i] for i in range(5)],
        )
    for base, part in zip((S_IN, XN_IN, G_IN, QQ_IN, XX_IN, YY_IN), whole_port):
        (put_vec if base in (G_IN, YY_IN) else put_mat)(port_ref, rows, base, part)
    port_ref[pl.ds(110 * rows, 2 * rows), :] = jnp.zeros((2 * rows, 128), F32)


def solve_kernel(inner, spots_ref, b0, b1, b2, b3, mid_ref, out_ref, ports, values):
    rows = 4 // inner
    group = spots_ref[0] if inner == 2 else spots_ref[2]
    for far, block in enumerate((b0, b1, b2, b3)):
        ports[lax.rem(group + far, 4)] = block[...]
    gains = []
    for piece in range(4):
        s, xn = get_mat(ports, rows, S_IN, piece), get_mat(ports, rows, XN_IN, piece)
        g = get_vec(ports, rows, G_IN, piece)
        if piece:
            h, v = gains[-1]
            gain = [[(1.0 if i == j else 0.0) - h[i][j] for j in range(5)] for i in range(5)]
            part = combine(
                rows_of(mat_cols(s, columns_of(h))), rows_of(mat_cols(xn, columns_of(gain))), 1.0
            )
            moved = mat_cols(combine(s, xn, -1.0), [v])[0]
            g = [g[i] + moved[i] for i in range(5)]
            s = part
        if piece < 3:
            yy = get_vec(ports, rows, YY_IN, piece + 1)
            reduced = combine(s, get_mat(ports, rows, XX_IN, piece + 1), -1.0)
            t = combine(reduced, get_mat(ports, rows, QQ_IN, piece + 1), 1.0)
            solved = solve(t, columns_of(reduced) + [[yy[i] + g[i] for i in range(5)]])
            gains.append((rows_of(solved[:5]), solved[5]))
        else:
            t = [[s[i][j] + (1.0 if i == j else 0.0) for j in range(5)] for i in range(5)]
            p = solve(t, [g])[0]
            put_vec(values, rows, 0, p, 4)
    for piece in range(2, -1, -1):
        h, v = gains[piece]
        moved = mat_cols(h, [p])[0]
        p = [(p[i] - moved[i]) + v[i] for i in range(5)]
        put_vec(values, rows, 0, p, piece + 1)
    put_vec(values, rows, 0, [jnp.zeros((rows, 128), F32)] * 5, 0)
    a = get_vec(values, rows, 0, group)
    c = get_vec(values, rows, 0, group + 1)
    out_ref[...] = jnp.zeros(out_ref.shape, F32)
    put_vec(out_ref, rows, 0, a)
    put_vec(out_ref, rows, 5 * inner, c)
    for piece in range(inner - 1, 0, -1):
        part = mat_cols(get_mat(mid_ref, rows, 0, piece - 1), [[c[i] - a[i] for i in range(5)]])[0]
        rest = mat_cols(get_mat(mid_ref, rows, 25, piece - 1), [a])[0]
        m0 = get_vec(mid_ref, rows, 50, piece - 1)
        c = [a[i] + ((part[i] + rest[i]) + m0[i]) for i in range(5)]
        put_vec(out_ref, rows, 5 * piece, c)


def begin_backward(inner, spots_ref, ends_refs, mid_ref, edge, ends8):
    rows = 4 // inner
    at = spots_ref[1] if inner == 2 else spots_ref[3]
    for offset, ends_ref in enumerate(ends_refs):
        plane = lax.rem(at + offset, inner) * rows
        for e in range(10):
            for z in range(rows):
                row = ends_ref[pl.ds(rows * (5 * at + e) + z, 1), :]
                ends8[e, pl.ds(2 * (plane + z), 1), :] = row
                ends8[e, pl.ds(2 * (plane + z) + 1, 1), :] = row
    a = [ends8[i] for i in range(5)]
    c = [ends8[5 + i] for i in range(5)]
    gap = [c[i] - a[i] for i in range(5)]
    part = mat_cols(load_mat(mid_ref, 0), [gap])[0]
    rest = mat_cols(load_mat(mid_ref, 25), [a])[0]
    even = even_rows()
    for i in range(5):
        middle = a[i] + ((part[i] + rest[i]) + mid_ref[50 + i])
        edge[i] = jnp.where(even, a[i], pltpu.roll(middle, 1, 0))
        edge[5 + i] = jnp.where(even, middle, c[i])


def between(k, left, right, tables, source):
    tab, eps, dlt = tables
    rows = cell_rows(k)
    e, d = eps[rows, :], dlt[rows, :]
    c = reciprocal(2.0 + d)
    gap = [right[i] - left[i] for i in range(5)]
    moved = mat_cols(table_mat(tab[rows, :], 0), [[e * value for value in gap]])[0]
    return [
        right[i] - c * ((gap[i] + moved[i]) + (d * right[i] - source[i])) for i in range(5)
    ]


def backward_chunk(fac_ref, mid_ref, edge, write, tables):
    step = pl.program_id(0)
    a = [edge[i] for i in range(5)]
    begin = jnp.where(step == 0, 1, 0)

    def one(at, following):
        slot = CHUNK - 1 - at
        m = (STEPS - 1 - step) * CHUNK + slot
        gap = [following[i] - a[i] for i in range(5)]
        r = [[fac_ref[slot, 5 * i + j] for j in range(5)] for i in range(5)]
        x = [[fac_ref[slot, 25 + 5 * i + j] for j in range(5)] for i in range(5)]
        part = mat_cols(r, [gap])[0]
        rest = mat_cols(x, [a])[0]
        here = tuple(
            following[i] - ((part[i] + rest[i]) + fac_ref[slot, 50 + i]) for i in range(5)
        )
        source = [fac_ref[slot, 55 + i] for i in range(5)]
        write(2 * m + 2, between(2 * m + 2, here, following, tables, source))
        write(2 * m + 1, here)
        return here

    @pl.when(step == 0)
    def _():
        here = one(1, tuple(edge[5 + i] for i in range(5)))
        for i in range(5):
            edge[5 + i] = here[i]

    def two(pair, following):
        return one(2 * pair + 1, one(2 * pair, following))

    final = lax.fori_loop(begin, CHUNK // 2, two, tuple(edge[5 + i] for i in range(5)))
    for i in range(5):
        edge[5 + i] = final[i]

    @pl.when(step == STEPS - 1)
    def _():
        write(0, between(0, a, final, tables, [mid_ref[55 + i] for i in range(5)]))


def backward_x_kernel(
    spots_ref, fac_ref, mid_ref, e0, e1, tab, eps, dlt, q_ref, out_ref, edge, ends8
):
    def write(k, value):
        rows = cell_rows(k)
        for i in range(5):
            out_ref[i, rows, :] = value[i] - q_ref[i, rows, :]

    @pl.when(pl.program_id(0) == 0)
    def _():
        begin_backward(2, spots_ref, (e0, e1), mid_ref, edge, ends8)
        write(HALF - 1, [edge[5 + i] for i in range(5)])

    backward_chunk(fac_ref, mid_ref, edge, write, (tab, eps, dlt))


def backward_y_kernel(
    spots_ref, fac_ref, mid_ref, e0, e1, e2, e3, tab, eps, dlt, out_ref, edge, ends8, field
):
    def write(k, value):
        for i in range(5):
            field[i, cell_rows(k), :] = value[i]

    @pl.when(pl.program_id(0) == 0)
    def _():
        begin_backward(4, spots_ref, (e0, e1, e2, e3), mid_ref, edge, ends8)
        write(HALF - 1, [edge[5 + i] for i in range(5)])

    backward_chunk(fac_ref, mid_ref, edge, write, (tab, eps, dlt))

    @pl.when(pl.program_id(0) == STEPS - 1)
    def _():
        for c in range(5):
            for z in range(4):
                rows = pl.ds(128 * z, 128)
                out_ref[c, rows, :] = field[c, rows, :].T


def whole(shape):
    return pl.BlockSpec(shape, lambda i: (0,) * len(shape))


def scalars():
    return pl.BlockSpec(memory_space=pltpu.SMEM)


def params():
    return pltpu.CompilerParams(
        dimension_semantics=("arbitrary",), vmem_limit_bytes=VMEM_LIMIT
    )


PLANE = (512, 128)


def forward_out(inner):
    ports = [(ENTRIES * 4 // inner, 128)] * inner
    shapes = [(KEPT, FACTORS, 8, 128), (60, 8, 128), PLANE, PLANE, PLANE] + ports
    return tuple(jax.ShapeDtypeStruct(shape, F32) for shape in shapes)


def forward_specs(inner):
    block = pl.BlockSpec((CHUNK, FACTORS, 8, 128), lambda i: (i, 0, 0, 0))
    return (block,) + tuple(whole(value.shape) for value in forward_out(inner)[1:])


def forward_scratch(fields):
    return (
        [pltpu.VMEM((STATE, 8, 128), F32), pltpu.VMEM((5, 8, 128), F32)]
        + fields
        + [
            pltpu.VMEM((128, 128), F32),
            pltpu.VMEM((25, 128), F32),
            pltpu.VMEM((1024, 128), F32),
        ]
    )


def forward(kernel, name, inner, flags, operands, fields):
    return pl.pallas_call(
        kernel,
        grid=(STEPS,),
        in_specs=[scalars() for _ in flags] + [whole(value.shape) for value in operands],
        out_specs=forward_specs(inner),
        out_shape=forward_out(inner),
        scratch_shapes=forward_scratch(fields),
        compiler_params=params(),
        name=name,
    )(*flags, *operands)


def small(kernel, name, flags, operands, outputs, scratch):
    vmem = pl.BlockSpec(memory_space=pltpu.VMEM)
    return pl.pallas_call(
        kernel,
        out_shape=tuple(jax.ShapeDtypeStruct(shape, F32) for shape in outputs),
        in_specs=[scalars() for _ in flags] + [vmem for _ in operands],
        out_specs=tuple(vmem for _ in outputs),
        scratch_shapes=[pltpu.VMEM(shape, F32) for shape in scratch],
        compiler_params=pltpu.CompilerParams(vmem_limit_bytes=VMEM_LIMIT),
        name=name,
    )(*flags, *operands)


FARTHEST_FIRST = {2: (1,), 4: (2, 1, 3)}


def exchange(values, axis, inner):
    count = lax.axis_size(axis)
    received = {0: values[0]}
    for offset in FARTHEST_FIRST[inner]:
        back = inner - offset
        moves = [(i, (i // inner) * inner + (i + back) % inner) for i in range(count)]
        received[offset] = lax.ppermute(values[back], axis, moves)
    return [received[offset] for offset in range(inner)]


def line_ends(ports, axis, spots):
    inner = len(ports)
    rows = 4 // inner
    count = lax.axis_size(axis)
    port_shape = (ENTRIES * rows, 128)
    mid_shape = (inner - 1, 56 * rows, 128)
    port, mid = small(
        functools.partial(join_kernel, inner), "join_" + axis, (spots,),
        exchange(ports, axis, inner), (port_shape, mid_shape), [(inner, *port_shape)],
    )
    blocks = {0: port}
    for far in FARTHEST_FIRST[4]:
        moves = [((i + far * inner) % count, i) for i in range(count)]
        blocks[far] = lax.ppermute(port, axis, moves)
    blocks = [blocks[far] for far in range(4)]
    (ends,) = small(
        functools.partial(solve_kernel, inner), "solve_" + axis, (spots,), (*blocks, mid),
        ((32, 128),), [(4, *port_shape), (5, 8 * rows, 128)],
    )
    return exchange([ends] * inner, axis, inner)


def backward(kernel, name, spots, operands, extra):
    return pl.pallas_call(
        kernel,
        grid=(STEPS,),
        in_specs=[
            scalars(),
            pl.BlockSpec((CHUNK, FACTORS, 8, 128), lambda i: (STEPS - 1 - i, 0, 0, 0)),
        ]
        + [whole(value.shape) for value in operands[1:]],
        out_specs=whole((5, 512, 128)),
        out_shape=jax.ShapeDtypeStruct((5, 512, 128), F32),
        scratch_shapes=[pltpu.VMEM((10, 8, 128), F32), pltpu.VMEM((10, 8, 128), F32)] + extra,
        compiler_params=params(),
        name=name,
    )(spots, *operands)


def halos(axis, last, initial):
    devices = lax.axis_size(axis)
    up = [(i, (i + 1) % devices) for i in range(devices)]
    down = [(j, i) for i, j in up]
    return lax.ppermute(last, axis, up), lax.ppermute(initial, axis, down)


def body(flow_state, viscosity, metric_x, metric_y, jacobian_x, jacobian_y):
    row, col = lax.axis_index("row"), lax.axis_index("col")
    spots = jnp.stack([row // 2, row % 2, col // 4, col % 4]).astype(jnp.int32)
    places = jnp.stack([row, col]).astype(jnp.int32)
    sizes = jnp.array([lax.axis_size("row"), lax.axis_size("col")], jnp.int32)
    first = (places == 0).astype(jnp.int32)
    last = (places == sizes - 1).astype(jnp.int32)
    jacx = jacobian_x.reshape(25, 128)
    jacy = jacobian_y.reshape(25, 128)

    south, north = halos(
        "col",
        flow_state[:, :, :, 127].reshape(20, 128),
        flow_state[:, :, :, 0].reshape(20, 128),
    )
    q = flow_state.reshape(5, 512, 128)
    visc = viscosity.reshape(512, 128)
    plane = [pltpu.VMEM(PLANE, F32), pltpu.VMEM(PLANE, F32)]
    field = pltpu.VMEM((5, 512, 128), F32)
    fac, mid, tab, eps, dlt, *ports = forward(
        forward_x_kernel, "forward_x", 2, (spots, first, last),
        (q, visc, metric_x, metric_y, jacx, jacy, south, north), plane,
    )
    ends = line_ends(ports, "row", spots)
    partial_value = backward(
        backward_x_kernel, "backward_x", spots, (fac, mid, *ends, tab, eps, dlt, q), []
    )
    fac, mid, tab, eps, dlt, *ports = forward(
        forward_y_kernel, "forward_y", 4, (spots,), (partial_value, visc, metric_y, jacy), [field]
    )
    ends = line_ends(ports, "col", spots)
    result = backward(
        backward_y_kernel, "backward_y", spots, (fac, mid, *ends, tab, eps, dlt), [field]
    )
    return result.reshape(5, 4, 128, 128)


def solution(mesh):
    return jax.shard_map(
        body,
        mesh=mesh,
        in_specs=(
            P(None, None, "row", "col"),
            P(None, "row", "col"),
            P("row", "col"),
            P("row", "col"),
            P(None, None, "row"),
            P(None, None, "col"),
        ),
        out_specs=P(None, None, "row", "col"),
        check_vma=False,
    )
```

```python
import functools

import jax
import jax.numpy as jnp
from jax import lax
from jax.experimental import pallas as pl
from jax.experimental.pallas import tpu as pltpu
from jax.sharding import PartitionSpec as P

F32 = jnp.float32
N = 128
HALF = 64
ENTRIES = 112
KEPT = HALF // 2
CHUNK = 8
STEPS = KEPT // CHUNK
FACTORS = 60
VMEM_LIMIT = 20 * 1024 * 1024


def zeros():
    return jnp.zeros((8, 128), F32)


def ones():
    return jnp.ones((8, 128), F32)


def lane(value, index):
    return jnp.broadcast_to(value[:, index : index + 1], (8, 128))


def mat_cols(matrix, columns):
    result = []
    for column in columns:
        out = []
        for i in range(5):
            total = matrix[i][0] * column[0]
            for k in range(1, 5):
                total = total + matrix[i][k] * column[k]
            out.append(total)
        result.append(out)
    return result


def reciprocal(value):
    guess = pl.reciprocal(value, approx=True)
    return guess * (2.0 - value * guess)


def factor(matrix):
    m = [list(row) for row in matrix]
    inverse = []
    for p in range(5):
        inv = reciprocal(m[p][p])
        inverse.append(inv)
        for i in range(p + 1, 5):
            m[i][p] = m[i][p] * inv
            for j in range(p + 1, 5):
                m[i][j] = m[i][j] - m[i][p] * m[p][j]
    for i in range(5):
        for j in range(i + 1, 5):
            m[i][j] = m[i][j] * inverse[i]
    return m, inverse


def triangular(factored, column):
    m, inverse = factored
    x = list(column)
    for i in range(1, 5):
        for p in range(i):
            x[i] = x[i] - m[i][p] * x[p]
    x = [x[i] * inverse[i] for i in range(5)]
    for i in range(3, -1, -1):
        for j in range(i + 1, 5):
            x[i] = x[i] - m[i][j] * x[j]
    return x


def solve(matrix, columns):
    factored = factor(matrix)
    return [triangular(factored, column) for column in columns]


def columns_of(matrix):
    return [[matrix[i][j] for i in range(5)] for j in range(5)]


def rows_of(columns):
    return [[columns[j][i] for j in range(5)] for i in range(5)]


def load_mat(ref, base):
    return [[ref[base + 5 * i + j] for j in range(5)] for i in range(5)]


def load_vec(ref, base):
    return [ref[base + i] for i in range(5)]


def store_mat(ref, base, matrix):
    for i in range(5):
        for j in range(5):
            ref[base + 5 * i + j] = matrix[i][j]


def store_vec(ref, base, vector):
    for i in range(5):
        ref[base + i] = vector[i]


R_AT, X_AT, W_AT, Q_AT, XQ_AT, Y_AT, STATE = 0, 25, 50, 55, 80, 105, 110


def init_state(state):
    for i in range(5):
        for j in range(5):
            state[R_AT + 5 * i + j] = ones() if i == j else zeros()
            state[X_AT + 5 * i + j] = zeros()
        state[W_AT + i] = zeros()


def init_first_edge(state):
    for i in range(5):
        for j in range(5):
            state[Q_AT + 5 * i + j] = ones() if i == j else zeros()
            state[XQ_AT + 5 * i + j] = zeros()
        state[Y_AT + i] = zeros()


def accumulate(state, r, x, w):
    q = load_mat(state, Q_AT)
    xq = load_mat(state, XQ_AT)
    y = load_vec(state, Y_AT)
    moved = mat_cols(q, columns_of(r) + columns_of(x) + [w])
    q_new = [[q[i][j] - moved[j][i] for j in range(5)] for i in range(5)]
    xq_new = [[xq[i][j] - moved[5 + j][i] for j in range(5)] for i in range(5)]
    y_new = [y[i] - moved[10][i] for i in range(5)]
    store_mat(state, Q_AT, q_new)
    store_mat(state, XQ_AT, xq_new)
    store_vec(state, Y_AT, y_new)
    return q_new, xq_new, y_new


def table_mat(table, base):
    return [[lane(table, base + 5 * i + j) for j in range(5)] for i in range(5)]


def kept_equation(m, source, tab, eps, dlt, last):
    k = 2 * m + 1
    here, back = cell_rows(k), cell_rows(k - 1)
    table = tab[here, :]
    e0, d0 = eps[here, :], dlt[here, :]
    em, dm = eps[back, :], dlt[back, :]
    cm = reciprocal(2.0 + dm)
    a = table_mat(table, 0)
    a1, a2 = cm * e0, cm * em
    a3 = a1 * em
    am, aam = table_mat(tab[back, :], 0), table_mat(table, 35)
    lower = [
        [(a1 * a[i][j] + a2 * am[i][j]) + a3 * aam[i][j] for j in range(5)] for i in range(5)
    ]
    fm, f0, fp = source
    low = cm * dm
    if last:
        shift, tilt = d0 + low, e0 * low
        first = [cm * fm[i] for i in range(5)]
        second = first
    else:
        ahead = cell_rows(k + 1)
        ep, dp = eps[ahead, :], dlt[ahead, :]
        cp = reciprocal(2.0 + dp)
        b1, b2 = cp * e0, cp * ep
        b3 = b1 * ep
        ap, aap = table_mat(tab[ahead, :], 0), table_mat(table, 60)
        upper = [
            [b3 * aap[i][j] - (b1 * a[i][j] + b2 * ap[i][j]) for j in range(5)] for i in range(5)
        ]
        high = cp * dp
        shift, tilt = d0 + (low + high), e0 * (low - high)
        first = [cm * fm[i] + cp * fp[i] for i in range(5)]
        second = [cm * fm[i] - cp * fp[i] for i in range(5)]
    excess = [[tilt * a[i][j] for j in range(5)] for i in range(5)]
    for i in range(5):
        excess[i][i] = excess[i][i] + shift
        lower[i][i] = lower[i][i] + cm
        if not last:
            upper[i][i] = upper[i][i] + cp
    moved = mat_cols(a, [[e0 * value for value in second]])[0]
    right = [(f0[i] + first[i]) + moved[i] for i in range(5)]
    if last:
        speed = [[e0 * a[i][j] for j in range(5)] for i in range(5)]
        return lower, excess, right, speed
    return lower, excess, right, upper


def local_relation(lower, excess, right, r, x, w):
    cols = mat_cols(lower, columns_of(r) + columns_of(x) + [w])
    s = [[cols[j][i] + excess[i][j] for j in range(5)] for i in range(5)]
    xn = [[cols[5 + j][i] + excess[i][j] for j in range(5)] for i in range(5)]
    g = [right[i] - cols[10][i] for i in range(5)]
    return s, xn, g


def sweep_step(m, state, fac_ref, slot, raw, keep, tables):
    r = load_mat(state, R_AT)
    x = load_mat(state, X_AT)
    w = load_vec(state, W_AT)
    fm = load_vec(keep, 0)
    f0, fp = raw(2 * m + 1), raw(2 * m + 2)
    lower, excess, right, upper = kept_equation(m, (fm, f0, fp), *tables, False)
    s, xn, g = local_relation(lower, excess, right, r, x, w)
    t = [[s[i][j] + upper[i][j] for j in range(5)] for i in range(5)]
    solved = solve(t, columns_of(s) + columns_of(xn) + [g])
    r_new = rows_of(solved[:5])
    x_new = rows_of(solved[5:10])
    w_new = [-value for value in solved[10]]
    live = jnp.where(m == 0, 0.0, 1.0)
    accumulate(
        state,
        [[live * e for e in row] for row in r],
        [[live * e for e in row] for row in x],
        [live * e for e in w],
    )
    store_mat(state, R_AT, r_new)
    store_mat(state, X_AT, x_new)
    store_vec(state, W_AT, w_new)
    store_vec(keep, 0, fp)
    for i in range(5):
        for j in range(5):
            fac_ref[slot, 5 * i + j] = r_new[i][j]
            fac_ref[slot, 25 + 5 * i + j] = x_new[i][j]
        fac_ref[slot, 50 + i] = w_new[i]
        fac_ref[slot, 55 + i] = fp[i]


def even_rows():
    return lax.broadcasted_iota(jnp.int32, (8, 128), 0) % 2 == 0


def finish_sweep(at, inner, state, port, port_refs, mid_ref, raw, keep, tables):
    tab, eps, dlt = tables
    r = load_mat(state, R_AT)
    x = load_mat(state, X_AT)
    w = load_vec(state, W_AT)
    q, xq, y = accumulate(state, r, x, w)
    rows = cell_rows(0)
    e0, d0 = eps[rows, :], dlt[rows, :]
    c0 = reciprocal(2.0 + d0)
    start_speed = [[e0 * value for value in row] for row in table_mat(tab[rows, :], 0)]
    cols = mat_cols(start_speed, columns_of(q) + columns_of(xq) + [y])
    q = [[c0 * (q[i][j] - cols[j][i]) for j in range(5)] for i in range(5)]
    xq = [[c0 * (xq[i][j] - cols[5 + j][i]) for j in range(5)] for i in range(5)]
    for i in range(5):
        xq[i][i] = xq[i][i] - c0 * d0
    y = [c0 * ((y[i] - cols[10][i]) + mid_ref[55 + i]) for i in range(5)]
    source = (load_vec(keep, 0), raw(HALF - 1), None)
    lower, excess, right, speed = kept_equation(KEPT - 1, source, tab, eps, dlt, True)
    s, xn, g = local_relation(lower, excess, right, r, x, w)
    ahead = [[(1.0 if i == j else 0.0) - speed[i][j] for j in range(5)] for i in range(5)]
    scaled = solve(ahead, columns_of(s) + columns_of(xn) + [g])
    s, xn, g = rows_of(scaled[:5]), rows_of(scaled[5:10]), scaled[10]

    def from_second(value):
        return pltpu.roll(value, 7, 0)

    q1 = [[from_second(e) for e in row] for row in q]
    xq1 = [[from_second(e) for e in row] for row in xq]
    y1 = [from_second(e) for e in y]
    t = [[s[i][j] + (q1[i][j] - xq1[i][j]) for j in range(5)] for i in range(5)]
    mx_right = [[xq1[i][j] - xn[i][j] for j in range(5)] for i in range(5)]
    m0_right = [y1[i] + g[i] for i in range(5)]
    solved = solve(t, columns_of(q1) + columns_of(mx_right) + [m0_right])
    mc, mx, m0 = rows_of(solved[:5]), rows_of(solved[5:10]), solved[10]
    for i in range(5):
        for j in range(5):
            mid_ref[5 * i + j] = mc[i][j]
            mid_ref[25 + 5 * i + j] = mx[i][j]
        mid_ref[50 + i] = m0[i]
    left = mat_cols(q, solved)
    s1 = [[from_second(e) for e in row] for row in s]
    xn1 = [[from_second(e) for e in row] for row in xn]
    g1 = [from_second(e) for e in g]
    n1 = [[xn1[i][j] - s1[i][j] for j in range(5)] for i in range(5)]
    cols = mat_cols(n1, solved)
    for i in range(5):
        for j in range(5):
            entry = 5 * i + j
            port[pl.ds(8 * entry, 8), :] = s1[i][j] + cols[j][i]
            port[pl.ds(8 * (25 + entry), 8), :] = xn1[i][j] + cols[5 + j][i]
            port[pl.ds(8 * (55 + entry), 8), :] = left[j][i]
            port[pl.ds(8 * (80 + entry), 8), :] = xq[i][j] + left[5 + j][i]
        port[pl.ds(8 * (50 + i), 8), :] = g1[i] - cols[10][i]
        port[pl.ds(8 * (105 + i), 8), :] = y[i] + left[10][i]
    for e in range(110, ENTRIES):
        port[pl.ds(8 * e, 8), :] = zeros()
    planes = 4 // inner
    for offset, port_ref in enumerate(port_refs):
        target = lax.rem(at + offset, inner) * planes
        for z in range(planes):
            block = port[pl.ds(2 * (target + z), ENTRIES, stride=8), :]
            port_ref[pl.ds(z, ENTRIES, stride=planes), :] = block


def cell_rows(k):
    return pl.ds(k, 8, stride=HALF)


def start_tables(jac_ref, tin, turned):
    tin[...] = jnp.zeros((128, 128), F32)
    jac = jac_ref[...]
    tin[pl.ds(0, 25), :] = jac
    for base, shift in ((35, 1), (60, 127)):
        turned[...] = pltpu.roll(jac, shift, 1)
        for i in range(5):
            for j in range(5):
                total = jac_ref[pl.ds(5 * i, 1), :] * turned[pl.ds(j, 1), :]
                for k in range(1, 5):
                    total = total + jac_ref[pl.ds(5 * i + k, 1), :] * turned[pl.ds(5 * k + j, 1), :]
                tin[pl.ds(base + 5 * i + j, 1), :] = total


def start_sweep(state, keep, mid_ref, raw):
    init_state(state)
    init_first_edge(state)
    f = raw(0)
    for i in range(5):
        keep[i] = f[i]
        mid_ref[55 + i] = f[i]


def run_chunk(state, fac_ref, raw, keep, tables):
    step = pl.program_id(0)
    count = jnp.where(step == STEPS - 1, CHUNK - 1, CHUNK)

    def one(slot, carry):
        sweep_step(step * CHUNK + slot, state, fac_ref, slot, raw, keep, tables)
        return carry

    def two(pair, carry):
        one(2 * pair, carry)
        return one(2 * pair + 1, carry)

    def four(quad, carry):
        two(2 * quad, carry)
        return two(2 * quad + 1, carry)

    lax.fori_loop(0, count // 4, four, 0)

    @pl.when(count % 4 == 3)
    def _():
        two(count // 2 - 1, 0)
        one(count - 1, 0)


def forward_x_kernel(
    spots_ref, first_ref, last_ref, q_ref, visc_ref, mx_ref, my_ref, jacx_ref, jacy_ref,
    south_ref, north_ref,
    fac_ref, mid_ref, tab, eps, dlt, port0, port1,
    state, keep, g1, g2, tin, turned, port,
):
    step = pl.program_id(0)
    lanes = lax.broadcasted_iota(jnp.int32, (8, 128), 1)

    def raw(k):
        rows = cell_rows(k)
        table = tab[rows, :]
        d, a, b = dlt[rows, :], g1[rows, :], g2[rows, :]
        diff_y, base = [], []
        for c in range(5):
            here = q_ref[c, rows, :]
            south = jnp.where(lanes == 0, lane(table, 25 + c), pltpu.roll(here, 1, 1))
            north = jnp.where(lanes == 127, lane(table, 30 + c), pltpu.roll(here, 127, 1))
            diff_y.append(north - south)
            base.append(d * here + a * ((north - 2.0 * here) + south))
        right = []
        for i in range(5):
            total = jacy_ref[pl.ds(5 * i, 1), :] * diff_y[0]
            for j in range(1, 5):
                total = total + jacy_ref[pl.ds(5 * i + j, 1), :] * diff_y[j]
            right.append(base[i] - b * total)
        return right

    @pl.when(step == 0)
    def _():
        mx = mx_ref[...]
        my = my_ref[...]
        not_first = jnp.where(first_ref[1] > 0, 0.0, 1.0)
        not_last = jnp.where(last_ref[1] > 0, 0.0, 1.0)
        start_tables(jacx_ref, tin, turned)
        for z in range(4):
            rows = pl.ds(128 * z, 128)
            visc = visc_ref[rows, :]
            e = 1.0 / (visc * mx)
            d = e * e * visc
            eps[rows, :] = e
            dlt[rows, :] = d
            g2[rows, :] = d * my
            g1[rows, :] = (d * my) * (my * visc)
            for c in range(5):
                tin[pl.ds(25 + c, 1), :] = south_ref[pl.ds(4 * c + z, 1), :] * not_first
                tin[pl.ds(30 + c, 1), :] = north_ref[pl.ds(4 * c + z, 1), :] * not_last
            tab[rows, :] = tin[...].T
        start_sweep(state, keep, mid_ref, raw)

    tables = (tab, eps, dlt)
    run_chunk(state, fac_ref, raw, keep, tables)

    @pl.when(step == STEPS - 1)
    def _():
        ports = (port0, port1)
        finish_sweep(spots_ref[1], 2, state, port, ports, mid_ref, raw, keep, tables)


def forward_y_kernel(
    spots_ref, p_ref, visc_ref, my_ref, jacy_ref,
    fac_ref, mid_ref, tab, eps, dlt, port0, port1, port2, port3,
    state, keep, field, tin, turned, port,
):
    step = pl.program_id(0)

    def raw(k):
        rows = cell_rows(k)
        d = dlt[rows, :]
        return [d * field[c, rows, :] for c in range(5)]

    @pl.when(step == 0)
    def _():
        my = my_ref[...].T
        start_tables(jacy_ref, tin, turned)
        table = tin[...].T
        for z in range(4):
            rows = pl.ds(128 * z, 128)
            visc = visc_ref[rows, :].T
            e = 1.0 / (visc * my)
            eps[rows, :] = e
            dlt[rows, :] = e * e * visc
            tab[rows, :] = table
            for c in range(5):
                field[c, rows, :] = p_ref[c, rows, :].T
        start_sweep(state, keep, mid_ref, raw)

    tables = (tab, eps, dlt)
    run_chunk(state, fac_ref, raw, keep, tables)

    @pl.when(step == STEPS - 1)
    def _():
        ports = (port0, port1, port2, port3)
        finish_sweep(spots_ref[3], 4, state, port, ports, mid_ref, raw, keep, tables)


S_IN, XN_IN, G_IN, QQ_IN, XX_IN, YY_IN = 0, 25, 50, 55, 80, 105


def get_vec(ref, rows, base, *at):
    return [ref[(*at, pl.ds(rows * (base + i), rows), slice(None))] for i in range(5)]


def get_mat(ref, rows, base, *at):
    return [get_vec(ref, rows, base + 5 * i, *at) for i in range(5)]


def put_vec(ref, rows, base, vector, *at):
    for i in range(5):
        ref[(*at, pl.ds(rows * (base + i), rows), slice(None))] = vector[i]


def put_mat(ref, rows, base, matrix, *at):
    for i in range(5):
        put_vec(ref, rows, base + 5 * i, matrix[i], *at)


def combine(left, right, sign):
    return [[a + sign * b for a, b in zip(p, q)] for p, q in zip(left, right)]


def get_port(ref, rows, *at):
    return (
        get_mat(ref, rows, S_IN, *at),
        get_mat(ref, rows, XN_IN, *at),
        get_vec(ref, rows, G_IN, *at),
        get_mat(ref, rows, QQ_IN, *at),
        get_mat(ref, rows, XX_IN, *at),
        get_vec(ref, rows, YY_IN, *at),
    )


def join_kernel(inner, *refs):
    spots_ref, blocks = refs[0], refs[1 : 1 + inner]
    port_ref, mid_ref, pieces = refs[1 + inner :]
    rows = 4 // inner
    at = spots_ref[1] if inner == 2 else spots_ref[3]
    for offset, block in enumerate(blocks):
        pieces[lax.rem(at + offset, inner)] = block[...]
    whole_port = get_port(pieces, rows, 0)
    for piece in range(1, inner):
        s, xn, g, qq, xx, yy = whole_port
        s1, xn1, g1, q1, x1, y1 = get_port(pieces, rows, piece)
        t = combine(s, combine(q1, x1, -1.0), 1.0)
        rhs = [y1[i] + g[i] for i in range(5)]
        solved = solve(t, columns_of(q1) + columns_of(combine(x1, xn, -1.0)) + [rhs])
        put_mat(mid_ref, rows, 0, rows_of(solved[:5]), piece - 1)
        put_mat(mid_ref, rows, 25, rows_of(solved[5:10]), piece - 1)
        put_vec(mid_ref, rows, 50, solved[10], piece - 1)
        left = mat_cols(qq, solved)
        right = mat_cols(combine(xn1, s1, -1.0), solved)
        whole_port = (
            combine(s1, rows_of(right[:5]), 1.0),
            combine(xn1, rows_of(right[5:10]), 1.0),
            [g1[i] - right[10][i] for i in range(5)],
            rows_of(left[:5]),
            combine(xx, rows_of(left[5:10]), 1.0),
            [yy[i] + left[10][i] for i in range(5)],
        )
    for base, part in zip((S_IN, XN_IN, G_IN, QQ_IN, XX_IN, YY_IN), whole_port):
        (put_vec if base in (G_IN, YY_IN) else put_mat)(port_ref, rows, base, part)
    port_ref[pl.ds(110 * rows, 2 * rows), :] = jnp.zeros((2 * rows, 128), F32)


def solve_kernel(inner, spots_ref, b0, b1, b2, b3, mid_ref, out_ref, ports, values):
    rows = 4 // inner
    group = spots_ref[0] if inner == 2 else spots_ref[2]
    for far, block in enumerate((b0, b1, b2, b3)):
        ports[lax.rem(group + far, 4)] = block[...]
    gains = []
    for piece in range(4):
        s, xn = get_mat(ports, rows, S_IN, piece), get_mat(ports, rows, XN_IN, piece)
        g = get_vec(ports, rows, G_IN, piece)
        if piece:
            h, v = gains[-1]
            gain = [[(1.0 if i == j else 0.0) - h[i][j] for j in range(5)] for i in range(5)]
            part = combine(
                rows_of(mat_cols(s, columns_of(h))), rows_of(mat_cols(xn, columns_of(gain))), 1.0
            )
            moved = mat_cols(combine(s, xn, -1.0), [v])[0]
            g = [g[i] + moved[i] for i in range(5)]
            s = part
        if piece < 3:
            yy = get_vec(ports, rows, YY_IN, piece + 1)
            reduced = combine(s, get_mat(ports, rows, XX_IN, piece + 1), -1.0)
            t = combine(reduced, get_mat(ports, rows, QQ_IN, piece + 1), 1.0)
            solved = solve(t, columns_of(reduced) + [[yy[i] + g[i] for i in range(5)]])
            gains.append((rows_of(solved[:5]), solved[5]))
        else:
            t = [[s[i][j] + (1.0 if i == j else 0.0) for j in range(5)] for i in range(5)]
            p = solve(t, [g])[0]
            put_vec(values, rows, 0, p, 4)
    for piece in range(2, -1, -1):
        h, v = gains[piece]
        moved = mat_cols(h, [p])[0]
        p = [(p[i] - moved[i]) + v[i] for i in range(5)]
        put_vec(values, rows, 0, p, piece + 1)
    put_vec(values, rows, 0, [jnp.zeros((rows, 128), F32)] * 5, 0)
    a = get_vec(values, rows, 0, group)
    c = get_vec(values, rows, 0, group + 1)
    out_ref[...] = jnp.zeros(out_ref.shape, F32)
    put_vec(out_ref, rows, 0, a)
    put_vec(out_ref, rows, 5 * inner, c)
    for piece in range(inner - 1, 0, -1):
        part = mat_cols(get_mat(mid_ref, rows, 0, piece - 1), [[c[i] - a[i] for i in range(5)]])[0]
        rest = mat_cols(get_mat(mid_ref, rows, 25, piece - 1), [a])[0]
        m0 = get_vec(mid_ref, rows, 50, piece - 1)
        c = [a[i] + ((part[i] + rest[i]) + m0[i]) for i in range(5)]
        put_vec(out_ref, rows, 5 * piece, c)


def begin_backward(inner, spots_ref, ends_refs, mid_ref, edge, ends8):
    rows = 4 // inner
    at = spots_ref[1] if inner == 2 else spots_ref[3]
    for offset, ends_ref in enumerate(ends_refs):
        plane = lax.rem(at + offset, inner) * rows
        for e in range(10):
            for z in range(rows):
                row = ends_ref[pl.ds(rows * (5 * at + e) + z, 1), :]
                ends8[e, pl.ds(2 * (plane + z), 1), :] = row
                ends8[e, pl.ds(2 * (plane + z) + 1, 1), :] = row
    a = [ends8[i] for i in range(5)]
    c = [ends8[5 + i] for i in range(5)]
    gap = [c[i] - a[i] for i in range(5)]
    part = mat_cols(load_mat(mid_ref, 0), [gap])[0]
    rest = mat_cols(load_mat(mid_ref, 25), [a])[0]
    even = even_rows()
    for i in range(5):
        middle = a[i] + ((part[i] + rest[i]) + mid_ref[50 + i])
        edge[i] = jnp.where(even, a[i], pltpu.roll(middle, 1, 0))
        edge[5 + i] = jnp.where(even, middle, c[i])


def between(k, left, right, tables, source):
    tab, eps, dlt = tables
    rows = cell_rows(k)
    e, d = eps[rows, :], dlt[rows, :]
    c = reciprocal(2.0 + d)
    gap = [right[i] - left[i] for i in range(5)]
    moved = mat_cols(table_mat(tab[rows, :], 0), [[e * value for value in gap]])[0]
    return [
        right[i] - c * ((gap[i] + moved[i]) + (d * right[i] - source[i])) for i in range(5)
    ]


def backward_chunk(fac_ref, mid_ref, edge, write, tables):
    step = pl.program_id(0)
    a = [edge[i] for i in range(5)]
    begin = jnp.where(step == 0, 1, 0)

    def one(at, following):
        slot = CHUNK - 1 - at
        m = (STEPS - 1 - step) * CHUNK + slot
        gap = [following[i] - a[i] for i in range(5)]
        r = [[fac_ref[slot, 5 * i + j] for j in range(5)] for i in range(5)]
        x = [[fac_ref[slot, 25 + 5 * i + j] for j in range(5)] for i in range(5)]
        part = mat_cols(r, [gap])[0]
        rest = mat_cols(x, [a])[0]
        here = tuple(
            following[i] - ((part[i] + rest[i]) + fac_ref[slot, 50 + i]) for i in range(5)
        )
        source = [fac_ref[slot, 55 + i] for i in range(5)]
        write(2 * m + 2, between(2 * m + 2, here, following, tables, source))
        write(2 * m + 1, here)
        return here

    def two(pair, following):
        return one(2 * pair + 1, one(2 * pair, following))

    @pl.when(step == 0)
    def _():
        here = two(1, one(1, tuple(edge[5 + i] for i in range(5))))
        for i in range(5):
            edge[5 + i] = here[i]

    def four(quad, following):
        return two(2 * quad + 1, two(2 * quad, following))

    final = lax.fori_loop(begin, CHUNK // 4, four, tuple(edge[5 + i] for i in range(5)))
    for i in range(5):
        edge[5 + i] = final[i]

    @pl.when(step == STEPS - 1)
    def _():
        write(0, between(0, a, final, tables, [mid_ref[55 + i] for i in range(5)]))


def backward_x_kernel(
    spots_ref, fac_ref, mid_ref, e0, e1, tab, eps, dlt, q_ref, out_ref, edge, ends8
):
    def write(k, value):
        rows = cell_rows(k)
        for i in range(5):
            out_ref[i, rows, :] = value[i] - q_ref[i, rows, :]

    @pl.when(pl.program_id(0) == 0)
    def _():
        begin_backward(2, spots_ref, (e0, e1), mid_ref, edge, ends8)
        write(HALF - 1, [edge[5 + i] for i in range(5)])

    backward_chunk(fac_ref, mid_ref, edge, write, (tab, eps, dlt))


def backward_y_kernel(
    spots_ref, fac_ref, mid_ref, e0, e1, e2, e3, tab, eps, dlt, out_ref, edge, ends8, field
):
    def write(k, value):
        for i in range(5):
            field[i, cell_rows(k), :] = value[i]

    @pl.when(pl.program_id(0) == 0)
    def _():
        begin_backward(4, spots_ref, (e0, e1, e2, e3), mid_ref, edge, ends8)
        write(HALF - 1, [edge[5 + i] for i in range(5)])

    backward_chunk(fac_ref, mid_ref, edge, write, (tab, eps, dlt))

    @pl.when(pl.program_id(0) == STEPS - 1)
    def _():
        for c in range(5):
            for z in range(4):
                rows = pl.ds(128 * z, 128)
                out_ref[c, rows, :] = field[c, rows, :].T


def whole(shape):
    return pl.BlockSpec(shape, lambda i: (0,) * len(shape))


def scalars():
    return pl.BlockSpec(memory_space=pltpu.SMEM)


def params():
    return pltpu.CompilerParams(
        dimension_semantics=("arbitrary",), vmem_limit_bytes=VMEM_LIMIT
    )


PLANE = (512, 128)


def forward_out(inner):
    ports = [(ENTRIES * 4 // inner, 128)] * inner
    shapes = [(KEPT, FACTORS, 8, 128), (60, 8, 128), PLANE, PLANE, PLANE] + ports
    return tuple(jax.ShapeDtypeStruct(shape, F32) for shape in shapes)


def forward_specs(inner):
    block = pl.BlockSpec((CHUNK, FACTORS, 8, 128), lambda i: (i, 0, 0, 0))
    return (block,) + tuple(whole(value.shape) for value in forward_out(inner)[1:])


def forward_scratch(fields):
    return (
        [pltpu.VMEM((STATE, 8, 128), F32), pltpu.VMEM((5, 8, 128), F32)]
        + fields
        + [
            pltpu.VMEM((128, 128), F32),
            pltpu.VMEM((25, 128), F32),
            pltpu.VMEM((1024, 128), F32),
        ]
    )


def forward(kernel, name, inner, flags, operands, fields):
    return pl.pallas_call(
        kernel,
        grid=(STEPS,),
        in_specs=[scalars() for _ in flags] + [whole(value.shape) for value in operands],
        out_specs=forward_specs(inner),
        out_shape=forward_out(inner),
        scratch_shapes=forward_scratch(fields),
        compiler_params=params(),
        name=name,
    )(*flags, *operands)


def small(kernel, name, flags, operands, outputs, scratch):
    vmem = pl.BlockSpec(memory_space=pltpu.VMEM)
    return pl.pallas_call(
        kernel,
        out_shape=tuple(jax.ShapeDtypeStruct(shape, F32) for shape in outputs),
        in_specs=[scalars() for _ in flags] + [vmem for _ in operands],
        out_specs=tuple(vmem for _ in outputs),
        scratch_shapes=[pltpu.VMEM(shape, F32) for shape in scratch],
        compiler_params=pltpu.CompilerParams(vmem_limit_bytes=VMEM_LIMIT),
        name=name,
    )(*flags, *operands)


FARTHEST_FIRST = {2: (1,), 4: (2, 1, 3)}


def exchange(values, axis, inner):
    count = lax.axis_size(axis)
    received = {0: values[0]}
    for offset in FARTHEST_FIRST[inner]:
        back = inner - offset
        moves = [(i, (i // inner) * inner + (i + back) % inner) for i in range(count)]
        received[offset] = lax.ppermute(values[back], axis, moves)
    return [received[offset] for offset in range(inner)]


def line_ends(ports, axis, spots):
    inner = len(ports)
    rows = 4 // inner
    count = lax.axis_size(axis)
    port_shape = (ENTRIES * rows, 128)
    mid_shape = (inner - 1, 56 * rows, 128)
    port, mid = small(
        functools.partial(join_kernel, inner), "join_" + axis, (spots,),
        exchange(ports, axis, inner), (port_shape, mid_shape), [(inner, *port_shape)],
    )
    blocks = {0: port}
    for far in FARTHEST_FIRST[4]:
        moves = [((i + far * inner) % count, i) for i in range(count)]
        blocks[far] = lax.ppermute(port, axis, moves)
    blocks = [blocks[far] for far in range(4)]
    (ends,) = small(
        functools.partial(solve_kernel, inner), "solve_" + axis, (spots,), (*blocks, mid),
        ((32, 128),), [(4, *port_shape), (5, 8 * rows, 128)],
    )
    return exchange([ends] * inner, axis, inner)


def backward(kernel, name, spots, operands, extra):
    return pl.pallas_call(
        kernel,
        grid=(STEPS,),
        in_specs=[
            scalars(),
            pl.BlockSpec((CHUNK, FACTORS, 8, 128), lambda i: (STEPS - 1 - i, 0, 0, 0)),
        ]
        + [whole(value.shape) for value in operands[1:]],
        out_specs=whole((5, 512, 128)),
        out_shape=jax.ShapeDtypeStruct((5, 512, 128), F32),
        scratch_shapes=[pltpu.VMEM((10, 8, 128), F32), pltpu.VMEM((10, 8, 128), F32)] + extra,
        compiler_params=params(),
        name=name,
    )(spots, *operands)


def halos(axis, last, initial):
    devices = lax.axis_size(axis)
    up = [(i, (i + 1) % devices) for i in range(devices)]
    down = [(j, i) for i, j in up]
    return lax.ppermute(last, axis, up), lax.ppermute(initial, axis, down)


def body(flow_state, viscosity, metric_x, metric_y, jacobian_x, jacobian_y):
    row, col = lax.axis_index("row"), lax.axis_index("col")
    spots = jnp.stack([row // 2, row % 2, col // 4, col % 4]).astype(jnp.int32)
    places = jnp.stack([row, col]).astype(jnp.int32)
    sizes = jnp.array([lax.axis_size("row"), lax.axis_size("col")], jnp.int32)
    first = (places == 0).astype(jnp.int32)
    last = (places == sizes - 1).astype(jnp.int32)
    jacx = jacobian_x.reshape(25, 128)
    jacy = jacobian_y.reshape(25, 128)

    south, north = halos(
        "col",
        flow_state[:, :, :, 127].reshape(20, 128),
        flow_state[:, :, :, 0].reshape(20, 128),
    )
    q = flow_state.reshape(5, 512, 128)
    visc = viscosity.reshape(512, 128)
    plane = [pltpu.VMEM(PLANE, F32), pltpu.VMEM(PLANE, F32)]
    field = pltpu.VMEM((5, 512, 128), F32)
    fac, mid, tab, eps, dlt, *ports = forward(
        forward_x_kernel, "forward_x", 2, (spots, first, last),
        (q, visc, metric_x, metric_y, jacx, jacy, south, north), plane,
    )
    ends = line_ends(ports, "row", spots)
    partial_value = backward(
        backward_x_kernel, "backward_x", spots, (fac, mid, *ends, tab, eps, dlt, q), []
    )
    fac, mid, tab, eps, dlt, *ports = forward(
        forward_y_kernel, "forward_y", 4, (spots,), (partial_value, visc, metric_y, jacy), [field]
    )
    ends = line_ends(ports, "col", spots)
    result = backward(
        backward_y_kernel, "backward_y", spots, (fac, mid, *ends, tab, eps, dlt), [field]
    )
    return result.reshape(5, 4, 128, 128)


def solution(mesh):
    return jax.shard_map(
        body,
        mesh=mesh,
        in_specs=(
            P(None, None, "row", "col"),
            P(None, "row", "col"),
            P("row", "col"),
            P("row", "col"),
            P(None, None, "row"),
            P(None, None, "col"),
        ),
        out_specs=P(None, None, "row", "col"),
        check_vma=False,
    )
```
